128 devices in a mesh: tm: 32 (over y, x, core), stream: 4 (over z).
Axes of the slice: x: 4, y: 4, z: 4, core: 2. Of those that a mesh axis runs over, the one named last changes fastest.
Arguments:
- raw: bfloat16 [4, 6, 524288], P('stream', None, 'tm'), may hold values from -6 to 6
- starts: int32 [4, 131072], P('stream', 'tm'), may hold values from 0 to 1, as said below
- neg_owner: int32 [4, 1024, 4], P('stream', 'tm'), may hold values from 0 to 127, all different within a row; in each aligned block of 32 rows (0 to 31, 32 to 63, ..., all dimensions but the last counted through in order) at most 2 rows name the same one
- neg_block: int32 [4, 1024, 4], P('stream', 'tm'), may hold values from 0 to 31
- enc_weight: bfloat16 [24, 256], replicated, may hold values from -1.25 to 1.25
- tcn_weight: bfloat16 [4, 2, 256, 256], replicated, may hold values from -0.25 to 0.25
- pred_weight: bfloat16 [256, 256], replicated, may hold values from -0.375 to 0.375
Outputs:
- grad_latent: float32 [4, 131072, 256], P('stream', 'tm')
The draws below stay inside these ranges and needn't reach their ends.
Inputs may be any that keep to these rules, and one draw needn't show every extreme that they name: `starts`: row 0 of every stream is 1. `neg_owner`: the owner is the flat device index tm * 4 + stream; each row names 4 different owners; within the 32 rows of one device no owner is named more than 2 times, a bound that some block reaches.
All inputs are finite; a program needn't handle non-finite values.
Results may differ from the reference program's by a relative error of at most 0.011.
Values may be sent and summed in bfloat16 or wider, within the bound.
No kernel may reach another device: no remote copies, remote signals or barrier semaphores. Data moves between devices by JAX's collectives and lax.ppermute only.
A program may use at most 192 MiB of HBM per device.

```python
import math
import jax
import jax.numpy as jnp
import numpy as np
from jax import lax

D = 256
CIN = 6
STRIDE = 4
LAYERS = 4
AHEAD = 4
BLOCK = 128
NEG = 4
LAT_DEV = 4096
STREAMS = 4
T_LAT = 131072
SAMPLES = 524288
NB = 32
T_BLOCKS = 1024
OWNERS = 128
CAP = 2
N_STREAM = 4


def draw_starts(key, part):
    key = jax.random.fold_in(key, 7)
    picks = jax.random.randint(key, (STREAMS, T_LAT), 0, 300)
    first = jnp.arange(T_LAT) == 0
    return jnp.where((picks == 0) | first[None, :], 1, 0).astype(jnp.int32)


def touch_ends(drawn, key, low, top_value):
    longest = drawn.shape.index(max(drawn.shape))
    spots = []
    for shift in (0, 1):
        where = [jax.random.randint(jax.random.fold_in(key, axis), (), 0, length) for axis, length in enumerate(drawn.shape)]
        where[longest] = (where[longest] + shift) % drawn.shape[longest]
        spots.append(tuple(where))
    return drawn.at[spots[0]].set(low).at[spots[1]].set(top_value)


def block_scale(stream_key, shape, pieces, least, largest):
    level = 1.0
    for axis_at, shards_of in pieces:
        heights = jax.random.uniform(jax.random.fold_in(jax.random.fold_in(stream_key, 6), axis_at), (shards_of,), jnp.float32, least / len(pieces), largest / len(pieces))
        level = level * jnp.repeat(jnp.exp(heights), shape[axis_at] // shards_of).reshape((-1,) + (1,) * (len(shape) - 1 - axis_at))
    return level


def shared_out(key, own, number, rows, amount, top, most, lean):
    ranking = jax.random.permutation(key, amount)
    packed, common = shares(amount, rows * top, most, lean, True), shares(amount, rows * top, most, lean, False)
    places = jnp.arange(amount)

    def named(sizes, rotation):
        used = int((sizes > 0).sum())
        fixed = max(1, used // 4)
        moved = fixed + (places - fixed + rotation * (used - fixed)) % max(1, amount - fixed)
        return jnp.zeros((amount,), jnp.int32).at[ranking[jnp.where(places < fixed, places, moved)]].set(jnp.asarray(sizes, jnp.int32))

    sizes = jnp.where(number % 4 == 0, named(packed, number // 4), named(common, number - number // 4 - 1))
    mixed = jax.random.permutation(jax.random.fold_in(own, 3), amount)
    source_of, receiver = mixed[0:amount // 2 * 2:2], mixed[1:amount // 2 * 2:2]
    slack = jnp.minimum(sizes[source_of] - 1, most - sizes[receiver]) // 2
    slack = jnp.where((source_of == ranking[0]) | (receiver == ranking[0]) | (sizes[receiver] == 0), 0, jnp.maximum(slack, 0))
    moved = jax.random.randint(jax.random.fold_in(own, 4), (amount // 2,), 0, 1 << 20) % (slack + 1)
    sizes = sizes.at[source_of].add(-moved).at[receiver].add(moved)
    members = jnp.searchsorted(jnp.cumsum(sizes), jnp.arange(rows * top), side="right").astype(jnp.int32)
    grid = members.reshape(top, rows).T
    grid = grid[jax.random.permutation(jax.random.fold_in(own, 1), rows)]
    rotation = jax.random.randint(jax.random.fold_in(own, 2), (rows, 1), 0, top)
    return jnp.take_along_axis(grid, (jnp.arange(top)[None, :] + rotation) % top, axis=1)


def shares(number_of, total, bound, lean, full):
    portions = [(1 << 20) // math.isqrt(grade ** lean) + 1 for grade in range(1, number_of + 1)]
    largest = bound if full else min(bound, max(-(-total // number_of), total * portions[0] // sum(portions)))
    least = 1 if total - largest >= number_of - 1 else 0
    given, surplus = [largest] + [least] * (number_of - 1), total - largest - least * (number_of - 1)
    while surplus > 0:
        candidates = [i for i in range(1, number_of) if given[i] < largest] or [i for i in range(1, number_of) if given[i] < bound]
        whole, left = sum([portions[i] for i in candidates]), surplus
        for i in candidates:
            more = min(bound - given[i], max(1, left * portions[i] // whole), surplus)
            given[i] = given[i] + more
            surplus = surplus - more
    return np.array(given)


def centred(key, shape, scale, bound, cuts=(), kind=jnp.bfloat16):
    loudness = block_scale(key, shape, cuts, -0.22, 0.18) if cuts else 1.0
    values = jax.random.normal(key, shape, jnp.float32) * scale * loudness
    return jnp.minimum(jnp.maximum(values, -bound), bound).astype(kind)


def setup_inputs(seed: int = 0) -> dict:
    seeds = jax.random.split(jax.random.key(seed), 8)
    raw = centred(seeds[0], (STREAMS, CIN, SAMPLES), 1.0, 6.0, ((0, 4), (2, 32)))
    starts = draw_starts(jax.random.fold_in(seeds[7], 71), 0)
    neg_owner_keys = jax.random.split(jax.random.fold_in(seeds[2], 1), STREAMS * T_BLOCKS // NB)
    neg_owner_turns = jax.random.permutation(jax.random.fold_in(seeds[2], 3), STREAMS * T_BLOCKS // NB)
    neg_owner = jax.vmap(lambda own, number: shared_out(jax.random.fold_in(seeds[2], 2), own, number, NB, OWNERS, NEG, CAP, 2))(neg_owner_keys, neg_owner_turns).reshape((STREAMS, T_BLOCKS, NEG))
    neg_block = touch_ends(jax.random.randint(seeds[3], (STREAMS, T_BLOCKS, NEG), 0, NB), jax.random.fold_in(seeds[3], 1), 0, NB - 1).astype(jnp.int32)
    enc_weight = centred(seeds[4], (STRIDE * CIN, D), (STRIDE * CIN) ** -0.5, 1.25)
    tcn_weight = centred(seeds[5], (LAYERS, 2, D, D), (2 * D) ** -0.5, 0.25)
    pred_weight = centred(seeds[6], (D, D), D ** -0.5, 0.375)
    return dict(raw=raw, starts=starts, neg_owner=neg_owner, neg_block=neg_block, enc_weight=enc_weight, tcn_weight=tcn_weight, pred_weight=pred_weight)


score_scale = 10.0
epsilon = 1e-06

def encode(raw_rows, enc_weight):
    channels, samples = raw_rows.shape
    patches = raw_rows.reshape(channels, samples // STRIDE, STRIDE).transpose(1, 2, 0)
    patches = patches.reshape(samples // STRIDE, STRIDE * channels)
    return jax.nn.silu(jnp.dot(patches, enc_weight, preferred_element_type=jnp.float32)).astype(jnp.bfloat16)

def shift_down(values, spacing):
    filler = jnp.zeros((spacing,) + values.shape[1:], values.dtype)
    return jnp.concatenate([filler, values[:-spacing]], axis=0)

def shift_up(values, spacing):
    filler = jnp.zeros((spacing,) + values.shape[1:], values.dtype)
    return jnp.concatenate([values[spacing:], filler], axis=0)

def build_masks(start_rows):
    running = jnp.cumsum(start_rows, dtype=jnp.int32)
    tap_gates = []
    for layer_index in range(LAYERS):
        spacing = 2 ** layer_index
        tap_gates.append(jnp.where(running - shift_down(running, spacing) == 0, 1.0, 0.0).astype(jnp.float32))
    return tap_gates

def context_forward(hidden, tap_gates, tcn_weight):
    preacts = []
    for layer_index in range(LAYERS):
        spacing = 2 ** layer_index
        current = jnp.dot(hidden, tcn_weight[layer_index, 0], preferred_element_type=jnp.float32)
        earlier = jnp.dot(hidden, tcn_weight[layer_index, 1], preferred_element_type=jnp.float32)
        preact = current + shift_down(earlier, spacing) * tap_gates[layer_index][:, None]
        hidden = (hidden.astype(jnp.float32) + jax.nn.silu(preact)).astype(jnp.bfloat16)
        preacts.append(preact)
    return (hidden, preacts)

def context_backward(cotangent, preacts, tap_gates, tcn_weight):
    for layer_index in reversed(range(LAYERS)):
        spacing = 2 ** layer_index
        preact = preacts[layer_index]
        sigmoid_value = jax.nn.sigmoid(preact)
        gated_back = (cotangent * sigmoid_value * (1.0 + preact * (1.0 - sigmoid_value))).astype(jnp.bfloat16)
        current = jnp.dot(gated_back, tcn_weight[layer_index, 0].T, preferred_element_type=jnp.float32)
        earlier = jnp.dot(gated_back, tcn_weight[layer_index, 1].T, preferred_element_type=jnp.float32)
        earlier = earlier * tap_gates[layer_index][:, None]
        cotangent = cotangent + current + shift_up(earlier, spacing)
    return cotangent

def predict(context_rows, pred_weight):
    raw_pred = jnp.dot(context_rows, pred_weight, preferred_element_type=jnp.float32)
    pred_scale = lax.rsqrt(lax.optimization_barrier(jnp.sum(raw_pred * raw_pred, axis=-1)) + epsilon)
    pred_unit = raw_pred * pred_scale[:, None]
    return (pred_scale, pred_unit, pred_unit.astype(jnp.bfloat16))

def predict_back(query_grad, pred_scale, pred_unit, pred_weight):
    along = lax.optimization_barrier(jnp.sum(pred_unit * query_grad, axis=-1, keepdims=True))
    pred_grad = (pred_scale[:, None] * (query_grad - along * pred_unit)).astype(jnp.bfloat16)
    return jnp.dot(pred_grad, pred_weight.T, preferred_element_type=jnp.float32)

def score_group(queries, targets, usable, negatives):
    target_f = targets.astype(jnp.float32)
    query_f = queries.astype(jnp.float32)
    neg_f = negatives.astype(jnp.float32)
    target_scale = lax.rsqrt(lax.optimization_barrier(jnp.sum(target_f * target_f, axis=-1)) + epsilon)
    neg_scale = lax.rsqrt(lax.optimization_barrier(jnp.sum(neg_f * neg_f, axis=-1)) + epsilon)
    positive = score_scale * lax.optimization_barrier(jnp.sum(query_f * target_f, axis=-1)) * target_scale
    scores = score_scale * jnp.einsum('gid,gkd->gik', query_f, neg_f) * neg_scale[:, None, :]
    exp_pos = jnp.exp(positive)
    exp_neg = jnp.exp(scores)
    partition = exp_pos + lax.optimization_barrier(jnp.sum(exp_neg, axis=-1))
    d_pos = usable * (exp_pos / partition - 1.0)
    d_score = usable[:, :, None] * exp_neg / partition[:, :, None]
    weighted = (d_score * neg_scale[:, None, :]).astype(jnp.bfloat16)
    weighted_f = weighted.astype(jnp.float32)
    query_grad = score_scale * (jnp.einsum('gik,gkd->gid', weighted_f, neg_f) + (d_pos * target_scale)[:, :, None] * target_f)
    target_grad = (score_scale * d_pos * target_scale)[:, :, None] * query_f - (d_pos * positive * target_scale * target_scale)[:, :, None] * target_f
    direct = score_scale * jnp.einsum('gik,gid->gkd', weighted_f, query_f)
    spread = lax.optimization_barrier(jnp.sum(d_score * scores, axis=1))
    negative_grad = (direct - (spread * neg_scale * neg_scale)[:, :, None] * neg_f).astype(jnp.bfloat16)
    return (query_grad, target_grad, negative_grad)

def reference(raw, starts, neg_owner, neg_block, enc_weight, tcn_weight, pred_weight):
    latents = jnp.stack([encode(raw[stream], enc_weight) for stream in range(STREAMS)])
    offsets = jnp.arange(BLOCK, dtype=jnp.int32)
    group_blocks = 4
    groups = T_BLOCKS // group_blocks
    gradient = jnp.zeros((STREAMS, T_LAT, D), jnp.float32)
    for stream in range(STREAMS):
        stream_latents = latents[stream]
        tap_gates = build_masks(starts[stream])
        context, preacts = context_forward(stream_latents, tap_gates, tcn_weight)
        pred_scale, pred_unit, queries = predict(shift_down(context, AHEAD), pred_weight)
        running = jnp.cumsum(starts[stream], dtype=jnp.int32)
        usable = jnp.where(running - shift_down(running, AHEAD) == 0, 1.0, 0.0).astype(jnp.float32)
        owner_stream = (neg_owner[stream] % N_STREAM).astype(jnp.int32)
        first_row = (neg_owner[stream] // N_STREAM * LAT_DEV + neg_block[stream] * BLOCK).astype(jnp.int32)

        def score_step(inputs):
            group_queries, group_targets, group_usable, group_streams, group_first = inputs
            negatives = latents[group_streams[:, :, None], group_first[:, :, None] + offsets]
            return score_group(group_queries, group_targets, group_usable, negatives.reshape(group_blocks, NEG * BLOCK, D))
        query_grad, target_grad, negative_grad = lax.map(score_step, (queries.reshape(groups, group_blocks, BLOCK, D), stream_latents.reshape(groups, group_blocks, BLOCK, D), usable.reshape(groups, group_blocks, BLOCK), owner_stream.reshape(groups, group_blocks, NEG), first_row.reshape(groups, group_blocks, NEG)))
        gradient = gradient.at[owner_stream[:, :, None], first_row[:, :, None] + offsets].add(negative_grad.reshape(T_BLOCKS, NEG, BLOCK, D).astype(jnp.float32))
        context_grad = shift_up(predict_back(query_grad.reshape(T_LAT, D), pred_scale, pred_unit, pred_weight), AHEAD)
        gradient = gradient.at[stream].add(context_backward(context_grad, preacts, tap_gates, tcn_weight) + target_grad.reshape(T_LAT, D))
    return gradient
```

```python
import jax
import jax.numpy as jnp
from jax import lax
from jax.experimental import pallas as pl
from jax.experimental.pallas import tpu as pltpu
from jax.sharding import PartitionSpec as P

BLOCK = 128
NEG = 4
HALO = 32
AHEAD = 4
CAP = 2
LAYERS = 4
PACK = 32
TOGETHER = 8
SEGMENT = 512
SCALE = 10.0
EPSILON = 1e-06
BF = jnp.bfloat16
F32 = jnp.float32
MIB = 1 << 20


def dot(a, b):
    return jnp.dot(a, b, preferred_element_type=F32)


def dot_nt(a, b):
    return lax.dot_general(a, b, (((1,), (1,)), ((), ())), preferred_element_type=F32)


def row_sum(x):
    return jnp.sum(x, axis=-1, keepdims=True)


def silu_of_half(half):
    return half + half * jnp.tanh(half)


def prep_kernel(owner_ref, block_ref, raw_ref, starts_ref, rim_ref, enc_ref,
                pack_ref, push_ref, slot_ref, bd_ref, lines, packs, seen):
    blocks = pack_ref.shape[0]
    lines[...] = jnp.zeros_like(lines)
    for b in range(blocks):
        lines[b, 0:6, :] = raw_ref[:, b * 512:(b + 1) * 512].astype(F32)
    row = lax.broadcasted_iota(jnp.int32, (512, 512), 0)
    col = lax.broadcasted_iota(jnp.int32, (512, 512), 1)
    perm = jnp.where(row == 4 * (col & 127) + (col >> 7), 1.0, 0.0).astype(BF)
    row = lax.broadcasted_iota(jnp.int32, (128, 128), 0)
    col = lax.broadcasted_iota(jnp.int32, (128, 128), 1)
    perm_halo = jnp.where(row == 4 * (col & 31) + (col >> 5), 1.0, 0.0).astype(BF)
    flat = lines[...].reshape(blocks * 8, 512).astype(BF)
    main = dot(flat, perm).reshape(blocks, 8, 512)
    halo = dot(flat[:, 384:512], perm_halo).reshape(blocks, 8, 128)
    rim = rim_ref[...]
    rim_halo = dot(rim, perm_halo)

    lane = lax.broadcasted_iota(jnp.int32, (blocks + 8, 128), 1)
    level_row = lax.broadcasted_iota(jnp.int32, (8, 128), 0)
    rim_f = rim.astype(F32)
    before = jnp.where(level_row == 7, pltpu.roll(rim_f, 1, 0), 0.0)
    started = jnp.concatenate([before, starts_ref[...].astype(F32)], axis=0)
    level = 1.0 - started
    for distance in (1, 2, 4):
        moved = pltpu.roll(started, distance, 1)
        started = jnp.maximum(
            started, jnp.where(lane < distance, pltpu.roll(moved, 1, 0), moved)
        )
        level = level + (1.0 - started)
    level_halo = jnp.where(lane < HALO, pltpu.roll(level, HALO, 1), 0.0)

    for k in range(4):
        packs[:, k * 6:(k + 1) * 6, :] = main[:, 0:6, k * 128:(k + 1) * 128]
    packs[0, 24:30, :] = rim_halo[0:6]
    packs[1:blocks, 24:30, :] = halo[0:blocks - 1, 0:6, :]
    for b in range(blocks):
        packs[b, 30:31, :] = level[8 + b:9 + b]
        packs[b, 31:32, :] = level_halo[7 + b:8 + b]
    pack_ref[...] = packs[...].astype(BF)

    at = lax.broadcasted_iota(jnp.int32, (PACK, 128), 0)
    lane = lax.broadcasted_iota(jnp.int32, (PACK, 128), 1)
    note = jnp.where((at == PACK - 1) & (lane >= 64), 1.0, 0.0)
    unused = (-note).astype(BF)

    def clear(i, carry):
        push_ref[i] = unused
        return carry

    lax.fori_loop(0, push_ref.shape[0], clear, 0)

    def forget(i, carry):
        seen[i] = 0
        return carry

    lax.fori_loop(0, seen.shape[0], forget, 0)

    def send(i, carry):
        owner = owner_ref[i]
        rank = seen[owner]
        seen[owner] = rank + 1
        slot = owner * CAP + rank
        slot_ref[i] = slot
        wanted = block_ref[i].astype(F32)
        push_ref[slot] = (packs[i // NEG] + note * wanted).astype(BF)
        return carry

    lax.fori_loop(0, blocks * NEG, send, 0)

    bd_ref[...] = jnp.zeros_like(bd_ref)
    half_enc = (enc_ref[...].astype(F32) * 0.5).astype(BF)
    for q in range(4):
        bd_ref[q * 32:q * 32 + 24, q * 256:(q + 1) * 256] = half_enc


def prep(owners, wanted, raw, starts, rim, enc_weight, owners_count):
    blocks = starts.shape[0]
    smem = pl.BlockSpec(memory_space=pltpu.SMEM)
    vmem = pl.BlockSpec(memory_space=pltpu.VMEM)
    return pl.pallas_call(
        prep_kernel,
        out_shape=(
            jax.ShapeDtypeStruct((blocks, PACK, 128), BF),
            jax.ShapeDtypeStruct((owners_count * CAP, PACK, 128), BF),
            jax.ShapeDtypeStruct((blocks * NEG,), jnp.int32),
            jax.ShapeDtypeStruct((128, 1024), BF),
        ),
        in_specs=[smem, smem, vmem, vmem, vmem, vmem],
        out_specs=(vmem, vmem, smem, vmem),
        scratch_shapes=[
            pltpu.VMEM((blocks, 8, 512), F32),
            pltpu.VMEM((blocks, PACK, 128), F32),
            pltpu.SMEM((owners_count,), jnp.int32),
        ],
        compiler_params=pltpu.CompilerParams(vmem_limit_bytes=32 * MIB),
        name="prep",
    )(owners, wanted, raw, starts, rim, enc_weight)


def turn(tiles):
    return jnp.transpose(jnp.concatenate(tiles, axis=0).astype(F32))


def encode_with_halo(turned, bd):
    lane = lax.broadcasted_iota(jnp.int32, (HALO, 128), 1) & 31
    halo = jnp.zeros((HALO, 128), F32)
    for k in range(4):
        moved = pltpu.roll(turned[k * 32:(k + 1) * 32], (6 * k - 24) % 128, 1)
        halo = jnp.where((lane >= 6 * k) & (lane < 6 * k + 6), moved, halo)
    rows = jnp.concatenate([turned, halo], axis=0).astype(BF)
    return silu_of_half(dot(rows, bd))


def layer_half(h, level, layer, w_ref):
    moved = pltpu.roll(h, 2**layer, 0)
    gated = jnp.where(level > layer, moved, 0.0)
    return dot(h.astype(BF), w_ref[layer, 0]) + dot(gated.astype(BF), w_ref[layer, 1])


def forward_kernel(pack_ref, bd_ref, w_ref, pred_ref, lat_ref, ctx_ref, slope_ref, level_ref,
                   rim_slope_ref, rim_level_ref, keyed_ref):
    first = pl.program_id(0) == 0
    turned = turn([pack_ref[q] for q in range(4)])
    encoded = encode_with_halo(turned, bd_ref[...])
    latent = jnp.concatenate(
        [encoded[128:160, 0:256]] + [encoded[0:128, q * 256:(q + 1) * 256] for q in range(4)],
        axis=0,
    ).astype(BF)
    columns = [turned[0:32, 31:32]] + [turned[:, q * 32 + 30:q * 32 + 31] for q in range(4)]
    level = jnp.broadcast_to(jnp.concatenate(columns, axis=0), (HALO + SEGMENT, 256))
    level_ref[...] = level[HALO:, 0:128]
    lat_ref[...] = latent[HALO:]
    h = latent.astype(F32)
    own = h[HALO:]
    key_scale = lax.rsqrt(row_sum(own * own) + EPSILON)
    keyed_ref[...] = dot_nt((own * key_scale).astype(BF), pred_ref[...]).astype(BF)
    slopes = []
    for layer in range(LAYERS):
        half = layer_half(h, level, layer, w_ref)
        tanh = jnp.tanh(half)
        slope = (0.5 * (1.0 + tanh)) * (1.0 + half * (1.0 - tanh))
        slope_ref[layer] = slope[HALO:].astype(BF)
        slopes.append(slope[:HALO].astype(BF))
        h = h + half + half * tanh
    ctx_ref[...] = h[HALO - AHEAD:HALO - AHEAD + SEGMENT].astype(BF)

    @pl.when(first)
    def _():
        rim_level_ref[...] = level[:HALO, 0:128]
        for layer in range(LAYERS):
            rim_slope_ref[layer] = slopes[layer]


def forward(pack, bd, half_weight, pred_weight):
    rows = pack.shape[0] * BLOCK
    steps = rows // SEGMENT
    whole = lambda *shape: pl.BlockSpec(shape, lambda i: (0,) * len(shape))
    rows_of = lambda width: pl.BlockSpec((SEGMENT, width), lambda i: (i, 0))
    return pl.pallas_call(
        forward_kernel,
        grid=(steps,),
        out_shape=(
            jax.ShapeDtypeStruct((rows, 256), BF),
            jax.ShapeDtypeStruct((rows, 256), BF),
            jax.ShapeDtypeStruct((LAYERS, rows, 256), BF),
            jax.ShapeDtypeStruct((rows, 128), F32),
            jax.ShapeDtypeStruct((LAYERS, HALO, 256), BF),
            jax.ShapeDtypeStruct((HALO, 128), F32),
            jax.ShapeDtypeStruct((rows, 256), BF),
        ),
        in_specs=[
            pl.BlockSpec((4, PACK, 128), lambda i: (i, 0, 0)),
            whole(128, 1024),
            whole(LAYERS, 2, 256, 256),
            whole(256, 256),
        ],
        out_specs=(
            rows_of(256),
            rows_of(256),
            pl.BlockSpec((LAYERS, SEGMENT, 256), lambda i: (0, i, 0)),
            rows_of(128),
            whole(LAYERS, HALO, 256),
            whole(HALO, 128),
            rows_of(256),
        ),
        compiler_params=pltpu.CompilerParams(vmem_limit_bytes=40 * MIB),
        cost_estimate=pl.CostEstimate(
            flops=rows * 2 * 65536 * 10, bytes_accessed=18 * MIB, transcendentals=rows * 256 * 5
        ),
        name="forward",
    )(pack, bd, half_weight, pred_weight)


def answer_kernel(wanted_ref, pack_ref, answer_ref, order_ref, count_ref):
    slots = wanted_ref.shape[0]

    def clear(i, carry):
        order_ref[i] = 0
        return carry

    lax.fori_loop(0, slots, clear, 0)

    def reply(i, count):
        wanted = wanted_ref[i]
        answer_ref[i] = pack_ref[jnp.maximum(wanted, 0)]
        order_ref[count] = i
        return count + jnp.where(wanted >= 0, 1, 0)

    count = lax.fori_loop(0, slots, reply, 0)
    count_ref[0] = count


def answer(wanted, pack):
    slots = wanted.shape[0]
    smem = pl.BlockSpec(memory_space=pltpu.SMEM)
    vmem = pl.BlockSpec(memory_space=pltpu.VMEM)
    return pl.pallas_call(
        answer_kernel,
        out_shape=(
            jax.ShapeDtypeStruct((slots, PACK, 128), BF),
            jax.ShapeDtypeStruct((slots,), jnp.int32),
            jax.ShapeDtypeStruct((1,), jnp.int32),
        ),
        in_specs=[smem, vmem],
        out_specs=(vmem, smem, smem),
        compiler_params=pltpu.CompilerParams(vmem_limit_bytes=16 * MIB),
        name="answer",
    )(wanted, pack)


def recompute_kernel(order_ref, count_ref, push_ref, bd_ref, w_ref, ctx_ref):
    base = pl.program_id(0) * TOGETHER

    @pl.when(base < count_ref[0])
    def _():
        bd = bd_ref[...]
        hidden, levels = [], []
        for part in range(TOGETHER // 4):
            turned = turn([push_ref[order_ref[base + part * 4 + q]] for q in range(4)])
            encoded = encode_with_halo(turned, bd)
            for q in range(4):
                hidden.append(encoded[128:160, q * 256:(q + 1) * 256])
                hidden.append(encoded[0:128, q * 256:(q + 1) * 256])
                levels.append(turned[0:32, q * 32 + 31:q * 32 + 32])
                levels.append(turned[:, q * 32 + 30:q * 32 + 31])
        h = jnp.concatenate(hidden, axis=0)
        level = jnp.broadcast_to(jnp.concatenate(levels, axis=0), h.shape)
        for layer in range(LAYERS):
            h = h + silu_of_half(layer_half(h, level, layer, w_ref))
        for j in range(TOGETHER):
            at = j * (HALO + BLOCK) + HALO - AHEAD
            ctx_ref[j] = h[at:at + BLOCK].astype(BF)


def last_step(count_ref):
    return jnp.maximum(count_ref[0] - 1, 0) // TOGETHER


def recompute(order, count, pushed, bd, half_weight):
    slots = pushed.shape[0]
    whole = lambda *shape: pl.BlockSpec(shape, lambda i, o, c: (0,) * len(shape))
    return pl.pallas_call(
        recompute_kernel,
        grid_spec=pltpu.PrefetchScalarGridSpec(
            num_scalar_prefetch=2,
            grid=(slots // TOGETHER,),
            in_specs=[whole(slots, PACK, 128), whole(128, 1024), whole(LAYERS, 2, 256, 256)],
            out_specs=pl.BlockSpec(
                (TOGETHER, BLOCK, 256), lambda i, o, c: (jnp.minimum(i, last_step(c)), 0, 0)
            ),
        ),
        out_shape=jax.ShapeDtypeStruct((slots, BLOCK, 256), BF),
        compiler_params=pltpu.CompilerParams(vmem_limit_bytes=48 * MIB),
        cost_estimate=pl.CostEstimate(
            flops=slots * 160 * 2 * 65536 * 10, bytes_accessed=20 * MIB,
            transcendentals=slots * 160 * 256 * 5,
        ),
        name="recompute",
    )(order, count, pushed, bd, half_weight)


def score_kernel(slot_ref, answer_ref, ctx_ref, lat_ref, level_ref, pred_ref, bd_ref,
                 pred_grad_ref, target_grad_ref, stats_ref):
    block = pl.program_id(0)
    raw_pred = dot(ctx_ref[...], pred_ref[...])
    pred_scale = lax.rsqrt(row_sum(raw_pred * raw_pred) + EPSILON)
    unit = raw_pred * pred_scale
    query = unit.astype(BF)
    query_f = query.astype(F32)

    turned = turn([answer_ref[slot_ref[block * NEG + j]] for j in range(NEG)])
    encoded = silu_of_half(dot(turned.astype(BF), bd_ref[...]))
    keys = []
    for j in range(NEG):
        negative = encoded[:, j * 256:(j + 1) * 256]
        key_scale = lax.rsqrt(row_sum(negative * negative) + EPSILON)
        keys.append((negative * key_scale).astype(BF))
    keys = jnp.concatenate(keys, axis=0)

    latent = lat_ref[...].astype(F32)
    usable = jnp.where(level_ref[:, 0:1] > 2.0, 1.0, 0.0)
    own_scale = lax.rsqrt(row_sum(latent * latent) + EPSILON)
    positive = SCALE * row_sum(query_f * latent) * own_scale
    exp_neg = jnp.exp(SCALE * dot_nt(query, keys))
    exp_pos = jnp.exp(positive)
    share = usable / (exp_pos + row_sum(exp_neg))
    d_pos = share * exp_pos - usable
    query_grad = SCALE * (
        dot((exp_neg * share).astype(BF), keys) + (d_pos * own_scale) * latent
    )
    target_grad_ref[...] = (SCALE * d_pos * own_scale) * query_f - (
        d_pos * positive * own_scale * own_scale
    ) * latent
    along = row_sum(unit * query_grad)
    pred_grad_ref[...] = (pred_scale * (query_grad - along * unit)).astype(BF)

    lane = lax.broadcasted_iota(jnp.int32, (BLOCK, 128), 1)
    columns = jnp.where(lane == 0, pred_scale, jnp.where(lane == 1, share, 0.0))
    rows = jnp.transpose(columns)[0:2]

    @pl.when(block == 0)
    def _():
        stats_ref[...] = jnp.zeros_like(stats_ref)

    for j in range(NEG):
        stats_ref[slot_ref[block * NEG + j]] = rows


def score(slots, answers, ctx, latents, levels, pred_weight, bd):
    rows = ctx.shape[0]
    count = answers.shape[0]
    whole = lambda *shape: pl.BlockSpec(shape, lambda i, s: (0,) * len(shape))
    rows_of = lambda width: pl.BlockSpec((BLOCK, width), lambda i, s: (i, 0))
    return pl.pallas_call(
        score_kernel,
        grid_spec=pltpu.PrefetchScalarGridSpec(
            num_scalar_prefetch=1,
            grid=(rows // BLOCK,),
            in_specs=[
                whole(count, PACK, 128), rows_of(256), rows_of(256), rows_of(128),
                whole(256, 256), whole(128, 1024),
            ],
            out_specs=(rows_of(256), rows_of(256), whole(count, 2, 128)),
        ),
        out_shape=(
            jax.ShapeDtypeStruct((rows, 256), BF),
            jax.ShapeDtypeStruct((rows, 256), F32),
            jax.ShapeDtypeStruct((count, 2, 128), F32),
        ),
        compiler_params=pltpu.CompilerParams(vmem_limit_bytes=40 * MIB),
        cost_estimate=pl.CostEstimate(
            flops=rows * 2 * 65536 * 10, bytes_accessed=16 * MIB, transcendentals=rows * 256 * 6
        ),
        name="score",
    )(slots, answers, ctx, latents, levels, pred_weight, bd)


def backward_kernel(pred_grad_ref, slope_ref, level_ref, target_grad_ref, rim_slope_ref,
                    rim_level_ref, pred_ref, w_ref, out_ref, rim_ref, carry):
    @pl.when(pl.program_id(0) == 0)
    def _():
        carry[...] = jnp.zeros_like(carry)

    def earlier(values, distance, place):
        longer = jnp.concatenate([values, carry[place]], axis=0)
        carry[place] = values[0:8]
        return longer[distance:distance + values.shape[0]]

    def through_layers(cotangent, slopes, level):
        for layer in reversed(range(LAYERS)):
            back = cotangent * slopes[layer].astype(F32)
            gated = jnp.where(level > layer, back, 0.0)
            cotangent = (
                cotangent
                + dot_nt(back.astype(BF), w_ref[layer, 0])
                + dot_nt(earlier(gated, 2**layer, layer).astype(BF), w_ref[layer, 1])
            )
        return cotangent

    context_rows = dot_nt(pred_grad_ref[...], pred_ref[...])
    cotangent = earlier(context_rows, AHEAD, LAYERS)
    level = jnp.broadcast_to(level_ref[:, 0:1], (SEGMENT, 256))
    out_ref[...] = through_layers(cotangent, slope_ref, level) + target_grad_ref[...]

    @pl.when(pl.program_id(0) == pl.num_programs(0) - 1)
    def _():
        cotangent = earlier(jnp.zeros((HALO, 256), F32), AHEAD, LAYERS)
        level = jnp.broadcast_to(rim_level_ref[:, 0:1], (HALO, 256))
        rim_ref[...] = through_layers(cotangent, rim_slope_ref, level)


def backward(pred_grad, slopes, levels, target_grad, rim_slopes, rim_levels, pred_weight, weight):
    rows = pred_grad.shape[0]
    steps = rows // SEGMENT
    whole = lambda *shape: pl.BlockSpec(shape, lambda i: (0,) * len(shape))
    rows_of = lambda width: pl.BlockSpec((SEGMENT, width), lambda i: (steps - 1 - i, 0))
    return pl.pallas_call(
        backward_kernel,
        grid=(steps,),
        out_shape=(
            jax.ShapeDtypeStruct((rows, 256), F32),
            jax.ShapeDtypeStruct((HALO, 256), F32),
        ),
        in_specs=[
            rows_of(256),
            pl.BlockSpec((LAYERS, SEGMENT, 256), lambda i: (0, steps - 1 - i, 0)),
            rows_of(128),
            rows_of(256),
            whole(LAYERS, HALO, 256),
            whole(HALO, 128),
            whole(256, 256),
            whole(LAYERS, 2, 256, 256),
        ],
        out_specs=(rows_of(256), whole(HALO, 256)),
        scratch_shapes=[pltpu.VMEM((LAYERS + 1, 8, 256), F32)],
        compiler_params=pltpu.CompilerParams(vmem_limit_bytes=40 * MIB),
        cost_estimate=pl.CostEstimate(
            flops=rows * 2 * 65536 * 9, bytes_accessed=22 * MIB, transcendentals=0
        ),
        name="backward",
    )(pred_grad, slopes, levels, target_grad, rim_slopes, rim_levels, pred_weight, weight)


def own_kernel(order_ref, count_ref, wanted_ref, ctx_ref, stats_ref, keyed_ref, part_ref, lat_ref,
               borrowed_ref, pred_ref, out_ref, total):
    step = pl.program_id(0)
    request_steps = order_ref.shape[0] // TOGETHER

    @pl.when(step == 0)
    def _():
        total[...] = jnp.zeros_like(total)

    @pl.when((step < request_steps) & (step * TOGETHER < count_ref[0]))
    def _():
        for j in range(TOGETHER):
            at = step * TOGETHER + j
            slot = order_ref[at]
            block = jnp.maximum(wanted_ref[slot], 0)
            rows = pl.ds(pl.multiple_of(block * BLOCK, BLOCK), BLOCK)
            stats = stats_ref[slot]
            pred_scale, share = stats[0:1], stats[1:2]
            scores = dot_nt(keyed_ref[rows, :], ctx_ref[j]) * (SCALE * pred_scale)
            weighted = jnp.exp(scores) * (share * pred_scale)
            weighted = jnp.where(at < count_ref[0], weighted, 0.0)
            total[rows, :] += dot(weighted.astype(BF), ctx_ref[j])

    @pl.when(step >= request_steps)
    def _():
        chunk = step - request_steps
        rows = pl.ds(pl.multiple_of(chunk * SEGMENT, SEGMENT), SEGMENT)
        direct = SCALE * dot(total[rows, :].astype(BF), pred_ref[...])
        latent = lat_ref[...].astype(F32)
        key_scale = lax.rsqrt(row_sum(latent * latent) + EPSILON)
        key = latent * key_scale
        out_ref[...] = part_ref[...] + key_scale * (direct - row_sum(key * direct) * key)

        @pl.when(step == pl.num_programs(0) - 1)
        def _():
            out_ref[SEGMENT - HALO:, :] += borrowed_ref[...]


def own(order, count, wanted, ctx, stats, keyed, part, latents, borrowed, pred_weight):
    rows = part.shape[0]
    slots = ctx.shape[0]
    request_steps = slots // TOGETHER
    whole = lambda *shape: pl.BlockSpec(shape, lambda i, o, c, w: (0,) * len(shape))
    chunk_of = pl.BlockSpec(
        (SEGMENT, 256), lambda i, o, c, w: (jnp.maximum(i - request_steps, 0), 0)
    )
    return pl.pallas_call(
        own_kernel,
        grid_spec=pltpu.PrefetchScalarGridSpec(
            num_scalar_prefetch=3,
            grid=(request_steps + rows // SEGMENT,),
            in_specs=[
                pl.BlockSpec(
                    (TOGETHER, BLOCK, 256),
                    lambda i, o, c, w: (jnp.minimum(i, last_step(c)), 0, 0),
                ),
                whole(slots, 2, 128),
                whole(rows, 256),
                chunk_of,
                chunk_of,
                whole(HALO, 256),
                whole(256, 256),
            ],
            out_specs=chunk_of,
            scratch_shapes=[pltpu.VMEM((rows, 256), F32)],
        ),
        out_shape=jax.ShapeDtypeStruct((rows, 256), F32),
        compiler_params=pltpu.CompilerParams(vmem_limit_bytes=40 * MIB),
        name="own",
    )(order, count, wanted, ctx, stats, keyed, part, latents, borrowed, pred_weight)


def shifted(block, axis, distance):
    devices = range(lax.axis_size(axis))
    route = [(i - distance, i) for i in devices if i - distance in devices]
    return lax.ppermute(block, axis, route)


def exchanged(slots):
    owners_count = slots.shape[0] // CAP
    sent = slots.reshape((owners_count, CAP) + slots.shape[1:])
    got = lax.all_to_all(sent, ("tm", "stream"), split_axis=0, concat_axis=0, tiled=True)
    return got.reshape(slots.shape)


def body(raw, starts, neg_owner, neg_block, enc_weight, tcn_weight, pred_weight):
    raw = raw[0]
    owners_count = lax.axis_size("tm") * lax.axis_size("stream")
    rim_starts = jnp.zeros((2, 128), BF).at[0, 128 - HALO:].set(starts[0, -HALO:].astype(BF))
    rim = shifted(jnp.concatenate([raw[:, -128:], rim_starts], axis=0), "tm", 1)
    half_weight = (tcn_weight * 0.5).astype(BF)
    pack, push, slots, bd = prep(
        neg_owner.reshape(-1), neg_block.reshape(-1), raw, starts.reshape(-1, BLOCK), rim,
        enc_weight, owners_count,
    )
    pushed = exchanged(push)
    latents, ctx, slopes, levels, rim_slopes, rim_levels, keyed = forward(
        pack, bd, half_weight, pred_weight
    )
    wanted = pushed[:, PACK - 1, 64].astype(jnp.int32)
    replies, order, count = answer(wanted, pack)
    answers = exchanged(replies)
    request_ctx = recompute(order, count, pushed, bd, half_weight)
    pred_grad, target_grad, stats = score(slots, answers, ctx, latents, levels, pred_weight, bd)
    got_stats = exchanged(stats)
    part, rim_grad = backward(
        pred_grad, slopes, levels, target_grad, rim_slopes, rim_levels, pred_weight, tcn_weight
    )
    borrowed = shifted(rim_grad, "tm", -1)
    return own(
        order, count, wanted, request_ctx, got_stats, keyed, part, latents, borrowed, pred_weight
    )[None]


def solution(mesh):
    placed = (
        P("stream", None, "tm"),
        P("stream", "tm"),
        P("stream", "tm", None),
        P("stream", "tm", None),
        P(),
        P(),
        P(),
    )
    return jax.shard_map(
        body, mesh=mesh, in_specs=placed, out_specs=P("stream", "tm", None), check_vma=False
    )
```

```python
import jax
import jax.numpy as jnp
from jax import lax
from jax.experimental import pallas as pl
from jax.experimental.pallas import tpu as pltpu
from jax.sharding import PartitionSpec as P

BLOCK = 128
NEG = 4
HALO = 32
AHEAD = 4
CAP = 2
LAYERS = 4
PACK = 32
TOGETHER = 16
LEAD = 20
SEGMENT = 512
SCORED = 4
SCALE = 10.0
EPSILON = 1e-06
BF = jnp.bfloat16
F32 = jnp.float32
MIB = 1 << 20
VMEM = 60 * MIB


def dot(a, b):
    return jnp.dot(a, b, preferred_element_type=F32)


def dot_nt(a, b):
    return lax.dot_general(a, b, (((1,), (1,)), ((), ())), preferred_element_type=F32)


def row_sum(x):
    return jnp.sum(x, axis=-1, keepdims=True)


def silu_of_half(half):
    return half + half * jnp.tanh(half)


def prep_kernel(owner_ref, block_ref, raw_ref, starts_ref, rim_ref, enc_ref,
                pack_ref, push_ref, slot_ref, bd_ref, lines, packs, seen):
    blocks = pack_ref.shape[0]
    lines[...] = jnp.zeros_like(lines)
    for b in range(blocks):
        lines[b, 0:6, :] = raw_ref[:, b * 512:(b + 1) * 512].astype(F32)
    row = lax.broadcasted_iota(jnp.int32, (512, 512), 0)
    col = lax.broadcasted_iota(jnp.int32, (512, 512), 1)
    perm = jnp.where(row == 4 * (col & 127) + (col >> 7), 1.0, 0.0).astype(BF)
    row = lax.broadcasted_iota(jnp.int32, (128, 128), 0)
    col = lax.broadcasted_iota(jnp.int32, (128, 128), 1)
    perm_halo = jnp.where(row == 4 * (col & 31) + (col >> 5), 1.0, 0.0).astype(BF)
    flat = lines[...].reshape(blocks * 8, 512).astype(BF)
    main = dot(flat, perm).reshape(blocks, 8, 512)
    halo = dot(flat[:, 384:512], perm_halo).reshape(blocks, 8, 128)
    rim = rim_ref[...]
    rim_halo = dot(rim, perm_halo)

    lane = lax.broadcasted_iota(jnp.int32, (blocks + 8, 128), 1)
    level_row = lax.broadcasted_iota(jnp.int32, (8, 128), 0)
    rim_f = rim.astype(F32)
    before = jnp.where(level_row == 7, pltpu.roll(rim_f, 1, 0), 0.0)
    started = jnp.concatenate([before, starts_ref[...].astype(F32)], axis=0)
    level = 1.0 - started
    for distance in (1, 2, 4):
        moved = pltpu.roll(started, distance, 1)
        started = jnp.maximum(
            started, jnp.where(lane < distance, pltpu.roll(moved, 1, 0), moved)
        )
        level = level + (1.0 - started)
    level_halo = jnp.where(lane < HALO, pltpu.roll(level, HALO, 1), 0.0)

    for k in range(4):
        packs[:, k * 6:(k + 1) * 6, :] = main[:, 0:6, k * 128:(k + 1) * 128]
    packs[0, 24:30, :] = rim_halo[0:6]
    packs[1:blocks, 24:30, :] = halo[0:blocks - 1, 0:6, :]
    for b in range(blocks):
        packs[b, 30:31, :] = level[8 + b:9 + b]
        packs[b, 31:32, :] = level_halo[7 + b:8 + b]
    pack_ref[...] = packs[...].astype(BF)

    at = lax.broadcasted_iota(jnp.int32, (PACK, 128), 0)
    lane = lax.broadcasted_iota(jnp.int32, (PACK, 128), 1)
    note = jnp.where((at == PACK - 1) & (lane >= 64), 1.0, 0.0)
    unused = (-note).astype(BF)

    def clear(i, carry):
        push_ref[i] = unused
        return carry

    lax.fori_loop(0, push_ref.shape[0], clear, 0)

    def forget(i, carry):
        seen[i] = 0
        return carry

    lax.fori_loop(0, seen.shape[0], forget, 0)

    def send(i, carry):
        owner = owner_ref[i]
        rank = seen[owner]
        seen[owner] = rank + 1
        slot = owner * CAP + rank
        slot_ref[i] = slot
        wanted = block_ref[i].astype(F32)
        push_ref[slot] = (packs[i // NEG] + note * wanted).astype(BF)
        return carry

    lax.fori_loop(0, blocks * NEG, send, 0)

    bd_ref[...] = jnp.zeros_like(bd_ref)
    half_enc = (enc_ref[...].astype(F32) * 0.5).astype(BF)
    for q in range(4):
        bd_ref[q * 32:q * 32 + 24, q * 256:(q + 1) * 256] = half_enc


def prep(owners, wanted, raw, starts, rim, enc_weight, owners_count):
    blocks = starts.shape[0]
    smem = pl.BlockSpec(memory_space=pltpu.SMEM)
    vmem = pl.BlockSpec(memory_space=pltpu.VMEM)
    return pl.pallas_call(
        prep_kernel,
        out_shape=(
            jax.ShapeDtypeStruct((blocks, PACK, 128), BF),
            jax.ShapeDtypeStruct((owners_count * CAP, PACK, 128), BF),
            jax.ShapeDtypeStruct((blocks * NEG,), jnp.int32),
            jax.ShapeDtypeStruct((128, 1024), BF),
        ),
        in_specs=[smem, smem, vmem, vmem, vmem, vmem],
        out_specs=(vmem, vmem, smem, vmem),
        scratch_shapes=[
            pltpu.VMEM((blocks, 8, 512), F32),
            pltpu.VMEM((blocks, PACK, 128), F32),
            pltpu.SMEM((owners_count,), jnp.int32),
        ],
        compiler_params=pltpu.CompilerParams(vmem_limit_bytes=VMEM),
        name="prep",
    )(owners, wanted, raw, starts, rim, enc_weight)


def turn(tiles):
    return jnp.transpose(jnp.concatenate(tiles, axis=0).astype(F32))


def encode_with_halo(turned, bd):
    lane = lax.broadcasted_iota(jnp.int32, (HALO, 128), 1) & 31
    halo = jnp.zeros((HALO, 128), F32)
    for k in range(4):
        moved = pltpu.roll(turned[k * 32:(k + 1) * 32], (6 * k - 24) % 128, 1)
        halo = jnp.where((lane >= 6 * k) & (lane < 6 * k + 6), moved, halo)
    rows = jnp.concatenate([turned, halo], axis=0).astype(BF)
    return silu_of_half(dot(rows, bd))


def layer_half(h, level, layer, w_ref):
    moved = pltpu.roll(h, 2**layer, 0)
    gated = jnp.where(level > layer, moved, 0.0)
    return dot(h.astype(BF), w_ref[layer, 0]) + dot(gated.astype(BF), w_ref[layer, 1])


def forward_kernel(pack_ref, bd_ref, w_ref, pred_ref, lat_ref, ctx_ref, slope_ref, level_ref,
                   rim_slope_ref, rim_level_ref, keyed_ref):
    first = pl.program_id(0) == 0
    turned = turn([pack_ref[q] for q in range(4)])
    encoded = encode_with_halo(turned, bd_ref[...])
    latent = jnp.concatenate(
        [encoded[128:160, 0:256]] + [encoded[0:128, q * 256:(q + 1) * 256] for q in range(4)],
        axis=0,
    ).astype(BF)
    columns = [turned[0:32, 31:32]] + [turned[:, q * 32 + 30:q * 32 + 31] for q in range(4)]
    level = jnp.broadcast_to(jnp.concatenate(columns, axis=0), (HALO + SEGMENT, 256))
    level_ref[...] = level[HALO:, 0:128]
    lat_ref[...] = latent[HALO:]
    h = latent.astype(F32)
    own = h[HALO:]
    key_scale = lax.rsqrt(row_sum(own * own) + EPSILON)
    keyed_ref[...] = dot_nt((own * key_scale).astype(BF), pred_ref[...]).astype(BF)
    slopes = []
    for layer in range(LAYERS):
        half = layer_half(h, level, layer, w_ref)
        tanh = jnp.tanh(half)
        slope = (0.5 * (1.0 + tanh)) * (1.0 + half * (1.0 - tanh))
        slope_ref[layer] = slope[HALO:].astype(BF)
        slopes.append(slope[:HALO].astype(BF))
        h = h + half + half * tanh
    ctx_ref[...] = h[HALO - AHEAD:HALO - AHEAD + SEGMENT].astype(BF)

    @pl.when(first)
    def _():
        rim_level_ref[...] = level[:HALO, 0:128]
        for layer in range(LAYERS):
            rim_slope_ref[layer] = slopes[layer]


def forward(pack, bd, half_weight, pred_weight):
    rows = pack.shape[0] * BLOCK
    steps = rows // SEGMENT
    whole = lambda *shape: pl.BlockSpec(shape, lambda i: (0,) * len(shape))
    rows_of = lambda width: pl.BlockSpec((SEGMENT, width), lambda i: (i, 0))
    return pl.pallas_call(
        forward_kernel,
        grid=(steps,),
        out_shape=(
            jax.ShapeDtypeStruct((rows, 256), BF),
            jax.ShapeDtypeStruct((rows, 256), BF),
            jax.ShapeDtypeStruct((LAYERS, rows, 256), BF),
            jax.ShapeDtypeStruct((rows, 128), F32),
            jax.ShapeDtypeStruct((LAYERS, HALO, 256), BF),
            jax.ShapeDtypeStruct((HALO, 128), F32),
            jax.ShapeDtypeStruct((rows, 256), BF),
        ),
        in_specs=[
            pl.BlockSpec((4, PACK, 128), lambda i: (i, 0, 0)),
            whole(128, 1024),
            whole(LAYERS, 2, 256, 256),
            whole(256, 256),
        ],
        out_specs=(
            rows_of(256),
            rows_of(256),
            pl.BlockSpec((LAYERS, SEGMENT, 256), lambda i: (0, i, 0)),
            rows_of(128),
            whole(LAYERS, HALO, 256),
            whole(HALO, 128),
            rows_of(256),
        ),
        compiler_params=pltpu.CompilerParams(vmem_limit_bytes=VMEM),
        cost_estimate=pl.CostEstimate(
            flops=rows * 2 * 65536 * 10, bytes_accessed=18 * MIB, transcendentals=rows * 256 * 5
        ),
        name="forward",
    )(pack, bd, half_weight, pred_weight)


def answer_kernel(push_ref, pack_ref, answer_ref, order_ref, count_ref, wanted_ref, listed, arrived):
    slots = push_ref.shape[0]
    notes = push_ref[:, PACK - 16:, :].astype(F32)[:, 15, :]
    listed[...] = jnp.transpose(notes)[64:72].astype(jnp.int32)
    pltpu.sync_copy(listed, arrived)

    def clear(i, carry):
        order_ref[i] = 0
        return carry

    lax.fori_loop(0, slots, clear, 0, unroll=8)

    def reply(i, count):
        wanted = arrived[0, i]
        wanted_ref[i] = jnp.maximum(wanted, 0)
        answer_ref[i] = pack_ref[jnp.maximum(wanted, 0)]
        order_ref[count] = i
        return count + jnp.where(wanted >= 0, 1, 0)

    count = lax.fori_loop(0, slots, reply, 0, unroll=8)
    count_ref[0] = count


def answer(pushed, pack):
    slots = pushed.shape[0]
    smem = pl.BlockSpec(memory_space=pltpu.SMEM)
    vmem = pl.BlockSpec(memory_space=pltpu.VMEM)
    return pl.pallas_call(
        answer_kernel,
        out_shape=(
            jax.ShapeDtypeStruct((slots, PACK, 128), BF),
            jax.ShapeDtypeStruct((slots + 8,), jnp.int32),
            jax.ShapeDtypeStruct((1,), jnp.int32),
            jax.ShapeDtypeStruct((slots,), jnp.int32),
        ),
        in_specs=[vmem, vmem],
        out_specs=(vmem, smem, smem, smem),
        scratch_shapes=[pltpu.VMEM((8, slots), jnp.int32), pltpu.SMEM((8, slots), jnp.int32)],
        compiler_params=pltpu.CompilerParams(vmem_limit_bytes=VMEM),
        name="answer",
    )(pushed, pack)


def halo_rows(turned):
    lane = lax.broadcasted_iota(jnp.int32, (HALO, 128), 1) & 31
    halo = jnp.where(lane == 30, pltpu.roll(turned[0:HALO], 127, 1), 0.0)
    for k in range(4):
        moved = pltpu.roll(turned[k * 32:(k + 1) * 32], (6 * k - 24) % 128, 1)
        halo = jnp.where((lane >= 6 * k) & (lane < 6 * k + 6), moved, halo)
    return halo


def recompute_kernel(order_ref, count_ref, push_ref, bd_ref, w_ref, ctx_ref,
                     patches, level, here, there, left, right):
    base = pl.program_id(0) * TOGETHER
    times = LEAD + BLOCK - AHEAD

    @pl.when(base < count_ref[0])
    def _():
        for part in range(TOGETHER // 4):
            turned = turn([push_ref[order_ref[base + part * 4 + q]] for q in range(4)])
            halo = halo_rows(turned)
            for q in range(4):
                j = part * 4 + q
                shift = (-32 * q) % 128
                own = pltpu.roll(turned, shift, 1) if q else turned
                before = pltpu.roll(halo, shift, 1) if q else halo
                patches[pl.ds(j, LEAD, stride=TOGETHER), :] = before[HALO - LEAD:]
                patches[pl.ds(LEAD * TOGETHER + j, BLOCK - AHEAD, stride=TOGETHER), :] = own[:BLOCK - AHEAD]
        enc = bd_ref[:, 0:256]
        row = lax.broadcasted_iota(jnp.int32, (128, 128), 0)
        pick = jnp.where(row == 30, 1.0, 0.0).astype(BF)

        def pieces(first, parts):
            edges = [first + (times - first) * p // parts for p in range(parts + 1)]
            return [(a * TOGETHER, b * TOGETHER) for a, b in zip(edges[:-1], edges[1:])]

        for a, b in pieces(0, 4):
            x = patches[a:b, :].astype(BF)
            here[a:b, :] = silu_of_half(dot(x, enc)).astype(BF)
            level[a:b, :] = dot(x, pick).astype(BF)
        source, target = here, there
        first = 0
        for layer in range(LAYERS):
            first += 2**layer if layer else 2
            back = 2**layer * TOGETHER
            for a, b in pieces(first, 4):
                h = source[a:b, :]
                gate = jnp.minimum(jnp.maximum(level[a:b, :] - float(layer), 0.0), 1.0)
                gated = source[a - back:b - back, :] * jnp.concatenate([gate, gate], axis=1)
                half = dot(h, w_ref[layer, 0]) + dot(gated, w_ref[layer, 1])
                result = h.astype(F32) + silu_of_half(half)
                if layer < LAYERS - 1:
                    target[a:b, :] = result.astype(BF)
                else:
                    at = first * TOGETHER
                    left[a - at:b - at, :] = result[:, 0:128]
                    right[a - at:b - at, :] = result[:, 128:256]
            source, target = target, source
        for j in range(TOGETHER):
            rows = pl.ds(j, BLOCK, stride=TOGETHER)
            ctx_ref[j] = jnp.concatenate([left[rows, :], right[rows, :]], axis=1).astype(BF)


def last_step(count_ref):
    return jnp.maximum(count_ref[0] - 1, 0) // TOGETHER


def recompute(order, count, pushed, bd, half_weight):
    slots = pushed.shape[0]
    times = LEAD + BLOCK - AHEAD
    whole = lambda *shape: pl.BlockSpec(shape, lambda i, o, c: (0,) * len(shape))
    return pl.pallas_call(
        recompute_kernel,
        grid_spec=pltpu.PrefetchScalarGridSpec(
            num_scalar_prefetch=2,
            grid=(slots // TOGETHER,),
            in_specs=[whole(slots, PACK, 128), whole(128, 1024), whole(LAYERS, 2, 256, 256)],
            out_specs=pl.BlockSpec(
                (TOGETHER, BLOCK, 256), lambda i, o, c: (jnp.minimum(i, last_step(c)), 0, 0)
            ),
            scratch_shapes=[
                pltpu.VMEM((times * TOGETHER, 128), F32),
                pltpu.VMEM((times * TOGETHER, 128), BF),
                pltpu.VMEM((times * TOGETHER, 256), BF),
                pltpu.VMEM((times * TOGETHER, 256), BF),
                pltpu.VMEM((BLOCK * TOGETHER, 128), F32),
                pltpu.VMEM((BLOCK * TOGETHER, 128), F32),
            ],
        ),
        out_shape=jax.ShapeDtypeStruct((slots, BLOCK, 256), BF),
        compiler_params=pltpu.CompilerParams(vmem_limit_bytes=VMEM),
        cost_estimate=pl.CostEstimate(
            flops=slots * 160 * 2 * 65536 * 10, bytes_accessed=20 * MIB,
            transcendentals=slots * 160 * 256 * 5,
        ),
        name="recompute",
    )(order, count, pushed, bd, half_weight)


def square_sums(x):
    return dot((x * x).astype(BF), jnp.ones((256, 128), BF))


def score_kernel(slot_ref, answer_ref, ctx_ref, lat_ref, level_ref, pred_ref, bd_ref,
                 pred_grad_ref, target_grad_ref, stats_ref):
    step = pl.program_id(0)

    @pl.when(step == 0)
    def _():
        stats_ref[...] = jnp.zeros_like(stats_ref)

    slots = [slot_ref[step * SCORED * NEG + i] for i in range(SCORED * NEG)]
    lane = lax.broadcasted_iota(jnp.int32, (BLOCK, 128), 1)
    raw_preds = dot(ctx_ref[...], pred_ref[...])
    for g in range(SCORED):
        at = slice(g * BLOCK, (g + 1) * BLOCK)
        raw_pred = raw_preds[at]
        pred_scale = lax.rsqrt(row_sum(raw_pred * raw_pred) + EPSILON)
        unit = raw_pred * pred_scale
        query = unit.astype(BF)
        query_f = query.astype(F32)

        turned = turn([answer_ref[slots[g * NEG + j]] for j in range(NEG)])
        encoded = silu_of_half(dot(turned.astype(BF), bd_ref[...]))
        keys = []
        for j in range(NEG):
            negative = encoded[:, j * 256:(j + 1) * 256]
            key_scale = lax.rsqrt(square_sums(negative) + EPSILON)
            keys.append((negative * jnp.concatenate([key_scale, key_scale], axis=1)).astype(BF))
        keys = jnp.concatenate(keys, axis=0)

        latent = lat_ref[at, :].astype(F32)
        usable = jnp.where(level_ref[at, 0:1] > 2.0, 1.0, 0.0)
        own_scale = lax.rsqrt(row_sum(latent * latent) + EPSILON)
        positive = SCALE * row_sum(query_f * latent) * own_scale
        exp_neg = jnp.exp(SCALE * dot_nt(query, keys))
        exp_pos = jnp.exp(positive)
        share = usable / (exp_pos + row_sum(exp_neg))
        d_pos = share * exp_pos - usable
        query_grad = SCALE * (
            dot((exp_neg * share).astype(BF), keys) + (d_pos * own_scale) * latent
        )
        target_grad_ref[at, :] = (SCALE * d_pos * own_scale) * query_f - (
            d_pos * positive * own_scale * own_scale
        ) * latent
        along = row_sum(unit * query_grad)
        pred_grad_ref[at, :] = (pred_scale * (query_grad - along * unit)).astype(BF)
        columns = jnp.where(lane == 0, pred_scale, jnp.where(lane == 1, share, 0.0))
        rows = jnp.transpose(columns)[0:2]
        for j in range(NEG):
            stats_ref[slots[g * NEG + j]] = rows


def score(slots, answers, ctx, latents, levels, pred_weight, bd):
    rows = ctx.shape[0]
    count = answers.shape[0]
    whole = lambda *shape: pl.BlockSpec(shape, lambda i, s: (0,) * len(shape))
    rows_of = lambda width: pl.BlockSpec((SCORED * BLOCK, width), lambda i, s: (i, 0))
    return pl.pallas_call(
        score_kernel,
        grid_spec=pltpu.PrefetchScalarGridSpec(
            num_scalar_prefetch=1,
            grid=(rows // BLOCK // SCORED,),
            in_specs=[
                whole(count, PACK, 128), rows_of(256), rows_of(256), rows_of(128),
                whole(256, 256), whole(128, 1024),
            ],
            out_specs=(rows_of(256), rows_of(256), whole(count, 2, 128)),
        ),
        out_shape=(
            jax.ShapeDtypeStruct((rows, 256), BF),
            jax.ShapeDtypeStruct((rows, 256), F32),
            jax.ShapeDtypeStruct((count, 2, 128), F32),
        ),
        compiler_params=pltpu.CompilerParams(vmem_limit_bytes=VMEM),
        cost_estimate=pl.CostEstimate(
            flops=rows * 2 * 65536 * 10, bytes_accessed=16 * MIB, transcendentals=rows * 256 * 6
        ),
        name="score",
    )(slots, answers, ctx, latents, levels, pred_weight, bd)


def backward_kernel(pred_grad_ref, slope_ref, level_ref, target_grad_ref, rim_slope_ref,
                    rim_level_ref, pred_ref, w_ref, out_ref, rim_ref, carry):
    @pl.when(pl.program_id(0) == 0)
    def _():
        carry[...] = jnp.zeros_like(carry)

    def earlier(values, distance, place):
        longer = jnp.concatenate([values, carry[place]], axis=0)
        carry[place] = values[0:8]
        return longer[distance:distance + values.shape[0]]

    def through_layers(cotangent, slopes, level):
        for layer in reversed(range(LAYERS)):
            back = cotangent * slopes[layer].astype(F32)
            gated = jnp.where(level > layer, back, 0.0)
            cotangent = (
                cotangent
                + dot_nt(back.astype(BF), w_ref[layer, 0])
                + dot_nt(earlier(gated, 2**layer, layer).astype(BF), w_ref[layer, 1])
            )
        return cotangent

    context_rows = dot_nt(pred_grad_ref[...], pred_ref[...])
    cotangent = earlier(context_rows, AHEAD, LAYERS)
    level = jnp.broadcast_to(level_ref[:, 0:1], (SEGMENT, 256))
    out_ref[...] = through_layers(cotangent, slope_ref, level) + target_grad_ref[...]

    @pl.when(pl.program_id(0) == pl.num_programs(0) - 1)
    def _():
        cotangent = earlier(jnp.zeros((HALO, 256), F32), AHEAD, LAYERS)
        level = jnp.broadcast_to(rim_level_ref[:, 0:1], (HALO, 256))
        rim_ref[...] = through_layers(cotangent, rim_slope_ref, level)


def backward(pred_grad, slopes, levels, target_grad, rim_slopes, rim_levels, pred_weight, weight):
    rows = pred_grad.shape[0]
    steps = rows // SEGMENT
    whole = lambda *shape: pl.BlockSpec(shape, lambda i: (0,) * len(shape))
    rows_of = lambda width: pl.BlockSpec((SEGMENT, width), lambda i: (steps - 1 - i, 0))
    return pl.pallas_call(
        backward_kernel,
        grid=(steps,),
        out_shape=(
            jax.ShapeDtypeStruct((rows, 256), F32),
            jax.ShapeDtypeStruct((HALO, 256), F32),
        ),
        in_specs=[
            rows_of(256),
            pl.BlockSpec((LAYERS, SEGMENT, 256), lambda i: (0, steps - 1 - i, 0)),
            rows_of(128),
            rows_of(256),
            whole(LAYERS, HALO, 256),
            whole(HALO, 128),
            whole(256, 256),
            whole(LAYERS, 2, 256, 256),
        ],
        out_specs=(rows_of(256), whole(HALO, 256)),
        scratch_shapes=[pltpu.VMEM((LAYERS + 1, 8, 256), F32)],
        compiler_params=pltpu.CompilerParams(vmem_limit_bytes=VMEM),
        cost_estimate=pl.CostEstimate(
            flops=rows * 2 * 65536 * 9, bytes_accessed=22 * MIB, transcendentals=0
        ),
        name="backward",
    )(pred_grad, slopes, levels, target_grad, rim_slopes, rim_levels, pred_weight, weight)


def own_kernel(order_ref, count_ref, wanted_ref, ctx_ref, stats_ref, keyed_ref, part_ref, lat_ref,
               borrowed_ref, pred_ref, out_ref, total):
    step = pl.program_id(0)
    request_steps = pl.num_programs(0) - total.shape[0] // SEGMENT

    @pl.when(step == 0)
    def _():
        total[...] = jnp.zeros_like(total)

    @pl.when((step < request_steps) & (step * TOGETHER < count_ref[0]))
    def _():
        for part in range(0, TOGETHER, 4):
            found = []
            for j in range(part, part + 4):
                at = step * TOGETHER + j
                slot = order_ref[at]
                block = wanted_ref[slot]
                rows = pl.ds(pl.multiple_of(block * BLOCK, BLOCK), BLOCK)
                stats = stats_ref[slot]
                pred_scale, share = stats[0:1], stats[1:2]
                scores = dot_nt(keyed_ref[rows, :], ctx_ref[j]) * (SCALE * pred_scale)
                weighted = jnp.exp(scores) * (share * pred_scale)
                weighted = jnp.where(at < count_ref[0], weighted, 0.0)
                found.append((rows, dot(weighted.astype(BF), ctx_ref[j])))
            for rows, addend in found:
                total[rows, :] += addend

    @pl.when(step >= request_steps)
    def _():
        chunk = step - request_steps
        rows = pl.ds(pl.multiple_of(chunk * SEGMENT, SEGMENT), SEGMENT)
        direct = SCALE * dot(total[rows, :].astype(BF), pred_ref[...])
        latent = lat_ref[...].astype(F32)
        key_scale = lax.rsqrt(row_sum(latent * latent) + EPSILON)
        key = latent * key_scale
        out_ref[...] = part_ref[...] + key_scale * (direct - row_sum(key * direct) * key)

        @pl.when(step == pl.num_programs(0) - 1)
        def _():
            out_ref[SEGMENT - HALO:, :] += borrowed_ref[...]


def own(order, count, wanted, ctx, stats, keyed, part, latents, borrowed, pred_weight):
    rows = part.shape[0]
    slots = ctx.shape[0]
    request_steps = slots // TOGETHER
    whole = lambda *shape: pl.BlockSpec(shape, lambda i, o, c, w: (0,) * len(shape))
    chunk_of = pl.BlockSpec(
        (SEGMENT, 256), lambda i, o, c, w: (jnp.maximum(i - request_steps, 0), 0)
    )
    return pl.pallas_call(
        own_kernel,
        grid_spec=pltpu.PrefetchScalarGridSpec(
            num_scalar_prefetch=3,
            grid=(request_steps + rows // SEGMENT,),
            in_specs=[
                pl.BlockSpec(
                    (TOGETHER, BLOCK, 256),
                    lambda i, o, c, w: (jnp.minimum(i, last_step(c)), 0, 0),
                ),
                whole(slots, 2, 128),
                whole(rows, 256),
                chunk_of,
                chunk_of,
                whole(HALO, 256),
                whole(256, 256),
            ],
            out_specs=chunk_of,
            scratch_shapes=[pltpu.VMEM((rows, 256), F32)],
        ),
        out_shape=jax.ShapeDtypeStruct((rows, 256), F32),
        compiler_params=pltpu.CompilerParams(vmem_limit_bytes=VMEM),
        name="own",
    )(order, count, wanted, ctx, stats, keyed, part, latents, borrowed, pred_weight)


def shifted(block, axis, distance):
    devices = range(lax.axis_size(axis))
    route = [(i - distance, i) for i in devices if i - distance in devices]
    return lax.ppermute(block, axis, route)


def exchanged(slots):
    owners_count = slots.shape[0] // CAP
    sent = slots.reshape((owners_count, CAP) + slots.shape[1:])
    got = lax.all_to_all(sent, ("tm", "stream"), split_axis=0, concat_axis=0, tiled=True)
    return got.reshape(slots.shape)


def body(raw, starts, neg_owner, neg_block, enc_weight, tcn_weight, pred_weight):
    raw = raw[0]
    owners_count = lax.axis_size("tm") * lax.axis_size("stream")
    rim_starts = jnp.concatenate(
        [jnp.zeros((1, 128 - HALO), BF), starts[:, -HALO:].astype(BF)], axis=1
    )
    rim = shifted(jnp.concatenate([raw[:, -128:], rim_starts, rim_starts], axis=0), "tm", 1)
    half_weight = (tcn_weight * 0.5).astype(BF)
    pack, push, slots, bd = prep(
        neg_owner.reshape(-1), neg_block.reshape(-1), raw, starts.reshape(-1, BLOCK), rim,
        enc_weight, owners_count,
    )
    pushed = exchanged(push)
    latents, ctx, slopes, levels, rim_slopes, rim_levels, keyed = forward(
        pack, bd, half_weight, pred_weight
    )
    pushed, ctx = lax.optimization_barrier((pushed, ctx))
    replies, order, count, wanted = answer(pushed, pack)
    answers = exchanged(replies)
    request_ctx = recompute(order, count, pushed, bd, half_weight)
    answers, request_ctx = lax.optimization_barrier((answers, request_ctx))
    pred_grad, target_grad, stats = score(slots, answers, ctx, latents, levels, pred_weight, bd)
    got_stats = exchanged(stats)
    part, rim_grad = backward(
        pred_grad, slopes, levels, target_grad, rim_slopes, rim_levels, pred_weight, tcn_weight
    )
    borrowed = shifted(rim_grad, "tm", -1)
    return own(
        order, count, wanted, request_ctx, got_stats, keyed, part, latents, borrowed, pred_weight
    )[None]


def solution(mesh):
    placed = (
        P("stream", None, "tm"),
        P("stream", "tm"),
        P("stream", "tm", None),
        P("stream", "tm", None),
        P(),
        P(),
        P(),
    )
    return jax.shard_map(
        body, mesh=mesh, in_specs=placed, out_specs=P("stream", "tm", None), check_vma=False
    )
```

```python
import jax
import jax.numpy as jnp
from jax import lax
from jax.experimental import pallas as pl
from jax.experimental.pallas import tpu as pltpu
from jax.sharding import PartitionSpec as P

BLOCK = 128
NEG = 4
HALO = 32
AHEAD = 4
CAP = 2
LAYERS = 4
PACK = 32
TOGETHER = 16
PAIRED = 1
PIECES = 4
SKEW = 1
GATHERED = 64
CHUNK = 1024
NOTE = 95
LEAD = 20
SEGMENT = 512
SCORED = 4
SCALE = 10.0
EPSILON = 1e-06
BF = jnp.bfloat16
F32 = jnp.float32
MIB = 1 << 20
VMEM = 60 * MIB


def dot(a, b):
    return jnp.dot(a, b, preferred_element_type=F32)


def dot_nt(a, b):
    return lax.dot_general(a, b, (((1,), (1,)), ((), ())), preferred_element_type=F32)


def row_sum(x):
    return jnp.sum(x, axis=-1, keepdims=True)


def silu_of_half(half):
    return half + half * jnp.tanh(half)


def wide(x):
    return jnp.concatenate([x, x], axis=1)


def prep_kernel(owner_ref, block_ref, raw_ref, starts_ref, rim_ref, enc_ref,
                pack_ref, push_ref, slot_ref, bd_ref, lines, packs, turned, seen):
    blocks = pack_ref.shape[0]
    lines[...] = jnp.zeros_like(lines)
    for b in range(blocks):
        lines[b, 0:6, :] = raw_ref[:, b * 512:(b + 1) * 512].astype(F32)
    row = lax.broadcasted_iota(jnp.int32, (512, 512), 0)
    col = lax.broadcasted_iota(jnp.int32, (512, 512), 1)
    perm = jnp.where(row == 4 * (col & 127) + (col >> 7), 1.0, 0.0).astype(BF)
    row = lax.broadcasted_iota(jnp.int32, (128, 128), 0)
    col = lax.broadcasted_iota(jnp.int32, (128, 128), 1)
    perm_halo = jnp.where(row == 4 * (col & 31) + (col >> 5), 1.0, 0.0).astype(BF)
    flat = lines[...].reshape(blocks * 8, 512).astype(BF)
    main = dot(flat, perm).reshape(blocks, 8, 512)
    halo = dot(flat[:, 384:512], perm_halo).reshape(blocks, 8, 128)
    rim = rim_ref[...]
    rim_halo = dot(rim, perm_halo)

    lane = lax.broadcasted_iota(jnp.int32, (blocks + 8, 128), 1)
    level_row = lax.broadcasted_iota(jnp.int32, (8, 128), 0)
    rim_f = rim.astype(F32)
    before = jnp.where(level_row == 7, pltpu.roll(rim_f, 1, 0), 0.0)
    started = jnp.concatenate([before, starts_ref[...].astype(F32)], axis=0)
    level = 1.0 - started
    for distance in (1, 2, 4):
        moved = pltpu.roll(started, distance, 1)
        started = jnp.maximum(
            started, jnp.where(lane < distance, pltpu.roll(moved, 1, 0), moved)
        )
        level = level + (1.0 - started)
    level_halo = jnp.where(lane < HALO, pltpu.roll(level, HALO, 1), 0.0)

    for k in range(4):
        packs[:, k * 6:(k + 1) * 6, :] = main[:, 0:6, k * 128:(k + 1) * 128]
    packs[0, 24:30, :] = rim_halo[0:6]
    packs[1:blocks, 24:30, :] = halo[0:blocks - 1, 0:6, :]
    for b in range(blocks):
        packs[b, 30:31, :] = level[8 + b:9 + b]
        packs[b, 31:32, :] = level_halo[7 + b:8 + b]
    quarter = lax.broadcasted_iota(jnp.int32, (PACK, 128), 1) >> 5
    for group in range(blocks // 4):
        four = [packs[group * 4 + q] for q in range(4)]
        parts = []
        for g in range(4):
            part = four[g]
            for q in range(4):
                if q != g:
                    part = jnp.where(quarter == q, pltpu.roll(four[q], (q - g) * 32 % 128, 1), part)
            parts.append(part)
        flipped = jnp.transpose(jnp.concatenate(parts, axis=0))
        for q in range(4):
            turned[group * 4 + q] = flipped[q * 32:(q + 1) * 32]
    pack_ref[...] = turned[...].astype(BF)

    lane = lax.broadcasted_iota(jnp.int32, (PACK, 128), 1)
    note = jnp.where(lane == NOTE, 1.0, 0.0)
    unused = (-note).astype(BF)

    def clear(i, carry):
        push_ref[i] = unused
        return carry

    lax.fori_loop(0, push_ref.shape[0], clear, 0, unroll=8)

    def forget(i, carry):
        seen[i] = 0
        return carry

    lax.fori_loop(0, seen.shape[0], forget, 0, unroll=8)

    def send(i, carry):
        owner = owner_ref[i % NEG, i // NEG]
        rank = seen[owner]
        seen[owner] = rank + 1
        slot = owner * CAP + rank
        slot_ref[i] = slot
        wanted = block_ref[i % NEG, i // NEG].astype(F32)
        push_ref[slot] = (turned[i // NEG] + note * wanted).astype(BF)
        return carry

    lax.fori_loop(0, blocks * NEG, send, 0, unroll=4)

    bd_ref[...] = jnp.zeros_like(bd_ref)
    half_enc = (enc_ref[...].astype(F32) * 0.5).astype(BF)
    for q in range(4):
        bd_ref[q * 32:q * 32 + 24, q * 256:(q + 1) * 256] = half_enc


def prep(owners, wanted, raw, starts, rim, enc_weight, owners_count):
    blocks = starts.shape[0]
    smem = pl.BlockSpec(memory_space=pltpu.SMEM)
    vmem = pl.BlockSpec(memory_space=pltpu.VMEM)
    return pl.pallas_call(
        prep_kernel,
        out_shape=(
            jax.ShapeDtypeStruct((blocks, PACK, 128), BF),
            jax.ShapeDtypeStruct((owners_count * CAP, PACK, 128), BF),
            jax.ShapeDtypeStruct((blocks * NEG,), jnp.int32),
            jax.ShapeDtypeStruct((128, 1024), BF),
        ),
        in_specs=[smem, smem, vmem, vmem, vmem, vmem],
        out_specs=(vmem, vmem, smem, vmem),
        scratch_shapes=[
            pltpu.VMEM((blocks, 8, 512), F32),
            pltpu.VMEM((blocks, PACK, 128), F32),
            pltpu.VMEM((blocks, PACK, 128), F32),
            pltpu.SMEM((owners_count,), jnp.int32),
        ],
        compiler_params=pltpu.CompilerParams(vmem_limit_bytes=VMEM),
        name="prep",
    )(owners, wanted, raw, starts, rim, enc_weight)


def halo_rows(pack):
    lane = lax.broadcasted_iota(jnp.int32, (HALO, 128), 1)
    halo = jnp.where(lane == 30, pltpu.roll(pack, 127, 1), 0.0)
    for g in range(4):
        moved = pltpu.roll(pack, (-26 * g - 24) % 128, 1)
        halo = jnp.where((lane >= 6 * g) & (lane < 6 * g + 6), moved, halo)
    return halo


def layer_half(h, level, layer, w_ref):
    moved = pltpu.roll(h, 2**layer, 0)
    gated = jnp.where(level > layer, moved, 0.0)
    return dot(h.astype(BF), w_ref[layer, 0]) + dot(gated.astype(BF), w_ref[layer, 1])


def forward_kernel(pack_ref, bd_ref, w_ref, pred_ref, lat_ref, ctx_ref, slope_ref, level_ref,
                   rim_slope_ref, rim_level_ref, keyed_ref):
    first = pl.program_id(0) == 0
    packs = pack_ref[...].reshape(4 * PACK, 128).astype(F32)
    halo = halo_rows(packs[0:PACK])
    rows = jnp.concatenate([packs, halo], axis=0)
    encoded = silu_of_half(dot(rows.astype(BF), bd_ref[...]))
    pieces, columns = [encoded[4 * PACK:, 0:256]], [halo[:, 30:31]]
    for q in range(4):
        for g in range(4):
            pieces.append(encoded[q * PACK:(q + 1) * PACK, g * 256:(g + 1) * 256])
            columns.append(packs[q * PACK:(q + 1) * PACK, g * 32 + 30:g * 32 + 31])
    latent = jnp.concatenate(pieces, axis=0).astype(BF)
    level = jnp.broadcast_to(jnp.concatenate(columns, axis=0), (HALO + SEGMENT, 256))
    level_ref[...] = level[HALO:, 0:128]
    lat_ref[...] = latent[HALO:]
    h = latent.astype(F32)
    own = h[HALO:]
    key_scale = lax.rsqrt(row_sum(own * own) + EPSILON)
    keyed_ref[...] = dot_nt((own * key_scale).astype(BF), pred_ref[...]).astype(BF)
    slopes = []
    for layer in range(LAYERS):
        half = layer_half(h, level, layer, w_ref)
        tanh = jnp.tanh(half)
        slope = (0.5 * (1.0 + tanh)) * (1.0 + half * (1.0 - tanh))
        slope_ref[layer] = slope[HALO:].astype(BF)
        slopes.append(slope[:HALO].astype(BF))
        h = h + half + half * tanh
    ctx_ref[...] = h[HALO - AHEAD:HALO - AHEAD + SEGMENT].astype(BF)

    @pl.when(first)
    def _():
        rim_level_ref[...] = level[:HALO, 0:128]
        for layer in range(LAYERS):
            rim_slope_ref[layer] = slopes[layer]


def forward(pack, bd, half_weight, pred_weight):
    rows = pack.shape[0] * BLOCK
    steps = rows // SEGMENT
    whole = lambda *shape: pl.BlockSpec(shape, lambda i: (0,) * len(shape))
    rows_of = lambda width: pl.BlockSpec((SEGMENT, width), lambda i: (i, 0))
    return pl.pallas_call(
        forward_kernel,
        grid=(steps,),
        out_shape=(
            jax.ShapeDtypeStruct((rows, 256), BF),
            jax.ShapeDtypeStruct((rows, 256), BF),
            jax.ShapeDtypeStruct((LAYERS, rows, 256), BF),
            jax.ShapeDtypeStruct((rows, 128), F32),
            jax.ShapeDtypeStruct((LAYERS, HALO, 256), BF),
            jax.ShapeDtypeStruct((HALO, 128), F32),
            jax.ShapeDtypeStruct((rows, 256), BF),
        ),
        in_specs=[
            pl.BlockSpec((4, PACK, 128), lambda i: (i, 0, 0)),
            whole(128, 1024),
            whole(LAYERS, 2, 256, 256),
            whole(256, 256),
        ],
        out_specs=(
            rows_of(256),
            rows_of(256),
            pl.BlockSpec((LAYERS, SEGMENT, 256), lambda i: (0, i, 0)),
            rows_of(128),
            whole(LAYERS, HALO, 256),
            whole(HALO, 128),
            rows_of(256),
        ),
        compiler_params=pltpu.CompilerParams(vmem_limit_bytes=VMEM),
        cost_estimate=pl.CostEstimate(
            flops=rows * 2 * 65536 * 10, bytes_accessed=18 * MIB, transcendentals=rows * 256 * 5
        ),
        name="forward",
    )(pack, bd, half_weight, pred_weight)


def kept(count, half):
    shared = ((count - half + 63) >> 6) << 5
    return jnp.where(count > half, jnp.minimum(count, half + shared), count)


def answer_kernel(push_ref, pack_ref, answer_ref, order_ref, bounds_ref, wanted_ref, extra_ref,
                  listed, arrived):
    slots = push_ref.shape[0]
    half = slots // 2
    notes = push_ref[:, 0:16, :].astype(F32)[:, 0, :]
    listed[...] = jnp.transpose(notes)[NOTE:NOTE + 1].astype(jnp.int32)
    pltpu.sync_copy(listed, arrived)

    def clear(i, carry):
        order_ref[i] = 0
        return carry

    lax.fori_loop(0, slots, clear, 0, unroll=8)

    def reply(i, count):
        wanted = arrived[0, i]
        wanted_ref[i] = jnp.maximum(wanted, 0)
        answer_ref[i] = pack_ref[jnp.maximum(wanted, 0)]
        order_ref[count] = i
        return count + jnp.where(wanted >= 0, 1, 0)

    count = lax.fori_loop(0, slots, reply, 0, unroll=8)
    bounds_ref[0] = 0
    bounds_ref[1] = kept(count, half)
    bounds_ref[2] = count
    extra_ref[...] = jnp.zeros_like(extra_ref)
    extra_ref[half] = jnp.full((PACK, 128), count.astype(F32)).astype(BF)

    def share(i, carry):
        extra_ref[i - half] = push_ref[order_ref[i]]
        return carry

    lax.fori_loop(half, jnp.maximum(count, half), share, 0)


def answer(pushed, pack):
    slots = pushed.shape[0]
    smem = pl.BlockSpec(memory_space=pltpu.SMEM)
    vmem = pl.BlockSpec(memory_space=pltpu.VMEM)
    return pl.pallas_call(
        answer_kernel,
        out_shape=(
            jax.ShapeDtypeStruct((slots, PACK, 128), BF),
            jax.ShapeDtypeStruct((slots + 8,), jnp.int32),
            jax.ShapeDtypeStruct((3,), jnp.int32),
            jax.ShapeDtypeStruct((slots,), jnp.int32),
            jax.ShapeDtypeStruct((slots // 2 + 1, PACK, 128), BF),
        ),
        in_specs=[vmem, vmem],
        out_specs=(vmem, smem, smem, smem, vmem),
        scratch_shapes=[pltpu.VMEM((1, slots), jnp.int32), pltpu.SMEM((1, slots), jnp.int32)],
        compiler_params=pltpu.CompilerParams(vmem_limit_bytes=VMEM),
        name="answer",
    )(pushed, pack)


def request_stages(base, order_ref, push_ref, bd_ref, w_ref, ctx_ref, first_out,
                   patches, level, here, there, left, right, gated, half_ref):
    times = LEAD + BLOCK - AHEAD

    def pieces(first, parts=PIECES):
        edges = [first + (times - first) * p // parts for p in range(parts + 1)]
        return [(a * TOGETHER, b * TOGETHER) for a, b in zip(edges[:-1], edges[1:])]

    def parts(a, b):
        return [slice(c, min(c + 32, b)) for c in range(a, b, 32)]

    for j in range(TOGETHER):
        pack = push_ref[order_ref[base + j]].astype(F32)
        patches[pl.ds(j, LEAD, stride=TOGETHER), :] = halo_rows(pack)[HALO - LEAD:]
        for g in range(4):
            count = min(32, BLOCK - AHEAD - g * 32)
            own = pltpu.roll(pack, -32 * g % 128, 1) if g else pack
            at = (LEAD + g * 32) * TOGETHER + j
            patches[pl.ds(at, count, stride=TOGETHER), :] = own[:count]
        if j % 4 == 3:
            yield
    enc = bd_ref[:, 0:256]
    for a, b in pieces(0):
        half_ref[a:b, :] = dot(patches[a:b, :].astype(BF), enc).astype(BF)
        yield
        level[a:b, :] = jnp.broadcast_to(patches[a:b, 30:31], (b - a, 128)).astype(BF)
        for at in parts(a, b):
            here[at, :] = silu_of_half(half_ref[at, :])
        yield
    source, target = here, there
    first = 0
    for layer in range(LAYERS):
        first += 2**layer if layer else 2
        back = 2**layer * TOGETHER
        both = w_ref[layer].reshape(512, 256)
        for a, b in pieces(first):
            for at in parts(a, b):
                gate = jnp.minimum(jnp.maximum(level[at, :] - float(layer), 0.0), 1.0)
                gated[at, :] = source[at.start - back:at.stop - back, :] * wide(gate)
            yield
            x = jnp.concatenate([source[a:b, :], gated[a:b, :]], axis=1)
            half_ref[a:b, :] = dot(x, both).astype(BF)
            yield
            for at in parts(a, b):
                result = source[at, :] + silu_of_half(half_ref[at, :])
                if layer < LAYERS - 1:
                    target[at, :] = result
                else:
                    result = result.astype(F32)
                    to = slice(at.start - first * TOGETHER, at.stop - first * TOGETHER)
                    left[to, :] = result[:, 0:128]
                    right[to, :] = result[:, 128:256]
            yield
        source, target = target, source
    for j in range(TOGETHER):
        rows = pl.ds(j, BLOCK, stride=TOGETHER)
        ctx_ref[first_out + j] = jnp.concatenate([left[rows, :], right[rows, :]], axis=1).astype(BF)
        if j % 4 == 3:
            yield


def recompute_kernel(order_ref, bounds_ref, push_ref, bd_ref, w_ref, ctx_ref, *scratch):
    base = bounds_ref[0] + pl.program_id(0) * PAIRED * TOGETHER

    @pl.when(base < bounds_ref[1])
    def _():
        each = len(scratch) // PAIRED
        waiting = [
            request_stages(
                base + p * TOGETHER, order_ref, push_ref, bd_ref, w_ref, ctx_ref, p * TOGETHER,
                *scratch[p * each:(p + 1) * each],
            )
            for p in range(PAIRED)
        ]
        for p, stages in enumerate(waiting):
            for _ in range(SKEW * (PAIRED - 1 - p)):
                next(stages)
        while waiting:
            waiting = [stages for stages in waiting if next(stages, True) is None]


def last_step(count, together):
    return jnp.maximum(count - 1, 0) // together


def recompute(order, bounds, pushed, bd, half_weight):
    slots = order.shape[0] // TOGETHER * TOGETHER
    together = PAIRED * TOGETHER
    times = LEAD + BLOCK - AHEAD
    whole = lambda *shape: pl.BlockSpec(shape, lambda i, o, c: (0,) * len(shape))
    return pl.pallas_call(
        recompute_kernel,
        grid_spec=pltpu.PrefetchScalarGridSpec(
            num_scalar_prefetch=2,
            grid=(slots // TOGETHER // PAIRED,),
            in_specs=[whole(*pushed.shape), whole(128, 1024), whole(LAYERS, 2, 256, 256)],
            out_specs=pl.BlockSpec(
                (together, BLOCK, 256),
                lambda i, o, c: (
                    jnp.minimum(c[0] // together + i, last_step(c[1], together)), 0, 0
                ),
            ),
            scratch_shapes=[
                pltpu.VMEM((times * TOGETHER, 128), F32),
                pltpu.VMEM((times * TOGETHER, 128), BF),
                pltpu.VMEM((times * TOGETHER, 256), BF),
                pltpu.VMEM((times * TOGETHER, 256), BF),
                pltpu.VMEM((BLOCK * TOGETHER, 128), F32),
                pltpu.VMEM((BLOCK * TOGETHER, 128), F32),
                pltpu.VMEM((times * TOGETHER, 256), BF),
                pltpu.VMEM((times * TOGETHER, 256), BF),
            ] * PAIRED,
        ),
        out_shape=jax.ShapeDtypeStruct((slots, BLOCK, 256), BF),
        compiler_params=pltpu.CompilerParams(vmem_limit_bytes=VMEM),
        cost_estimate=pl.CostEstimate(
            flops=slots * 160 * 2 * 65536 * 10, bytes_accessed=20 * MIB,
            transcendentals=slots * 160 * 256 * 5,
        ),
        name="recompute",
    )(order, bounds, pushed, bd, half_weight)


def score_kernel(slot_ref, answer_ref, ctx_ref, lat_ref, level_ref, pred_ref, bd_ref,
                 pred_grad_ref, target_grad_ref, stats_ref):
    step = pl.program_id(0)

    @pl.when(step == 0)
    def _():
        stats_ref[...] = jnp.zeros_like(stats_ref)

    blocks = range(SCORED)
    slots = [slot_ref[step * SCORED * NEG + i] for i in range(SCORED * NEG)]
    lane = lax.broadcasted_iota(jnp.int32, (BLOCK, 128), 1)
    ats = [slice(g * BLOCK, (g + 1) * BLOCK) for g in blocks]
    packs = [
        jnp.concatenate([answer_ref[slots[g * NEG + j]] for j in range(NEG)], axis=0) for g in blocks
    ]
    raw_pred = [dot(ctx_ref[at, :], pred_ref[...]) for at in ats]
    half = [dot(pack, bd_ref[...]) for pack in packs]
    pred_scale = [lax.rsqrt(row_sum(x * x) + EPSILON) for x in raw_pred]
    unit = [x * y for x, y in zip(raw_pred, pred_scale)]
    query = [x.astype(BF) for x in unit]
    keys = []
    for g in blocks:
        pieces = []
        for j in range(4):
            negative = silu_of_half(half[g][:, j * 256:(j + 1) * 256])
            key_scale = lax.rsqrt(row_sum(negative * negative) + EPSILON)
            pieces.append((negative * (key_scale)).astype(BF))
        keys.append(jnp.concatenate(pieces, axis=0))
    scores = [dot_nt(query[g], keys[g]) for g in blocks]
    exp_neg = [jnp.exp(SCALE * x) for x in scores]
    both = [dot(exp_neg[g].astype(BF), keys[g]) for g in blocks]
    sums = [row_sum(x) for x in exp_neg]
    columns = jnp.zeros((BLOCK, 128), F32)
    for g in blocks:
        at = ats[g]
        query_f = query[g].astype(F32)
        latent = lat_ref[at, :].astype(F32)
        usable = jnp.where(level_ref[at, 0:1] > 2.0, 1.0, 0.0)
        own_scale = lax.rsqrt(row_sum(latent * latent) + EPSILON)
        positive = SCALE * row_sum(query_f * latent) * own_scale
        exp_pos = jnp.exp(positive)
        share = usable / (exp_pos + sums[g])
        d_pos = share * exp_pos - usable
        pull = SCALE * d_pos * own_scale
        query_grad = (SCALE * share) * both[g] + (pull) * latent
        target_grad_ref[at, :] = (
            (pull) * query_f - (d_pos * positive * own_scale * own_scale) * latent
        )
        along = row_sum(unit[g] * query_grad)
        pred_grad_ref[at, :] = (
            (pred_scale[g]) * (query_grad - (along) * unit[g])
        ).astype(BF)
        columns = jnp.where(lane == 2 * g, pred_scale[g], columns)
        columns = jnp.where(lane == 2 * g + 1, share, columns)
    rows = jnp.transpose(columns)
    for i in range(SCORED * NEG):
        g = i // NEG
        stats_ref[slots[i]] = rows[2 * g:2 * g + 2]


def score(slots, answers, ctx, latents, levels, pred_weight, bd):
    rows = ctx.shape[0]
    count = answers.shape[0]
    whole = lambda *shape: pl.BlockSpec(shape, lambda i, s: (0,) * len(shape))
    rows_of = lambda width: pl.BlockSpec((SCORED * BLOCK, width), lambda i, s: (i, 0))
    return pl.pallas_call(
        score_kernel,
        grid_spec=pltpu.PrefetchScalarGridSpec(
            num_scalar_prefetch=1,
            grid=(rows // BLOCK // SCORED,),
            in_specs=[
                whole(count, PACK, 128), rows_of(256), rows_of(256), rows_of(128),
                whole(256, 256), whole(128, 1024),
            ],
            out_specs=(rows_of(256), rows_of(256), whole(count, 2, 128)),
        ),
        out_shape=(
            jax.ShapeDtypeStruct((rows, 256), BF),
            jax.ShapeDtypeStruct((rows, 256), F32),
            jax.ShapeDtypeStruct((count, 2, 128), F32),
        ),
        compiler_params=pltpu.CompilerParams(vmem_limit_bytes=VMEM),
        cost_estimate=pl.CostEstimate(
            flops=rows * 2 * 65536 * 10, bytes_accessed=16 * MIB, transcendentals=rows * 256 * 6
        ),
        name="score",
    )(slots, answers, ctx, latents, levels, pred_weight, bd)


def backward_kernel(pred_grad_ref, slope_ref, level_ref, target_grad_ref, rim_slope_ref,
                    rim_level_ref, pred_ref, w_ref, out_ref, rim_ref, carry):
    @pl.when(pl.program_id(0) == 0)
    def _():
        carry[...] = jnp.zeros_like(carry)

    def earlier(values, distance, place):
        longer = jnp.concatenate([values, carry[place]], axis=0)
        carry[place] = values[0:8]
        return longer[distance:distance + values.shape[0]]

    def through_layers(cotangent, slopes, level):
        for layer in reversed(range(LAYERS)):
            back = cotangent * slopes[layer].astype(F32)
            gated = jnp.where(level > layer, back, 0.0)
            cotangent = (
                cotangent
                + dot(
                    jnp.concatenate([back, earlier(gated, 2**layer, layer)], axis=1).astype(BF),
                    w_ref[layer].reshape(512, 256),
                )
            )
        return cotangent

    context_rows = dot(pred_grad_ref[...], pred_ref[...])
    cotangent = earlier(context_rows, AHEAD, LAYERS)
    level = wide(level_ref[...])
    out_ref[...] = through_layers(cotangent, slope_ref, level) + target_grad_ref[...]

    @pl.when(pl.program_id(0) == pl.num_programs(0) - 1)
    def _():
        cotangent = earlier(jnp.zeros((HALO, 256), F32), AHEAD, LAYERS)
        level = wide(rim_level_ref[...])
        rim_ref[...] = through_layers(cotangent, rim_slope_ref, level)


def backward(pred_grad, slopes, levels, target_grad, rim_slopes, rim_levels, pred_weight, weight):
    rows = pred_grad.shape[0]
    steps = rows // SEGMENT
    whole = lambda *shape: pl.BlockSpec(shape, lambda i: (0,) * len(shape))
    rows_of = lambda width: pl.BlockSpec((SEGMENT, width), lambda i: (steps - 1 - i, 0))
    return pl.pallas_call(
        backward_kernel,
        grid=(steps,),
        out_shape=(
            jax.ShapeDtypeStruct((rows, 256), F32),
            jax.ShapeDtypeStruct((HALO, 256), F32),
        ),
        in_specs=[
            rows_of(256),
            pl.BlockSpec((LAYERS, SEGMENT, 256), lambda i: (0, steps - 1 - i, 0)),
            rows_of(128),
            rows_of(256),
            whole(LAYERS, HALO, 256),
            whole(HALO, 128),
            whole(256, 256),
            whole(LAYERS, 2, 256, 256),
        ],
        out_specs=(rows_of(256), whole(HALO, 256)),
        scratch_shapes=[pltpu.VMEM((LAYERS + 1, 8, 256), F32)],
        compiler_params=pltpu.CompilerParams(vmem_limit_bytes=VMEM),
        cost_estimate=pl.CostEstimate(
            flops=rows * 2 * 65536 * 9, bytes_accessed=22 * MIB, transcendentals=0
        ),
        name="backward",
    )(pred_grad, slopes, levels, target_grad, rim_slopes, rim_levels, pred_weight, weight)


def own_kernel(order_ref, bounds_ref, wanted_ref, ctx_ref, help_ref, stats_ref, keyed_ref, part_ref, lat_ref,
               borrowed_ref, pred_ref, out_ref, total):
    step = pl.program_id(0)
    request_steps = pl.num_programs(0) - total.shape[0] // CHUNK

    @pl.when(step == 0)
    def _():
        total[...] = jnp.zeros_like(total)

    @pl.when((step < request_steps) & (step * GATHERED < bounds_ref[2]))
    def _():
        for part in range(0, GATHERED, 4):
            found = []
            for j in range(part, part + 4):
                at = step * GATHERED + j
                slot = order_ref[at]
                block = wanted_ref[slot]
                rows = pl.ds(pl.multiple_of(block * BLOCK, BLOCK), BLOCK)
                stats = stats_ref[slot]
                helped = jnp.where(at < bounds_ref[2], help_ref[j], jnp.zeros((BLOCK, 256), BF))
                ctx = jnp.where(at < bounds_ref[1], ctx_ref[j], helped)
                pred_scale, share = stats[0:1], stats[1:2]
                scores = dot_nt(keyed_ref[rows, :], ctx) * (SCALE * pred_scale)
                weighted = jnp.exp(scores) * (share * pred_scale)
                weighted = jnp.where(at < bounds_ref[2], weighted, 0.0)
                found.append((rows, dot(weighted.astype(BF), ctx)))
            for rows, addend in found:
                total[rows, :] += addend

    @pl.when(step >= request_steps)
    def _():
        chunk = step - request_steps
        rows = pl.ds(pl.multiple_of(chunk * CHUNK, CHUNK), CHUNK)
        direct = SCALE * dot(total[rows, :].astype(BF), pred_ref[...])
        latent = lat_ref[...].astype(F32)
        key_scale = lax.rsqrt(row_sum(latent * latent) + EPSILON)
        key = latent * key_scale
        along = row_sum(key * direct)
        out_ref[...] = part_ref[...] + key_scale * (direct - along * key)

        @pl.when(step == pl.num_programs(0) - 1)
        def _():
            out_ref[CHUNK - HALO:, :] += borrowed_ref[...]


def own(order, bounds, wanted, ctx, helped, stats, keyed, part, latents, borrowed, pred_weight):
    rows = part.shape[0]
    slots = ctx.shape[0]
    request_steps = slots // GATHERED
    first_help = slots // 2 // GATHERED
    whole = lambda *shape: pl.BlockSpec(shape, lambda i, o, c, w: (0,) * len(shape))
    chunk_of = pl.BlockSpec(
        (CHUNK, 256), lambda i, o, c, w: (jnp.maximum(i - request_steps, 0), 0)
    )
    return pl.pallas_call(
        own_kernel,
        grid_spec=pltpu.PrefetchScalarGridSpec(
            num_scalar_prefetch=3,
            grid=(request_steps + rows // CHUNK,),
            in_specs=[
                pl.BlockSpec(
                    (GATHERED, BLOCK, 256),
                    lambda i, o, c, w: (jnp.minimum(i, last_step(c[1], GATHERED)), 0, 0),
                ),
                pl.BlockSpec(
                    (GATHERED, BLOCK, 256),
                    lambda i, o, c, w: (
                        jnp.clip(i - first_help, 0, last_step(c[2] - slots // 2, GATHERED)), 0, 0
                    ),
                ),
                whole(slots, 2, 128),
                whole(rows, 256),
                chunk_of,
                chunk_of,
                whole(HALO, 256),
                whole(256, 256),
            ],
            out_specs=chunk_of,
            scratch_shapes=[pltpu.VMEM((rows, 256), F32)],
        ),
        out_shape=jax.ShapeDtypeStruct((rows, 256), F32),
        compiler_params=pltpu.CompilerParams(vmem_limit_bytes=VMEM),
        name="own",
    )(order, bounds, wanted, ctx, helped, stats, keyed, part, latents, borrowed, pred_weight)


def shifted(block, axis, distance):
    devices = range(lax.axis_size(axis))
    route = [(i - distance, i) for i in devices if i - distance in devices]
    return lax.ppermute(block, axis, route)


def swapped(block, axis):
    return lax.ppermute(block, axis, [(i, i ^ 1) for i in range(lax.axis_size(axis))])


def exchanged(slots):
    owners_count = slots.shape[0] // CAP
    sent = slots.reshape((owners_count, CAP) + slots.shape[1:])
    got = lax.all_to_all(sent, ("tm", "stream"), split_axis=0, concat_axis=0, tiled=True)
    return got.reshape(slots.shape)


def body(raw, starts, neg_owner, neg_block, enc_weight, tcn_weight, pred_weight):
    raw = raw[0]
    owners_count = lax.axis_size("tm") * lax.axis_size("stream")
    rim_starts = jnp.concatenate(
        [jnp.zeros((1, 128 - HALO), BF), starts[:, -HALO:].astype(BF)], axis=1
    )
    rim = shifted(jnp.concatenate([raw[:, -128:], rim_starts, rim_starts], axis=0), "tm", 1)
    half_weight = (tcn_weight * 0.5).astype(BF)
    tcn_back = jnp.swapaxes(tcn_weight, 2, 3)
    pred_back = pred_weight.T
    pack, push, slots, bd = prep(
        neg_owner[0].T, neg_block[0].T, raw, starts.reshape(-1, BLOCK), rim,
        enc_weight, owners_count,
    )
    pushed = exchanged(push)
    latents, ctx, slopes, levels, rim_slopes, rim_levels, keyed = forward(
        pack, bd, half_weight, pred_weight
    )
    pushed, ctx = lax.optimization_barrier((pushed, ctx))
    replies, order, bounds, wanted, extra = answer(pushed, pack)
    answers = exchanged(replies)
    half = order.shape[0] // TOGETHER * TOGETHER // 2
    shared = swapped(extra, "tm")
    request_ctx = recompute(order, bounds, pushed, bd, half_weight)
    mate_count = shared[half, 0, 0].astype(jnp.int32)
    mate_bounds = jnp.stack([kept(mate_count, half) - half, mate_count - half])
    helped = swapped(
        recompute(
            lax.iota(jnp.int32, half), jnp.maximum(mate_bounds, 0), shared, bd, half_weight
        ),
        "tm",
    )
    answers, request_ctx = lax.optimization_barrier((answers, request_ctx))
    pred_grad, target_grad, stats = score(slots, answers, ctx, latents, levels, pred_weight, bd)
    got_stats = exchanged(stats)
    part, rim_grad = backward(
        pred_grad, slopes, levels, target_grad, rim_slopes, rim_levels, pred_back, tcn_back
    )
    borrowed = shifted(rim_grad, "tm", -1)
    return own(
        order, bounds, wanted, request_ctx, helped, got_stats, keyed, part, latents, borrowed, pred_weight
    )[None]


def solution(mesh):
    placed = (
        P("stream", None, "tm"),
        P("stream", "tm"),
        P("stream", "tm", None),
        P("stream", "tm", None),
        P(),
        P(),
        P(),
    )
    return jax.shard_map(
        body, mesh=mesh, in_specs=placed, out_specs=P("stream", "tm", None), check_vma=False
    )
```

```python
import jax
import jax.numpy as jnp
from jax import lax
from jax.experimental import pallas as pl
from jax.experimental.pallas import tpu as pltpu
from jax.sharding import PartitionSpec as P

BLOCK = 128
NEG = 4
HALO = 32
AHEAD = 4
CAP = 2
LAYERS = 4
PACK = 32
TOGETHER = 16
PAIRED = 1
PIECES = 4
SKEW = 1
GATHERED = 64
CHUNK = 1024
NOTE = 95
LEAD = 20
SEGMENT = 512
SCORED = 4
SCALE = 10.0
EPSILON = 1e-06
BF = jnp.bfloat16
F32 = jnp.float32
MIB = 1 << 20
VMEM = 60 * MIB


def dot(a, b):
    return jnp.dot(a, b, preferred_element_type=F32)


def dot_nt(a, b):
    return lax.dot_general(a, b, (((1,), (1,)), ((), ())), preferred_element_type=F32)


def row_sum(x):
    return jnp.sum(x, axis=-1, keepdims=True)


def silu_of_half(half):
    return half + half * jnp.tanh(half)


def wide(x):
    return jnp.concatenate([x, x], axis=1)


def prep_kernel(owner_ref, block_ref, raw_ref, starts_ref, rim_ref, enc_ref,
                pack_ref, push_ref, slot_ref, bd_ref, lines, packs, turned, seen):
    blocks = pack_ref.shape[0]
    lines[...] = jnp.zeros_like(lines)
    for b in range(blocks):
        lines[b, 0:6, :] = raw_ref[:, b * 512:(b + 1) * 512].astype(F32)
    row = lax.broadcasted_iota(jnp.int32, (512, 512), 0)
    col = lax.broadcasted_iota(jnp.int32, (512, 512), 1)
    perm = jnp.where(row == 4 * (col & 127) + (col >> 7), 1.0, 0.0).astype(BF)
    row = lax.broadcasted_iota(jnp.int32, (128, 128), 0)
    col = lax.broadcasted_iota(jnp.int32, (128, 128), 1)
    perm_halo = jnp.where(row == 4 * (col & 31) + (col >> 5), 1.0, 0.0).astype(BF)
    flat = lines[...].reshape(blocks * 8, 512).astype(BF)
    main = dot(flat, perm).reshape(blocks, 8, 512)
    halo = dot(flat[:, 384:512], perm_halo).reshape(blocks, 8, 128)
    rim = rim_ref[...]
    rim_halo = dot(rim, perm_halo)

    lane = lax.broadcasted_iota(jnp.int32, (blocks + 8, 128), 1)
    level_row = lax.broadcasted_iota(jnp.int32, (8, 128), 0)
    rim_f = rim.astype(F32)
    before = jnp.where(level_row == 7, pltpu.roll(rim_f, 1, 0), 0.0)
    started = jnp.concatenate([before, starts_ref[...].astype(F32)], axis=0)
    level = 1.0 - started
    for distance in (1, 2, 4):
        moved = pltpu.roll(started, distance, 1)
        started = jnp.maximum(
            started, jnp.where(lane < distance, pltpu.roll(moved, 1, 0), moved)
        )
        level = level + (1.0 - started)
    level_halo = jnp.where(lane < HALO, pltpu.roll(level, HALO, 1), 0.0)

    for k in range(4):
        packs[:, k * 6:(k + 1) * 6, :] = main[:, 0:6, k * 128:(k + 1) * 128]
    packs[0, 24:30, :] = rim_halo[0:6]
    packs[1:blocks, 24:30, :] = halo[0:blocks - 1, 0:6, :]
    for b in range(blocks):
        packs[b, 30:31, :] = level[8 + b:9 + b]
        packs[b, 31:32, :] = level_halo[7 + b:8 + b]
    quarter = lax.broadcasted_iota(jnp.int32, (PACK, 128), 1) >> 5
    for group in range(blocks // 4):
        four = [packs[group * 4 + q] for q in range(4)]
        parts = []
        for g in range(4):
            part = four[g]
            for q in range(4):
                if q != g:
                    part = jnp.where(quarter == q, pltpu.roll(four[q], (q - g) * 32 % 128, 1), part)
            parts.append(part)
        flipped = jnp.transpose(jnp.concatenate(parts, axis=0))
        for q in range(4):
            turned[group * 4 + q] = flipped[q * 32:(q + 1) * 32]
    pack_ref[...] = turned[...].astype(BF)

    lane = lax.broadcasted_iota(jnp.int32, (PACK, 128), 1)
    note = jnp.where(lane == NOTE, 1.0, 0.0)
    unused = (-note).astype(BF)

    def clear(i, carry):
        push_ref[i] = unused
        return carry

    lax.fori_loop(0, push_ref.shape[0], clear, 0, unroll=8)

    def forget(i, carry):
        seen[i] = 0
        return carry

    lax.fori_loop(0, seen.shape[0], forget, 0, unroll=8)

    def send(i, carry):
        owner = owner_ref[i % NEG, i // NEG]
        rank = seen[owner]
        seen[owner] = rank + 1
        slot = owner * CAP + rank
        slot_ref[i] = slot
        wanted = block_ref[i % NEG, i // NEG].astype(F32)
        push_ref[slot] = (turned[i // NEG] + note * wanted).astype(BF)
        return carry

    lax.fori_loop(0, blocks * NEG, send, 0, unroll=4)

    bd_ref[...] = jnp.zeros_like(bd_ref)
    half_enc = (enc_ref[...].astype(F32) * 0.5).astype(BF)
    for q in range(4):
        bd_ref[q * 32:q * 32 + 24, q * 256:(q + 1) * 256] = half_enc


def prep(owners, wanted, raw, starts, rim, enc_weight, owners_count):
    blocks = starts.shape[0]
    smem = pl.BlockSpec(memory_space=pltpu.SMEM)
    vmem = pl.BlockSpec(memory_space=pltpu.VMEM)
    return pl.pallas_call(
        prep_kernel,
        out_shape=(
            jax.ShapeDtypeStruct((blocks, PACK, 128), BF),
            jax.ShapeDtypeStruct((owners_count * CAP, PACK, 128), BF),
            jax.ShapeDtypeStruct((blocks * NEG,), jnp.int32),
            jax.ShapeDtypeStruct((128, 1024), BF),
        ),
        in_specs=[smem, smem, vmem, vmem, vmem, vmem],
        out_specs=(vmem, vmem, smem, vmem),
        scratch_shapes=[
            pltpu.VMEM((blocks, 8, 512), F32),
            pltpu.VMEM((blocks, PACK, 128), F32),
            pltpu.VMEM((blocks, PACK, 128), F32),
            pltpu.SMEM((owners_count,), jnp.int32),
        ],
        compiler_params=pltpu.CompilerParams(vmem_limit_bytes=VMEM),
        name="prep",
    )(owners, wanted, raw, starts, rim, enc_weight)


def halo_rows(pack):
    lane = lax.broadcasted_iota(jnp.int32, (HALO, 128), 1)
    halo = jnp.where(lane == 30, pltpu.roll(pack, 127, 1), 0.0)
    for g in range(4):
        moved = pltpu.roll(pack, (-26 * g - 24) % 128, 1)
        halo = jnp.where((lane >= 6 * g) & (lane < 6 * g + 6), moved, halo)
    return halo


def layer_half(h, level, layer, w_ref):
    moved = pltpu.roll(h, 2**layer, 0)
    gated = jnp.where(level > layer, moved, 0.0)
    return dot(h.astype(BF), w_ref[layer, 0]) + dot(gated.astype(BF), w_ref[layer, 1])


def forward_kernel(pack_ref, bd_ref, w_ref, pred_ref, lat_ref, ctx_ref, slope_ref, level_ref,
                   rim_slope_ref, rim_level_ref, keyed_ref):
    first = pl.program_id(0) == 0
    packs = pack_ref[...].reshape(4 * PACK, 128).astype(F32)
    halo = halo_rows(packs[0:PACK])
    rows = jnp.concatenate([packs, halo], axis=0)
    encoded = silu_of_half(dot(rows.astype(BF), bd_ref[...]))
    pieces, columns = [encoded[4 * PACK:, 0:256]], [halo[:, 30:31]]
    for q in range(4):
        for g in range(4):
            pieces.append(encoded[q * PACK:(q + 1) * PACK, g * 256:(g + 1) * 256])
            columns.append(packs[q * PACK:(q + 1) * PACK, g * 32 + 30:g * 32 + 31])
    latent = jnp.concatenate(pieces, axis=0).astype(BF)
    level = jnp.broadcast_to(jnp.concatenate(columns, axis=0), (HALO + SEGMENT, 256))
    level_ref[...] = level[HALO:, 0:128]
    lat_ref[...] = latent[HALO:]
    h = latent.astype(F32)
    own = h[HALO:]
    key_scale = lax.rsqrt(row_sum(own * own) + EPSILON)
    keyed_ref[...] = dot_nt((own * key_scale).astype(BF), pred_ref[...]).astype(BF)
    slopes = []
    for layer in range(LAYERS):
        half = layer_half(h, level, layer, w_ref)
        tanh = jnp.tanh(half)
        slope = (0.5 * (1.0 + tanh)) * (1.0 + half * (1.0 - tanh))
        slope_ref[layer] = slope[HALO:].astype(BF)
        slopes.append(slope[:HALO].astype(BF))
        h = h + half + half * tanh
    ctx_ref[...] = h[HALO - AHEAD:HALO - AHEAD + SEGMENT].astype(BF)

    @pl.when(first)
    def _():
        rim_level_ref[...] = level[:HALO, 0:128]
        for layer in range(LAYERS):
            rim_slope_ref[layer] = slopes[layer]


def forward(pack, bd, half_weight, pred_weight):
    rows = pack.shape[0] * BLOCK
    steps = rows // SEGMENT
    whole = lambda *shape: pl.BlockSpec(shape, lambda i: (0,) * len(shape))
    rows_of = lambda width: pl.BlockSpec((SEGMENT, width), lambda i: (i, 0))
    return pl.pallas_call(
        forward_kernel,
        grid=(steps,),
        out_shape=(
            jax.ShapeDtypeStruct((rows, 256), BF),
            jax.ShapeDtypeStruct((rows, 256), BF),
            jax.ShapeDtypeStruct((LAYERS, rows, 256), BF),
            jax.ShapeDtypeStruct((rows, 128), F32),
            jax.ShapeDtypeStruct((LAYERS, HALO, 256), BF),
            jax.ShapeDtypeStruct((HALO, 128), F32),
            jax.ShapeDtypeStruct((rows, 256), BF),
        ),
        in_specs=[
            pl.BlockSpec((4, PACK, 128), lambda i: (i, 0, 0)),
            whole(128, 1024),
            whole(LAYERS, 2, 256, 256),
            whole(256, 256),
        ],
        out_specs=(
            rows_of(256),
            rows_of(256),
            pl.BlockSpec((LAYERS, SEGMENT, 256), lambda i: (0, i, 0)),
            rows_of(128),
            whole(LAYERS, HALO, 256),
            whole(HALO, 128),
            rows_of(256),
        ),
        compiler_params=pltpu.CompilerParams(vmem_limit_bytes=VMEM),
        cost_estimate=pl.CostEstimate(
            flops=rows * 2 * 65536 * 10, bytes_accessed=18 * MIB, transcendentals=rows * 256 * 5
        ),
        name="forward",
    )(pack, bd, half_weight, pred_weight)


def kept(count, half):
    shared = ((count - half + 63) >> 6) << 5
    return jnp.where(count > half, jnp.minimum(count, half + shared), count)


def answer_kernel(push_ref, pack_ref, answer_ref, order_ref, bounds_ref, wanted_ref, extra_ref,
                  listed, arrived):
    slots = push_ref.shape[0]
    half = slots // 2
    notes = push_ref[:, 0:16, :].astype(F32)[:, 0, :]
    listed[...] = jnp.transpose(notes)[NOTE:NOTE + 1].astype(jnp.int32)
    pltpu.sync_copy(listed, arrived)

    def clear(i, carry):
        order_ref[i] = 0
        return carry

    lax.fori_loop(0, slots, clear, 0, unroll=8)

    def reply(i, count):
        wanted = arrived[0, i]
        wanted_ref[i] = jnp.maximum(wanted, 0)
        answer_ref[i] = pack_ref[jnp.maximum(wanted, 0)]
        order_ref[count] = i
        return count + jnp.where(wanted >= 0, 1, 0)

    count = lax.fori_loop(0, slots, reply, 0, unroll=8)
    bounds_ref[0] = 0
    bounds_ref[1] = kept(count, half)
    bounds_ref[2] = count
    extra_ref[...] = jnp.zeros_like(extra_ref)
    extra_ref[half] = jnp.full((PACK, 128), count.astype(F32)).astype(BF)

    def share(i, carry):
        extra_ref[i - half] = push_ref[order_ref[i]]
        return carry

    lax.fori_loop(half, jnp.maximum(count, half), share, 0)


def answer(pushed, pack):
    slots = pushed.shape[0]
    smem = pl.BlockSpec(memory_space=pltpu.SMEM)
    vmem = pl.BlockSpec(memory_space=pltpu.VMEM)
    return pl.pallas_call(
        answer_kernel,
        out_shape=(
            jax.ShapeDtypeStruct((slots, PACK, 128), BF),
            jax.ShapeDtypeStruct((slots + 8,), jnp.int32),
            jax.ShapeDtypeStruct((3,), jnp.int32),
            jax.ShapeDtypeStruct((slots,), jnp.int32),
            jax.ShapeDtypeStruct((slots // 2 + 1, PACK, 128), BF),
        ),
        in_specs=[vmem, vmem],
        out_specs=(vmem, smem, smem, smem, vmem),
        scratch_shapes=[pltpu.VMEM((1, slots), jnp.int32), pltpu.SMEM((1, slots), jnp.int32)],
        compiler_params=pltpu.CompilerParams(vmem_limit_bytes=VMEM),
        name="answer",
    )(pushed, pack)


def request_stages(base, order_ref, push_ref, bd_ref, w_ref, ctx_ref, first_out,
                   patches, level, here, there, left, right, gated, half_ref):
    times = LEAD + BLOCK - AHEAD

    def pieces(first, parts=PIECES):
        edges = [first + (times - first) * p // parts for p in range(parts + 1)]
        return [(a * TOGETHER, b * TOGETHER) for a, b in zip(edges[:-1], edges[1:])]

    def parts(a, b):
        return [slice(c, min(c + 32, b)) for c in range(a, b, 32)]

    for j in range(TOGETHER):
        pack = push_ref[order_ref[base + j]].astype(F32)
        patches[pl.ds(j, LEAD, stride=TOGETHER), :] = halo_rows(pack)[HALO - LEAD:]
        for g in range(4):
            count = min(32, BLOCK - AHEAD - g * 32)
            own = pltpu.roll(pack, -32 * g % 128, 1) if g else pack
            at = (LEAD + g * 32) * TOGETHER + j
            patches[pl.ds(at, count, stride=TOGETHER), :] = own[:count]
        if j % 4 == 3:
            yield
    enc = bd_ref[:, 0:256]
    for a, b in pieces(0):
        half_ref[a:b, :] = dot(patches[a:b, :].astype(BF), enc).astype(BF)
        yield
        level[a:b, :] = jnp.broadcast_to(patches[a:b, 30:31], (b - a, 128)).astype(BF)
        for at in parts(a, b):
            here[at, :] = silu_of_half(half_ref[at, :])
        yield
    source, target = here, there
    first = 0
    for layer in range(LAYERS):
        first += 2**layer if layer else 2
        back = 2**layer * TOGETHER
        both = w_ref[layer].reshape(512, 256)
        for a, b in pieces(first):
            for at in parts(a, b):
                gate = jnp.minimum(jnp.maximum(level[at, :] - float(layer), 0.0), 1.0)
                gated[at, :] = source[at.start - back:at.stop - back, :] * wide(gate)
            yield
            x = jnp.concatenate([source[a:b, :], gated[a:b, :]], axis=1)
            half_ref[a:b, :] = dot(x, both).astype(BF)
            yield
            for at in parts(a, b):
                result = source[at, :] + silu_of_half(half_ref[at, :])
                if layer < LAYERS - 1:
                    target[at, :] = result
                else:
                    result = result.astype(F32)
                    to = slice(at.start - first * TOGETHER, at.stop - first * TOGETHER)
                    left[to, :] = result[:, 0:128]
                    right[to, :] = result[:, 128:256]
            yield
        source, target = target, source
    for j in range(TOGETHER):
        rows = pl.ds(j, BLOCK, stride=TOGETHER)
        ctx_ref[first_out + j] = jnp.concatenate([left[rows, :], right[rows, :]], axis=1).astype(BF)
        if j % 4 == 3:
            yield


def recompute_kernel(order_ref, bounds_ref, push_ref, bd_ref, w_ref, ctx_ref, *scratch):
    base = bounds_ref[0] + pl.program_id(0) * PAIRED * TOGETHER

    @pl.when(base < bounds_ref[1])
    def _():
        each = len(scratch) // PAIRED
        waiting = [
            request_stages(
                base + p * TOGETHER, order_ref, push_ref, bd_ref, w_ref, ctx_ref, p * TOGETHER,
                *scratch[p * each:(p + 1) * each],
            )
            for p in range(PAIRED)
        ]
        for p, stages in enumerate(waiting):
            for _ in range(SKEW * (PAIRED - 1 - p)):
                next(stages)
        while waiting:
            waiting = [stages for stages in waiting if next(stages, True) is None]


def last_step(count, together):
    return jnp.maximum(count - 1, 0) // together


def recompute(order, bounds, pushed, bd, half_weight):
    slots = order.shape[0] // TOGETHER * TOGETHER
    together = PAIRED * TOGETHER
    times = LEAD + BLOCK - AHEAD
    whole = lambda *shape: pl.BlockSpec(shape, lambda i, o, c: (0,) * len(shape))
    return pl.pallas_call(
        recompute_kernel,
        grid_spec=pltpu.PrefetchScalarGridSpec(
            num_scalar_prefetch=2,
            grid=(slots // TOGETHER // PAIRED,),
            in_specs=[whole(*pushed.shape), whole(128, 1024), whole(LAYERS, 2, 256, 256)],
            out_specs=pl.BlockSpec(
                (together, BLOCK, 256),
                lambda i, o, c: (
                    jnp.minimum(c[0] // together + i, last_step(c[1], together)), 0, 0
                ),
            ),
            scratch_shapes=[
                pltpu.VMEM((times * TOGETHER, 128), F32),
                pltpu.VMEM((times * TOGETHER, 128), BF),
                pltpu.VMEM((times * TOGETHER, 256), BF),
                pltpu.VMEM((times * TOGETHER, 256), BF),
                pltpu.VMEM((BLOCK * TOGETHER, 128), F32),
                pltpu.VMEM((BLOCK * TOGETHER, 128), F32),
                pltpu.VMEM((times * TOGETHER, 256), BF),
                pltpu.VMEM((times * TOGETHER, 256), BF),
            ] * PAIRED,
        ),
        out_shape=jax.ShapeDtypeStruct((slots, BLOCK, 256), BF),
        compiler_params=pltpu.CompilerParams(vmem_limit_bytes=VMEM),
        cost_estimate=pl.CostEstimate(
            flops=slots * 160 * 2 * 65536 * 10, bytes_accessed=20 * MIB,
            transcendentals=slots * 160 * 256 * 5,
        ),
        name="recompute",
    )(order, bounds, pushed, bd, half_weight)


def score_kernel(slot_ref, answer_ref, ctx_ref, lat_ref, level_ref, pred_ref, bd_ref,
                 pred_grad_ref, target_grad_ref, stats_ref):
    step = pl.program_id(0)

    @pl.when(step == 0)
    def _():
        stats_ref[...] = jnp.zeros_like(stats_ref)

    blocks = range(SCORED)
    slots = [slot_ref[step * SCORED * NEG + i] for i in range(SCORED * NEG)]
    lane = lax.broadcasted_iota(jnp.int32, (BLOCK, 128), 1)
    ats = [slice(g * BLOCK, (g + 1) * BLOCK) for g in blocks]
    packs = [
        jnp.concatenate([answer_ref[slots[g * NEG + j]] for j in range(NEG)], axis=0) for g in blocks
    ]
    raw_pred = [dot(ctx_ref[at, :], pred_ref[...]) for at in ats]
    half = [dot(pack, bd_ref[...]) for pack in packs]
    pred_scale = [lax.rsqrt(row_sum(x * x) + EPSILON) for x in raw_pred]
    unit = [x * y for x, y in zip(raw_pred, pred_scale)]
    query = [x.astype(BF) for x in unit]
    keys = []
    for g in blocks:
        pieces = []
        for j in range(4):
            negative = silu_of_half(half[g][:, j * 256:(j + 1) * 256])
            key_scale = lax.rsqrt(row_sum(negative * negative) + EPSILON)
            pieces.append((negative * (key_scale)).astype(BF))
        keys.append(jnp.concatenate(pieces, axis=0))
    scores = [dot_nt(query[g], keys[g]) for g in blocks]
    exp_neg = [jnp.exp(SCALE * x) for x in scores]
    both = [dot(exp_neg[g].astype(BF), keys[g]) for g in blocks]
    sums = [row_sum(x) for x in exp_neg]
    columns = jnp.zeros((BLOCK, 128), F32)
    for g in blocks:
        at = ats[g]
        query_f = query[g].astype(F32)
        latent = lat_ref[at, :].astype(F32)
        usable = jnp.where(level_ref[at, 0:1] > 2.0, 1.0, 0.0)
        own_scale = lax.rsqrt(row_sum(latent * latent) + EPSILON)
        positive = SCALE * row_sum(query_f * latent) * own_scale
        exp_pos = jnp.exp(positive)
        share = usable / (exp_pos + sums[g])
        d_pos = share * exp_pos - usable
        pull = SCALE * d_pos * own_scale
        query_grad = (SCALE * share) * both[g] + (pull) * latent
        target_grad_ref[at, :] = (
            (pull) * query_f - (d_pos * positive * own_scale * own_scale) * latent
        )
        along = row_sum(unit[g] * query_grad)
        pred_grad_ref[at, :] = (
            (pred_scale[g]) * (query_grad - (along) * unit[g])
        ).astype(BF)
        columns = jnp.where(lane == 2 * g, pred_scale[g], columns)
        columns = jnp.where(lane == 2 * g + 1, share, columns)
    rows = jnp.transpose(columns)
    for i in range(SCORED * NEG):
        g = i // NEG
        stats_ref[slots[i]] = rows[2 * g:2 * g + 2]


def score(slots, answers, ctx, latents, levels, pred_weight, bd):
    rows = ctx.shape[0]
    count = answers.shape[0]
    whole = lambda *shape: pl.BlockSpec(shape, lambda i, s: (0,) * len(shape))
    rows_of = lambda width: pl.BlockSpec((SCORED * BLOCK, width), lambda i, s: (i, 0))
    return pl.pallas_call(
        score_kernel,
        grid_spec=pltpu.PrefetchScalarGridSpec(
            num_scalar_prefetch=1,
            grid=(rows // BLOCK // SCORED,),
            in_specs=[
                whole(count, PACK, 128), rows_of(256), rows_of(256), rows_of(128),
                whole(256, 256), whole(128, 1024),
            ],
            out_specs=(rows_of(256), rows_of(256), whole(count, 2, 128)),
        ),
        out_shape=(
            jax.ShapeDtypeStruct((rows, 256), BF),
            jax.ShapeDtypeStruct((rows, 256), F32),
            jax.ShapeDtypeStruct((count, 2, 128), F32),
        ),
        compiler_params=pltpu.CompilerParams(vmem_limit_bytes=VMEM),
        cost_estimate=pl.CostEstimate(
            flops=rows * 2 * 65536 * 10, bytes_accessed=16 * MIB, transcendentals=rows * 256 * 6
        ),
        name="score",
    )(slots, answers, ctx, latents, levels, pred_weight, bd)


def backward_kernel(pred_grad_ref, slope_ref, level_ref, target_grad_ref, rim_slope_ref,
                    rim_level_ref, pred_ref, w_ref, out_ref, rim_ref, carry):
    @pl.when(pl.program_id(0) == 0)
    def _():
        carry[...] = jnp.zeros_like(carry)

    def earlier(values, distance, place):
        longer = jnp.concatenate([values, carry[place]], axis=0)
        carry[place] = values[0:8]
        return longer[distance:distance + values.shape[0]]

    def through_layers(cotangent, slopes, level):
        for layer in reversed(range(LAYERS)):
            back = cotangent * slopes[layer].astype(F32)
            gated = jnp.where(level > layer, back, 0.0)
            cotangent = (
                cotangent
                + dot(
                    jnp.concatenate([back, earlier(gated, 2**layer, layer)], axis=1).astype(BF),
                    w_ref[layer].reshape(512, 256),
                )
            )
        return cotangent

    context_rows = dot(pred_grad_ref[...], pred_ref[...])
    cotangent = earlier(context_rows, AHEAD, LAYERS)
    level = wide(level_ref[...])
    out_ref[...] = through_layers(cotangent, slope_ref, level) + target_grad_ref[...]

    @pl.when(pl.program_id(0) == pl.num_programs(0) - 1)
    def _():
        cotangent = earlier(jnp.zeros((HALO, 256), F32), AHEAD, LAYERS)
        level = wide(rim_level_ref[...])
        rim_ref[...] = through_layers(cotangent, rim_slope_ref, level)


def backward(pred_grad, slopes, levels, target_grad, rim_slopes, rim_levels, pred_weight, weight):
    rows = pred_grad.shape[0]
    steps = rows // SEGMENT
    whole = lambda *shape: pl.BlockSpec(shape, lambda i: (0,) * len(shape))
    rows_of = lambda width: pl.BlockSpec((SEGMENT, width), lambda i: (steps - 1 - i, 0))
    return pl.pallas_call(
        backward_kernel,
        grid=(steps,),
        out_shape=(
            jax.ShapeDtypeStruct((rows, 256), F32),
            jax.ShapeDtypeStruct((HALO, 256), F32),
        ),
        in_specs=[
            rows_of(256),
            pl.BlockSpec((LAYERS, SEGMENT, 256), lambda i: (0, steps - 1 - i, 0)),
            rows_of(128),
            rows_of(256),
            whole(LAYERS, HALO, 256),
            whole(HALO, 128),
            whole(256, 256),
            whole(LAYERS, 2, 256, 256),
        ],
        out_specs=(rows_of(256), whole(HALO, 256)),
        scratch_shapes=[pltpu.VMEM((LAYERS + 1, 8, 256), F32)],
        compiler_params=pltpu.CompilerParams(vmem_limit_bytes=VMEM),
        cost_estimate=pl.CostEstimate(
            flops=rows * 2 * 65536 * 9, bytes_accessed=22 * MIB, transcendentals=0
        ),
        name="backward",
    )(pred_grad, slopes, levels, target_grad, rim_slopes, rim_levels, pred_weight, weight)


def own_kernel(order_ref, bounds_ref, wanted_ref, ctx_ref, help_ref, stats_ref, keyed_ref, part_ref, lat_ref,
               borrowed_ref, pred_ref, out_ref, total):
    step = pl.program_id(0)
    request_steps = pl.num_programs(0) - total.shape[0] // CHUNK

    @pl.when(step == 0)
    def _():
        total[...] = jnp.zeros_like(total)

    @pl.when((step < request_steps) & (step * GATHERED < bounds_ref[2]))
    def _():
        for part in range(0, GATHERED, 4):
            found = []
            for j in range(part, part + 4):
                at = step * GATHERED + j
                slot = order_ref[at]
                block = wanted_ref[slot]
                rows = pl.ds(pl.multiple_of(block * BLOCK, BLOCK), BLOCK)
                stats = stats_ref[slot]
                helped = jnp.where(at < bounds_ref[2], help_ref[j], jnp.zeros((BLOCK, 256), BF))
                ctx = jnp.where(at < bounds_ref[1], ctx_ref[j], helped)
                pred_scale, share = stats[0:1], stats[1:2]
                scores = dot_nt(keyed_ref[rows, :], ctx) * (SCALE * pred_scale)
                weighted = jnp.exp(scores) * (share * pred_scale)
                weighted = jnp.where(at < bounds_ref[2], weighted, 0.0)
                found.append((rows, dot(weighted.astype(BF), ctx)))
            for rows, addend in found:
                total[rows, :] += addend

    @pl.when(step >= request_steps)
    def _():
        chunk = step - request_steps
        rows = pl.ds(pl.multiple_of(chunk * CHUNK, CHUNK), CHUNK)
        direct = SCALE * dot(total[rows, :].astype(BF), pred_ref[...])
        latent = lat_ref[...].astype(F32)
        key_scale = lax.rsqrt(row_sum(latent * latent) + EPSILON)
        key = latent * key_scale
        along = row_sum(key * direct)
        out_ref[...] = part_ref[...] + key_scale * (direct - along * key)

        @pl.when(step == pl.num_programs(0) - 1)
        def _():
            out_ref[CHUNK - HALO:, :] += borrowed_ref[...]


def own(order, bounds, wanted, ctx, helped, stats, keyed, part, latents, borrowed, pred_weight):
    rows = part.shape[0]
    slots = ctx.shape[0]
    request_steps = slots // GATHERED
    first_help = slots // 2 // GATHERED
    whole = lambda *shape: pl.BlockSpec(shape, lambda i, o, c, w: (0,) * len(shape))
    chunk_of = pl.BlockSpec(
        (CHUNK, 256), lambda i, o, c, w: (jnp.maximum(i - request_steps, 0), 0)
    )
    return pl.pallas_call(
        own_kernel,
        grid_spec=pltpu.PrefetchScalarGridSpec(
            num_scalar_prefetch=3,
            grid=(request_steps + rows // CHUNK,),
            in_specs=[
                pl.BlockSpec(
                    (GATHERED, BLOCK, 256),
                    lambda i, o, c, w: (jnp.minimum(i, last_step(c[1], GATHERED)), 0, 0),
                ),
                pl.BlockSpec(
                    (GATHERED, BLOCK, 256),
                    lambda i, o, c, w: (
                        jnp.clip(i - first_help, 0, last_step(c[2] - slots // 2, GATHERED)), 0, 0
                    ),
                ),
                whole(slots, 2, 128),
                whole(rows, 256),
                chunk_of,
                chunk_of,
                whole(HALO, 256),
                whole(256, 256),
            ],
            out_specs=chunk_of,
            scratch_shapes=[pltpu.VMEM((rows, 256), F32)],
        ),
        out_shape=jax.ShapeDtypeStruct((rows, 256), F32),
        compiler_params=pltpu.CompilerParams(vmem_limit_bytes=VMEM),
        name="own",
    )(order, bounds, wanted, ctx, helped, stats, keyed, part, latents, borrowed, pred_weight)


def shifted(block, axis, distance):
    devices = range(lax.axis_size(axis))
    route = [(i - distance, i) for i in devices if i - distance in devices]
    return lax.ppermute(block, axis, route)


def swapped(block, axis):
    return lax.ppermute(block, axis, [(i, i ^ 1) for i in range(lax.axis_size(axis))])


def exchanged(slots):
    owners_count = slots.shape[0] // CAP
    sent = slots.reshape((owners_count, CAP) + slots.shape[1:])
    got = lax.all_to_all(sent, ("tm", "stream"), split_axis=0, concat_axis=0, tiled=True)
    return got.reshape(slots.shape)


def body(raw, starts, neg_owner, neg_block, enc_weight, tcn_weight, pred_weight):
    raw = raw[0]
    owners_count = lax.axis_size("tm") * lax.axis_size("stream")
    rim_starts = jnp.concatenate(
        [jnp.zeros((1, 128 - HALO), BF), starts[:, -HALO:].astype(BF)], axis=1
    )
    rim = shifted(jnp.concatenate([raw[:, -128:], rim_starts, rim_starts], axis=0), "tm", 1)
    half_weight = (tcn_weight * 0.5).astype(BF)
    tcn_back = jnp.swapaxes(tcn_weight, 2, 3)
    pred_back = pred_weight.T
    pack, push, slots, bd = prep(
        neg_owner[0].T, neg_block[0].T, raw, starts.reshape(-1, BLOCK), rim,
        enc_weight, owners_count,
    )
    pushed = exchanged(push)
    latents, ctx, slopes, levels, rim_slopes, rim_levels, keyed = forward(
        pack, bd, half_weight, pred_weight
    )
    pushed, ctx = lax.optimization_barrier((pushed, ctx))
    replies, order, bounds, wanted, extra = answer(pushed, pack)
    answers = exchanged(replies)
    half = order.shape[0] // TOGETHER * TOGETHER // 2
    shared = swapped(extra, "tm")
    request_ctx = recompute(order, bounds, pushed, bd, half_weight)
    shared, request_ctx = lax.optimization_barrier((shared, request_ctx))
    mate_count = shared[half, 0, 0].astype(jnp.int32)
    mate_bounds = jnp.stack([kept(mate_count, half) - half, mate_count - half])
    helped = swapped(
        recompute(
            lax.iota(jnp.int32, half), jnp.maximum(mate_bounds, 0), shared, bd, half_weight
        ),
        "tm",
    )
    answers, request_ctx = lax.optimization_barrier((answers, request_ctx))
    pred_grad, target_grad, stats = score(slots, answers, ctx, latents, levels, pred_weight, bd)
    got_stats = exchanged(stats)
    part, rim_grad = backward(
        pred_grad, slopes, levels, target_grad, rim_slopes, rim_levels, pred_back, tcn_back
    )
    borrowed = shifted(rim_grad, "tm", -1)
    return own(
        order, bounds, wanted, request_ctx, helped, got_stats, keyed, part, latents, borrowed, pred_weight
    )[None]


def solution(mesh):
    placed = (
        P("stream", None, "tm"),
        P("stream", "tm"),
        P("stream", "tm", None),
        P("stream", "tm", None),
        P(),
        P(),
        P(),
    )
    return jax.shard_map(
        body, mesh=mesh, in_specs=placed, out_specs=P("stream", "tm", None), check_vma=False
    )
```

```python
import jax
import jax.numpy as jnp
from jax import lax
from jax.experimental import pallas as pl
from jax.experimental.pallas import tpu as pltpu
from jax.sharding import PartitionSpec as P

BLOCK = 128
NEG = 4
HALO = 32
AHEAD = 4
CAP = 2
LAYERS = 4
PACK = 32
TOGETHER = 16
PAIRED = 1
PIECES = 4
SKEW = 1
GATHERED = 64
CHUNK = 1024
NOTE = 95
LEAD = 20
SEGMENT = 512
SCORED = 4
SCALE = 10.0
EPSILON = 1e-06
BF = jnp.bfloat16
F32 = jnp.float32
MIB = 1 << 20
VMEM = 60 * MIB


def dot(a, b):
    return jnp.dot(a, b, preferred_element_type=F32)


def dot_nt(a, b):
    return lax.dot_general(a, b, (((1,), (1,)), ((), ())), preferred_element_type=F32)


def row_sum(x):
    return jnp.sum(x, axis=-1, keepdims=True)


def silu_of_half(half):
    return half + half * jnp.tanh(half)


def wide(x):
    return jnp.concatenate([x, x], axis=1)


def prep_kernel(owner_ref, block_ref, raw_ref, starts_ref, rim_ref, enc_ref,
                pack_ref, push_ref, slot_ref, bd_ref, lines, packs, turned, seen):
    blocks = pack_ref.shape[0]
    lines[...] = jnp.zeros_like(lines)
    for b in range(blocks):
        lines[b, 0:6, :] = raw_ref[:, b * 512:(b + 1) * 512].astype(F32)
    row = lax.broadcasted_iota(jnp.int32, (512, 512), 0)
    col = lax.broadcasted_iota(jnp.int32, (512, 512), 1)
    perm = jnp.where(row == 4 * (col & 127) + (col >> 7), 1.0, 0.0).astype(BF)
    row = lax.broadcasted_iota(jnp.int32, (128, 128), 0)
    col = lax.broadcasted_iota(jnp.int32, (128, 128), 1)
    perm_halo = jnp.where(row == 4 * (col & 31) + (col >> 5), 1.0, 0.0).astype(BF)
    flat = lines[...].reshape(blocks * 8, 512).astype(BF)
    main = dot(flat, perm).reshape(blocks, 8, 512)
    halo = dot(flat[:, 384:512], perm_halo).reshape(blocks, 8, 128)
    rim = rim_ref[...]
    rim_halo = dot(rim, perm_halo)

    lane = lax.broadcasted_iota(jnp.int32, (blocks + 8, 128), 1)
    level_row = lax.broadcasted_iota(jnp.int32, (8, 128), 0)
    rim_f = rim.astype(F32)
    before = jnp.where(level_row == 7, pltpu.roll(rim_f, 1, 0), 0.0)
    started = jnp.concatenate([before, starts_ref[...].astype(F32)], axis=0)
    level = 1.0 - started
    for distance in (1, 2, 4):
        moved = pltpu.roll(started, distance, 1)
        started = jnp.maximum(
            started, jnp.where(lane < distance, pltpu.roll(moved, 1, 0), moved)
        )
        level = level + (1.0 - started)
    level_halo = jnp.where(lane < HALO, pltpu.roll(level, HALO, 1), 0.0)

    for k in range(4):
        packs[:, k * 6:(k + 1) * 6, :] = main[:, 0:6, k * 128:(k + 1) * 128]
    packs[0, 24:30, :] = rim_halo[0:6]
    packs[1:blocks, 24:30, :] = halo[0:blocks - 1, 0:6, :]
    for b in range(blocks):
        packs[b, 30:31, :] = level[8 + b:9 + b]
        packs[b, 31:32, :] = level_halo[7 + b:8 + b]
    quarter = lax.broadcasted_iota(jnp.int32, (PACK, 128), 1) >> 5
    for group in range(blocks // 4):
        four = [packs[group * 4 + q] for q in range(4)]
        parts = []
        for g in range(4):
            part = four[g]
            for q in range(4):
                if q != g:
                    part = jnp.where(quarter == q, pltpu.roll(four[q], (q - g) * 32 % 128, 1), part)
            parts.append(part)
        flipped = jnp.transpose(jnp.concatenate(parts, axis=0))
        for q in range(4):
            turned[group * 4 + q] = flipped[q * 32:(q + 1) * 32]
    pack_ref[...] = turned[...].astype(BF)

    lane = lax.broadcasted_iota(jnp.int32, (PACK, 128), 1)
    note = jnp.where(lane == NOTE, 1.0, 0.0)
    unused = (-note).astype(BF)

    def clear(i, carry):
        push_ref[i] = unused
        return carry

    lax.fori_loop(0, push_ref.shape[0], clear, 0, unroll=8)

    def forget(i, carry):
        seen[i] = 0
        return carry

    lax.fori_loop(0, seen.shape[0], forget, 0, unroll=8)

    def send(i, carry):
        owner = owner_ref[i % NEG, i // NEG]
        rank = seen[owner]
        seen[owner] = rank + 1
        slot = owner * CAP + rank
        slot_ref[i] = slot
        wanted = block_ref[i % NEG, i // NEG].astype(F32)
        push_ref[slot] = (turned[i // NEG] + note * wanted).astype(BF)
        return carry

    lax.fori_loop(0, blocks * NEG, send, 0, unroll=4)

    bd_ref[...] = jnp.zeros_like(bd_ref)
    half_enc = (enc_ref[...].astype(F32) * 0.5).astype(BF)
    for q in range(4):
        bd_ref[q * 32:q * 32 + 24, q * 256:(q + 1) * 256] = half_enc


def prep(owners, wanted, raw, starts, rim, enc_weight, owners_count):
    blocks = starts.shape[0]
    smem = pl.BlockSpec(memory_space=pltpu.SMEM)
    vmem = pl.BlockSpec(memory_space=pltpu.VMEM)
    return pl.pallas_call(
        prep_kernel,
        out_shape=(
            jax.ShapeDtypeStruct((blocks, PACK, 128), BF),
            jax.ShapeDtypeStruct((owners_count * CAP, PACK, 128), BF),
            jax.ShapeDtypeStruct((blocks * NEG,), jnp.int32),
            jax.ShapeDtypeStruct((128, 1024), BF),
        ),
        in_specs=[smem, smem, vmem, vmem, vmem, vmem],
        out_specs=(vmem, vmem, smem, vmem),
        scratch_shapes=[
            pltpu.VMEM((blocks, 8, 512), F32),
            pltpu.VMEM((blocks, PACK, 128), F32),
            pltpu.VMEM((blocks, PACK, 128), F32),
            pltpu.SMEM((owners_count,), jnp.int32),
        ],
        compiler_params=pltpu.CompilerParams(vmem_limit_bytes=VMEM),
        name="prep",
    )(owners, wanted, raw, starts, rim, enc_weight)


def halo_rows(pack):
    lane = lax.broadcasted_iota(jnp.int32, (HALO, 128), 1)
    halo = jnp.where(lane == 30, pltpu.roll(pack, 127, 1), 0.0)
    for g in range(4):
        moved = pltpu.roll(pack, (-26 * g - 24) % 128, 1)
        halo = jnp.where((lane >= 6 * g) & (lane < 6 * g + 6), moved, halo)
    return halo


def layer_half(h, level, layer, w_ref):
    moved = pltpu.roll(h, 2**layer, 0)
    gated = jnp.where(level > layer, moved, 0.0)
    return dot(h.astype(BF), w_ref[layer, 0]) + dot(gated.astype(BF), w_ref[layer, 1])


def forward_kernel(pack_ref, bd_ref, w_ref, pred_ref, lat_ref, ctx_ref, slope_ref, level_ref,
                   rim_slope_ref, rim_level_ref, keyed_ref):
    first = pl.program_id(0) == 0
    packs = pack_ref[...].reshape(4 * PACK, 128).astype(F32)
    halo = halo_rows(packs[0:PACK])
    rows = jnp.concatenate([packs, halo], axis=0)
    encoded = silu_of_half(dot(rows.astype(BF), bd_ref[...]))
    pieces, columns = [encoded[4 * PACK:, 0:256]], [halo[:, 30:31]]
    for q in range(4):
        for g in range(4):
            pieces.append(encoded[q * PACK:(q + 1) * PACK, g * 256:(g + 1) * 256])
            columns.append(packs[q * PACK:(q + 1) * PACK, g * 32 + 30:g * 32 + 31])
    latent = jnp.concatenate(pieces, axis=0).astype(BF)
    level = jnp.broadcast_to(jnp.concatenate(columns, axis=0), (HALO + SEGMENT, 256))
    level_ref[...] = level[HALO:, 0:128]
    lat_ref[...] = latent[HALO:]
    h = latent.astype(F32)
    own = h[HALO:]
    key_scale = lax.rsqrt(row_sum(own * own) + EPSILON)
    keyed_ref[...] = dot_nt((own * key_scale).astype(BF), pred_ref[...]).astype(BF)
    slopes = []
    for layer in range(LAYERS):
        half = layer_half(h, level, layer, w_ref)
        tanh = jnp.tanh(half)
        slope = (0.5 * (1.0 + tanh)) * (1.0 + half * (1.0 - tanh))
        slope_ref[layer] = slope[HALO:].astype(BF)
        slopes.append(slope[:HALO].astype(BF))
        h = h + half + half * tanh
    ctx_ref[...] = h[HALO - AHEAD:HALO - AHEAD + SEGMENT].astype(BF)

    @pl.when(first)
    def _():
        rim_level_ref[...] = level[:HALO, 0:128]
        for layer in range(LAYERS):
            rim_slope_ref[layer] = slopes[layer]


def forward(pack, bd, half_weight, pred_weight):
    rows = pack.shape[0] * BLOCK
    steps = rows // SEGMENT
    whole = lambda *shape: pl.BlockSpec(shape, lambda i: (0,) * len(shape))
    rows_of = lambda width: pl.BlockSpec((SEGMENT, width), lambda i: (i, 0))
    return pl.pallas_call(
        forward_kernel,
        grid=(steps,),
        out_shape=(
            jax.ShapeDtypeStruct((rows, 256), BF),
            jax.ShapeDtypeStruct((rows, 256), BF),
            jax.ShapeDtypeStruct((LAYERS, rows, 256), BF),
            jax.ShapeDtypeStruct((rows, 128), F32),
            jax.ShapeDtypeStruct((LAYERS, HALO, 256), BF),
            jax.ShapeDtypeStruct((HALO, 128), F32),
            jax.ShapeDtypeStruct((rows, 256), BF),
        ),
        in_specs=[
            pl.BlockSpec((4, PACK, 128), lambda i: (i, 0, 0)),
            whole(128, 1024),
            whole(LAYERS, 2, 256, 256),
            whole(256, 256),
        ],
        out_specs=(
            rows_of(256),
            rows_of(256),
            pl.BlockSpec((LAYERS, SEGMENT, 256), lambda i: (0, i, 0)),
            rows_of(128),
            whole(LAYERS, HALO, 256),
            whole(HALO, 128),
            rows_of(256),
        ),
        compiler_params=pltpu.CompilerParams(vmem_limit_bytes=VMEM),
        cost_estimate=pl.CostEstimate(
            flops=rows * 2 * 65536 * 10, bytes_accessed=18 * MIB, transcendentals=rows * 256 * 5
        ),
        name="forward",
    )(pack, bd, half_weight, pred_weight)


def kept(count, half):
    shared = ((count - half + 63) >> 6) << 5
    return jnp.where(count > half, jnp.minimum(count, half + shared), count)


def answer_kernel(push_ref, pack_ref, answer_ref, order_ref, bounds_ref, wanted_ref, extra_ref,
                  listed, arrived):
    slots = push_ref.shape[0]
    half = slots // 2
    notes = push_ref[:, 0:16, :].astype(F32)[:, 0, :]
    listed[...] = jnp.transpose(notes)[NOTE:NOTE + 1].astype(jnp.int32)
    pltpu.sync_copy(listed, arrived)

    def clear(i, carry):
        order_ref[i] = 0
        return carry

    lax.fori_loop(0, slots, clear, 0, unroll=8)

    def reply(i, count):
        wanted = arrived[0, i]
        wanted_ref[i] = jnp.maximum(wanted, 0)
        answer_ref[i] = pack_ref[jnp.maximum(wanted, 0)]
        order_ref[count] = i
        return count + jnp.where(wanted >= 0, 1, 0)

    count = lax.fori_loop(0, slots, reply, 0, unroll=8)
    bounds_ref[0] = 0
    bounds_ref[1] = kept(count, half)
    bounds_ref[2] = count
    extra_ref[...] = jnp.zeros_like(extra_ref)
    extra_ref[half] = jnp.full((PACK, 128), count.astype(F32)).astype(BF)

    def share(i, carry):
        extra_ref[i - half] = push_ref[order_ref[i]]
        return carry

    lax.fori_loop(half, jnp.maximum(count, half), share, 0)


def answer(pushed, pack):
    slots = pushed.shape[0]
    smem = pl.BlockSpec(memory_space=pltpu.SMEM)
    vmem = pl.BlockSpec(memory_space=pltpu.VMEM)
    return pl.pallas_call(
        answer_kernel,
        out_shape=(
            jax.ShapeDtypeStruct((slots, PACK, 128), BF),
            jax.ShapeDtypeStruct((slots + 8,), jnp.int32),
            jax.ShapeDtypeStruct((3,), jnp.int32),
            jax.ShapeDtypeStruct((slots,), jnp.int32),
            jax.ShapeDtypeStruct((slots // 2 + 1, PACK, 128), BF),
        ),
        in_specs=[vmem, vmem],
        out_specs=(vmem, smem, smem, smem, vmem),
        scratch_shapes=[pltpu.VMEM((1, slots), jnp.int32), pltpu.SMEM((1, slots), jnp.int32)],
        compiler_params=pltpu.CompilerParams(vmem_limit_bytes=VMEM),
        name="answer",
    )(pushed, pack)


def request_stages(base, order_ref, push_ref, bd_ref, w_ref, ctx_ref, first_out,
                   patches, level, here, there, left, right, gated, half_ref):
    times = LEAD + BLOCK - AHEAD

    def pieces(first, parts=PIECES):
        edges = [first + (times - first) * p // parts for p in range(parts + 1)]
        return [(a * TOGETHER, b * TOGETHER) for a, b in zip(edges[:-1], edges[1:])]

    def parts(a, b):
        return [slice(c, min(c + 32, b)) for c in range(a, b, 32)]

    for j in range(TOGETHER):
        pack = push_ref[order_ref[base + j]].astype(F32)
        patches[pl.ds(j, LEAD, stride=TOGETHER), :] = halo_rows(pack)[HALO - LEAD:]
        for g in range(4):
            count = min(32, BLOCK - AHEAD - g * 32)
            own = pltpu.roll(pack, -32 * g % 128, 1) if g else pack
            at = (LEAD + g * 32) * TOGETHER + j
            patches[pl.ds(at, count, stride=TOGETHER), :] = own[:count]
        if j % 4 == 3:
            yield
    enc = bd_ref[:, 0:256]
    for a, b in pieces(0):
        half_ref[a:b, :] = dot(patches[a:b, :].astype(BF), enc).astype(BF)
        yield
        level[a:b, :] = jnp.broadcast_to(patches[a:b, 30:31], (b - a, 128)).astype(BF)
        for at in parts(a, b):
            here[at, :] = silu_of_half(half_ref[at, :])
        yield
    source, target = here, there
    first = 0
    for layer in range(LAYERS):
        first += 2**layer if layer else 2
        back = 2**layer * TOGETHER
        both = w_ref[layer].reshape(512, 256)
        for a, b in pieces(first):
            for at in parts(a, b):
                gate = jnp.minimum(jnp.maximum(level[at, :] - float(layer), 0.0), 1.0)
                gated[at, :] = source[at.start - back:at.stop - back, :] * wide(gate)
            yield
            x = jnp.concatenate([source[a:b, :], gated[a:b, :]], axis=1)
            half_ref[a:b, :] = dot(x, both).astype(BF)
            yield
            for at in parts(a, b):
                result = source[at, :] + silu_of_half(half_ref[at, :])
                if layer < LAYERS - 1:
                    target[at, :] = result
                else:
                    result = result.astype(F32)
                    to = slice(at.start - first * TOGETHER, at.stop - first * TOGETHER)
                    left[to, :] = result[:, 0:128]
                    right[to, :] = result[:, 128:256]
            yield
        source, target = target, source
    for j in range(TOGETHER):
        rows = pl.ds(j, BLOCK, stride=TOGETHER)
        ctx_ref[first_out + j] = jnp.concatenate([left[rows, :], right[rows, :]], axis=1).astype(BF)
        if j % 4 == 3:
            yield


def recompute_kernel(order_ref, bounds_ref, push_ref, bd_ref, w_ref, ctx_ref, *scratch):
    base = bounds_ref[0] + pl.program_id(0) * PAIRED * TOGETHER

    @pl.when(base < bounds_ref[1])
    def _():
        each = len(scratch) // PAIRED
        waiting = [
            request_stages(
                base + p * TOGETHER, order_ref, push_ref, bd_ref, w_ref, ctx_ref, p * TOGETHER,
                *scratch[p * each:(p + 1) * each],
            )
            for p in range(PAIRED)
        ]
        for p, stages in enumerate(waiting):
            for _ in range(SKEW * (PAIRED - 1 - p)):
                next(stages)
        while waiting:
            waiting = [stages for stages in waiting if next(stages, True) is None]


def last_step(count, together):
    return jnp.maximum(count - 1, 0) // together


def recompute(order, bounds, pushed, bd, half_weight):
    slots = order.shape[0] // TOGETHER * TOGETHER
    together = PAIRED * TOGETHER
    times = LEAD + BLOCK - AHEAD
    whole = lambda *shape: pl.BlockSpec(shape, lambda i, o, c: (0,) * len(shape))
    return pl.pallas_call(
        recompute_kernel,
        grid_spec=pltpu.PrefetchScalarGridSpec(
            num_scalar_prefetch=2,
            grid=(slots // TOGETHER // PAIRED,),
            in_specs=[whole(*pushed.shape), whole(128, 1024), whole(LAYERS, 2, 256, 256)],
            out_specs=pl.BlockSpec(
                (together, BLOCK, 256),
                lambda i, o, c: (
                    jnp.minimum(c[0] // together + i, last_step(c[1], together)), 0, 0
                ),
            ),
            scratch_shapes=[
                pltpu.VMEM((times * TOGETHER, 128), F32),
                pltpu.VMEM((times * TOGETHER, 128), BF),
                pltpu.VMEM((times * TOGETHER, 256), BF),
                pltpu.VMEM((times * TOGETHER, 256), BF),
                pltpu.VMEM((BLOCK * TOGETHER, 128), F32),
                pltpu.VMEM((BLOCK * TOGETHER, 128), F32),
                pltpu.VMEM((times * TOGETHER, 256), BF),
                pltpu.VMEM((times * TOGETHER, 256), BF),
            ] * PAIRED,
        ),
        out_shape=jax.ShapeDtypeStruct((slots, BLOCK, 256), BF),
        compiler_params=pltpu.CompilerParams(vmem_limit_bytes=VMEM),
        cost_estimate=pl.CostEstimate(
            flops=slots * 160 * 2 * 65536 * 10, bytes_accessed=20 * MIB,
            transcendentals=slots * 160 * 256 * 5,
        ),
        name="recompute",
    )(order, bounds, pushed, bd, half_weight)


def score_kernel(slot_ref, answer_ref, ctx_ref, lat_ref, level_ref, pred_ref, bd_ref,
                 pred_grad_ref, target_grad_ref, stats_ref):
    step = pl.program_id(0)

    @pl.when(step == 0)
    def _():
        stats_ref[...] = jnp.zeros_like(stats_ref)

    blocks = range(SCORED)
    slots = [slot_ref[step * SCORED * NEG + i] for i in range(SCORED * NEG)]
    lane = lax.broadcasted_iota(jnp.int32, (BLOCK, 128), 1)
    ats = [slice(g * BLOCK, (g + 1) * BLOCK) for g in blocks]
    packs = [
        jnp.concatenate([answer_ref[slots[g * NEG + j]] for j in range(NEG)], axis=0) for g in blocks
    ]
    raw_pred = [dot(ctx_ref[at, :], pred_ref[...]) for at in ats]
    half = [dot(pack, bd_ref[...]) for pack in packs]
    pred_scale = [lax.rsqrt(row_sum(x * x) + EPSILON) for x in raw_pred]
    unit = [x * y for x, y in zip(raw_pred, pred_scale)]
    query = [x.astype(BF) for x in unit]
    keys = []
    for g in blocks:
        pieces = []
        for j in range(4):
            negative = silu_of_half(half[g][:, j * 256:(j + 1) * 256])
            key_scale = lax.rsqrt(row_sum(negative * negative) + EPSILON)
            pieces.append((negative * (key_scale)).astype(BF))
        keys.append(jnp.concatenate(pieces, axis=0))
    scores = [dot_nt(query[g], keys[g]) for g in blocks]
    exp_neg = [jnp.exp(SCALE * x) for x in scores]
    both = [dot(exp_neg[g].astype(BF), keys[g]) for g in blocks]
    sums = [row_sum(x) for x in exp_neg]
    columns = jnp.zeros((BLOCK, 128), F32)
    for g in blocks:
        at = ats[g]
        query_f = query[g].astype(F32)
        latent = lat_ref[at, :].astype(F32)
        usable = jnp.where(level_ref[at, 0:1] > 2.0, 1.0, 0.0)
        own_scale = lax.rsqrt(row_sum(latent * latent) + EPSILON)
        positive = SCALE * row_sum(query_f * latent) * own_scale
        exp_pos = jnp.exp(positive)
        share = usable / (exp_pos + sums[g])
        d_pos = share * exp_pos - usable
        pull = SCALE * d_pos * own_scale
        query_grad = (SCALE * share) * both[g] + (pull) * latent
        target_grad_ref[at, :] = (
            (pull) * query_f - (d_pos * positive * own_scale * own_scale) * latent
        )
        along = row_sum(unit[g] * query_grad)
        pred_grad_ref[at, :] = (
            (pred_scale[g]) * (query_grad - (along) * unit[g])
        ).astype(BF)
        columns = jnp.where(lane == 2 * g, pred_scale[g], columns)
        columns = jnp.where(lane == 2 * g + 1, share, columns)
    rows = jnp.transpose(columns)
    for i in range(SCORED * NEG):
        g = i // NEG
        stats_ref[slots[i]] = rows[2 * g:2 * g + 2]


def score(slots, answers, ctx, latents, levels, pred_weight, bd):
    rows = ctx.shape[0]
    count = answers.shape[0]
    whole = lambda *shape: pl.BlockSpec(shape, lambda i, s: (0,) * len(shape))
    rows_of = lambda width: pl.BlockSpec((SCORED * BLOCK, width), lambda i, s: (i, 0))
    return pl.pallas_call(
        score_kernel,
        grid_spec=pltpu.PrefetchScalarGridSpec(
            num_scalar_prefetch=1,
            grid=(rows // BLOCK // SCORED,),
            in_specs=[
                whole(count, PACK, 128), rows_of(256), rows_of(256), rows_of(128),
                whole(256, 256), whole(128, 1024),
            ],
            out_specs=(rows_of(256), rows_of(256), whole(count, 2, 128)),
        ),
        out_shape=(
            jax.ShapeDtypeStruct((rows, 256), BF),
            jax.ShapeDtypeStruct((rows, 256), F32),
            jax.ShapeDtypeStruct((count, 2, 128), F32),
        ),
        compiler_params=pltpu.CompilerParams(vmem_limit_bytes=VMEM),
        cost_estimate=pl.CostEstimate(
            flops=rows * 2 * 65536 * 10, bytes_accessed=16 * MIB, transcendentals=rows * 256 * 6
        ),
        name="score",
    )(slots, answers, ctx, latents, levels, pred_weight, bd)


def backward_kernel(pred_grad_ref, slope_ref, level_ref, target_grad_ref, rim_slope_ref,
                    rim_level_ref, pred_ref, w_ref, out_ref, rim_ref, carry):
    @pl.when(pl.program_id(0) == 0)
    def _():
        carry[...] = jnp.zeros_like(carry)

    def earlier(values, distance, place):
        longer = jnp.concatenate([values, carry[place]], axis=0)
        carry[place] = values[0:8]
        return longer[distance:distance + values.shape[0]]

    def through_layers(cotangent, slopes, level):
        for layer in reversed(range(LAYERS)):
            back = cotangent * slopes[layer].astype(F32)
            gated = jnp.where(level > layer, back, 0.0)
            cotangent = (
                cotangent
                + dot(
                    jnp.concatenate([back, earlier(gated, 2**layer, layer)], axis=1).astype(BF),
                    w_ref[layer].reshape(512, 256),
                )
            )
        return cotangent

    context_rows = dot(pred_grad_ref[...], pred_ref[...])
    cotangent = earlier(context_rows, AHEAD, LAYERS)
    level = wide(level_ref[...])
    out_ref[...] = through_layers(cotangent, slope_ref, level) + target_grad_ref[...]

    @pl.when(pl.program_id(0) == pl.num_programs(0) - 1)
    def _():
        cotangent = earlier(jnp.zeros((HALO, 256), F32), AHEAD, LAYERS)
        level = wide(rim_level_ref[...])
        rim_ref[...] = through_layers(cotangent, rim_slope_ref, level)


def backward(pred_grad, slopes, levels, target_grad, rim_slopes, rim_levels, pred_weight, weight):
    rows = pred_grad.shape[0]
    steps = rows // SEGMENT
    whole = lambda *shape: pl.BlockSpec(shape, lambda i: (0,) * len(shape))
    rows_of = lambda width: pl.BlockSpec((SEGMENT, width), lambda i: (steps - 1 - i, 0))
    return pl.pallas_call(
        backward_kernel,
        grid=(steps,),
        out_shape=(
            jax.ShapeDtypeStruct((rows, 256), F32),
            jax.ShapeDtypeStruct((HALO, 256), F32),
        ),
        in_specs=[
            rows_of(256),
            pl.BlockSpec((LAYERS, SEGMENT, 256), lambda i: (0, steps - 1 - i, 0)),
            rows_of(128),
            rows_of(256),
            whole(LAYERS, HALO, 256),
            whole(HALO, 128),
            whole(256, 256),
            whole(LAYERS, 2, 256, 256),
        ],
        out_specs=(rows_of(256), whole(HALO, 256)),
        scratch_shapes=[pltpu.VMEM((LAYERS + 1, 8, 256), F32)],
        compiler_params=pltpu.CompilerParams(vmem_limit_bytes=VMEM),
        cost_estimate=pl.CostEstimate(
            flops=rows * 2 * 65536 * 9, bytes_accessed=22 * MIB, transcendentals=0
        ),
        name="backward",
    )(pred_grad, slopes, levels, target_grad, rim_slopes, rim_levels, pred_weight, weight)


def own_kernel(order_ref, bounds_ref, wanted_ref, ctx_ref, help_ref, stats_ref, keyed_ref, part_ref, lat_ref,
               borrowed_ref, pred_ref, out_ref, total):
    step = pl.program_id(0)
    request_steps = pl.num_programs(0) - total.shape[0] // CHUNK

    @pl.when(step == 0)
    def _():
        total[...] = jnp.zeros_like(total)

    @pl.when((step < request_steps) & (step * GATHERED < bounds_ref[2]))
    def _():
        for part in range(0, GATHERED, 4):
            found = []
            for j in range(part, part + 4):
                at = step * GATHERED + j
                slot = order_ref[at]
                block = wanted_ref[slot]
                rows = pl.ds(pl.multiple_of(block * BLOCK, BLOCK), BLOCK)
                stats = stats_ref[slot]
                helped = jnp.where(at < bounds_ref[2], help_ref[j], jnp.zeros((BLOCK, 256), BF))
                ctx = jnp.where(at < bounds_ref[1], ctx_ref[j], helped)
                pred_scale, share = stats[0:1], stats[1:2]
                scores = dot_nt(keyed_ref[rows, :], ctx) * (SCALE * pred_scale)
                weighted = jnp.exp(scores) * (share * pred_scale)
                weighted = jnp.where(at < bounds_ref[2], weighted, 0.0)
                found.append((rows, dot(weighted.astype(BF), ctx)))
            for rows, addend in found:
                total[rows, :] += addend

    @pl.when(step >= request_steps)
    def _():
        chunk = step - request_steps
        rows = pl.ds(pl.multiple_of(chunk * CHUNK, CHUNK), CHUNK)
        direct = SCALE * dot(total[rows, :].astype(BF), pred_ref[...])
        latent = lat_ref[...].astype(F32)
        key_scale = lax.rsqrt(row_sum(latent * latent) + EPSILON)
        key = latent * key_scale
        along = row_sum(key * direct)
        out_ref[...] = part_ref[...] + key_scale * (direct - along * key)

        @pl.when(step == pl.num_programs(0) - 1)
        def _():
            out_ref[CHUNK - HALO:, :] += borrowed_ref[...]


def own(order, bounds, wanted, ctx, helped, stats, keyed, part, latents, borrowed, pred_weight):
    rows = part.shape[0]
    slots = ctx.shape[0]
    request_steps = slots // GATHERED
    first_help = slots // 2 // GATHERED
    whole = lambda *shape: pl.BlockSpec(shape, lambda i, o, c, w: (0,) * len(shape))
    chunk_of = pl.BlockSpec(
        (CHUNK, 256), lambda i, o, c, w: (jnp.maximum(i - request_steps, 0), 0)
    )
    return pl.pallas_call(
        own_kernel,
        grid_spec=pltpu.PrefetchScalarGridSpec(
            num_scalar_prefetch=3,
            grid=(request_steps + rows // CHUNK,),
            in_specs=[
                pl.BlockSpec(
                    (GATHERED, BLOCK, 256),
                    lambda i, o, c, w: (jnp.minimum(i, last_step(c[1], GATHERED)), 0, 0),
                ),
                pl.BlockSpec(
                    (GATHERED, BLOCK, 256),
                    lambda i, o, c, w: (
                        jnp.clip(i - first_help, 0, last_step(c[2] - slots // 2, GATHERED)), 0, 0
                    ),
                ),
                whole(slots, 2, 128),
                whole(rows, 256),
                chunk_of,
                chunk_of,
                whole(HALO, 256),
                whole(256, 256),
            ],
            out_specs=chunk_of,
            scratch_shapes=[pltpu.VMEM((rows, 256), F32)],
        ),
        out_shape=jax.ShapeDtypeStruct((rows, 256), F32),
        compiler_params=pltpu.CompilerParams(vmem_limit_bytes=VMEM),
        name="own",
    )(order, bounds, wanted, ctx, helped, stats, keyed, part, latents, borrowed, pred_weight)


def shifted(block, axis, distance):
    devices = range(lax.axis_size(axis))
    route = [(i - distance, i) for i in devices if i - distance in devices]
    return lax.ppermute(block, axis, route)


def swapped(block, axis):
    return lax.ppermute(block, axis, [(i, i ^ 1) for i in range(lax.axis_size(axis))])


def exchanged(slots):
    owners_count = slots.shape[0] // CAP
    sent = slots.reshape((owners_count, CAP) + slots.shape[1:])
    got = lax.all_to_all(sent, ("tm", "stream"), split_axis=0, concat_axis=0, tiled=True)
    return got.reshape(slots.shape)


def body(raw, starts, neg_owner, neg_block, enc_weight, tcn_weight, pred_weight):
    raw = raw[0]
    owners_count = lax.axis_size("tm") * lax.axis_size("stream")
    rim_starts = jnp.concatenate(
        [jnp.zeros((1, 128 - HALO), BF), starts[:, -HALO:].astype(BF)], axis=1
    )
    rim = shifted(jnp.concatenate([raw[:, -128:], rim_starts, rim_starts], axis=0), "tm", 1)
    half_weight = (tcn_weight * 0.5).astype(BF)
    tcn_back = jnp.swapaxes(tcn_weight, 2, 3)
    pred_back = pred_weight.T
    pack, push, slots, bd = prep(
        neg_owner[0].T, neg_block[0].T, raw, starts.reshape(-1, BLOCK), rim,
        enc_weight, owners_count,
    )
    pushed = exchanged(push)
    latents, ctx, slopes, levels, rim_slopes, rim_levels, keyed = forward(
        pack, bd, half_weight, pred_weight
    )
    pushed, ctx = lax.optimization_barrier((pushed, ctx))
    replies, order, bounds, wanted, extra = answer(pushed, pack)
    half = order.shape[0] // TOGETHER * TOGETHER // 2
    shared, replies = lax.optimization_barrier((swapped(extra, "tm"), replies))
    answers = exchanged(replies)
    request_ctx = recompute(order, bounds, pushed, bd, half_weight)
    shared, request_ctx = lax.optimization_barrier((shared, request_ctx))
    mate_count = shared[half, 0, 0].astype(jnp.int32)
    mate_bounds = jnp.stack([kept(mate_count, half) - half, mate_count - half])
    helped = swapped(
        recompute(
            lax.iota(jnp.int32, half), jnp.maximum(mate_bounds, 0), shared, bd, half_weight
        ),
        "tm",
    )
    answers, request_ctx = lax.optimization_barrier((answers, request_ctx))
    pred_grad, target_grad, stats = score(slots, answers, ctx, latents, levels, pred_weight, bd)
    got_stats = exchanged(stats)
    part, rim_grad = backward(
        pred_grad, slopes, levels, target_grad, rim_slopes, rim_levels, pred_back, tcn_back
    )
    borrowed = shifted(rim_grad, "tm", -1)
    return own(
        order, bounds, wanted, request_ctx, helped, got_stats, keyed, part, latents, borrowed, pred_weight
    )[None]


def solution(mesh):
    placed = (
        P("stream", None, "tm"),
        P("stream", "tm"),
        P("stream", "tm", None),
        P("stream", "tm", None),
        P(),
        P(),
        P(),
    )
    return jax.shard_map(
        body, mesh=mesh, in_specs=placed, out_specs=P("stream", "tm", None), check_vma=False
    )
```

```python
import jax
import jax.numpy as jnp
from jax import lax
from jax.experimental import pallas as pl
from jax.experimental.pallas import tpu as pltpu
from jax.sharding import PartitionSpec as P

BLOCK = 128
NEG = 4
HALO = 32
AHEAD = 4
CAP = 2
LAYERS = 4
PACK = 32
TOGETHER = 16
PAIRED = 1
PIECES = 4
SKEW = 1
GATHERED = 64
CHUNK = 1024
NOTE = 95
LEAD = 20
SEGMENT = 512
SCORED = 4
SCALE = 10.0
EPSILON = 1e-06
BF = jnp.bfloat16
F32 = jnp.float32
MIB = 1 << 20
VMEM = 60 * MIB


def dot(a, b):
    return jnp.dot(a, b, preferred_element_type=F32)


def dot_nt(a, b):
    return lax.dot_general(a, b, (((1,), (1,)), ((), ())), preferred_element_type=F32)


def row_sum(x):
    return jnp.sum(x, axis=-1, keepdims=True)


def silu_of_half(half):
    return half + half * jnp.tanh(half)


def wide(x):
    return jnp.concatenate([x, x], axis=1)


def prep_kernel(owner_ref, block_ref, raw_ref, starts_ref, rim_ref, enc_ref,
                pack_ref, push_ref, slot_ref, bd_ref, lines, packs, turned, seen):
    blocks = pack_ref.shape[0]
    lines[...] = jnp.zeros_like(lines)
    for b in range(blocks):
        lines[b, 0:6, :] = raw_ref[:, b * 512:(b + 1) * 512].astype(F32)
    row = lax.broadcasted_iota(jnp.int32, (512, 512), 0)
    col = lax.broadcasted_iota(jnp.int32, (512, 512), 1)
    perm = jnp.where(row == 4 * (col & 127) + (col >> 7), 1.0, 0.0).astype(BF)
    row = lax.broadcasted_iota(jnp.int32, (128, 128), 0)
    col = lax.broadcasted_iota(jnp.int32, (128, 128), 1)
    perm_halo = jnp.where(row == 4 * (col & 31) + (col >> 5), 1.0, 0.0).astype(BF)
    flat = lines[...].reshape(blocks * 8, 512).astype(BF)
    main = dot(flat, perm).reshape(blocks, 8, 512)
    halo = dot(flat[:, 384:512], perm_halo).reshape(blocks, 8, 128)
    rim = rim_ref[...]
    rim_halo = dot(rim, perm_halo)

    lane = lax.broadcasted_iota(jnp.int32, (blocks + 8, 128), 1)
    level_row = lax.broadcasted_iota(jnp.int32, (8, 128), 0)
    rim_f = rim.astype(F32)
    before = jnp.where(level_row == 7, pltpu.roll(rim_f, 1, 0), 0.0)
    started = jnp.concatenate([before, starts_ref[...].astype(F32)], axis=0)
    level = 1.0 - started
    for distance in (1, 2, 4):
        moved = pltpu.roll(started, distance, 1)
        started = jnp.maximum(
            started, jnp.where(lane < distance, pltpu.roll(moved, 1, 0), moved)
        )
        level = level + (1.0 - started)
    level_halo = jnp.where(lane < HALO, pltpu.roll(level, HALO, 1), 0.0)

    for k in range(4):
        packs[:, k * 6:(k + 1) * 6, :] = main[:, 0:6, k * 128:(k + 1) * 128]
    packs[0, 24:30, :] = rim_halo[0:6]
    packs[1:blocks, 24:30, :] = halo[0:blocks - 1, 0:6, :]
    for b in range(blocks):
        packs[b, 30:31, :] = level[8 + b:9 + b]
        packs[b, 31:32, :] = level_halo[7 + b:8 + b]
    quarter = lax.broadcasted_iota(jnp.int32, (PACK, 128), 1) >> 5
    for group in range(blocks // 4):
        four = [packs[group * 4 + q] for q in range(4)]
        parts = []
        for g in range(4):
            part = four[g]
            for q in range(4):
                if q != g:
                    part = jnp.where(quarter == q, pltpu.roll(four[q], (q - g) * 32 % 128, 1), part)
            parts.append(part)
        flipped = jnp.transpose(jnp.concatenate(parts, axis=0))
        for q in range(4):
            turned[group * 4 + q] = flipped[q * 32:(q + 1) * 32]
    pack_ref[...] = turned[...].astype(BF)

    lane = lax.broadcasted_iota(jnp.int32, (PACK, 128), 1)
    note = jnp.where(lane == NOTE, 1.0, 0.0)
    unused = (-note).astype(BF)

    def clear(i, carry):
        push_ref[i] = unused
        return carry

    lax.fori_loop(0, push_ref.shape[0], clear, 0, unroll=8)

    def forget(i, carry):
        seen[i] = 0
        return carry

    lax.fori_loop(0, seen.shape[0], forget, 0, unroll=8)

    def send(i, carry):
        owner = owner_ref[i % NEG, i // NEG]
        rank = seen[owner]
        seen[owner] = rank + 1
        slot = owner * CAP + rank
        slot_ref[i] = slot
        wanted = block_ref[i % NEG, i // NEG].astype(F32)
        push_ref[slot] = (turned[i // NEG] + note * wanted).astype(BF)
        return carry

    lax.fori_loop(0, blocks * NEG, send, 0, unroll=4)

    bd_ref[...] = jnp.zeros_like(bd_ref)
    half_enc = (enc_ref[...].astype(F32) * 0.5).astype(BF)
    for q in range(4):
        bd_ref[q * 32:q * 32 + 24, q * 256:(q + 1) * 256] = half_enc


def prep(owners, wanted, raw, starts, rim, enc_weight, owners_count):
    blocks = starts.shape[0]
    smem = pl.BlockSpec(memory_space=pltpu.SMEM)
    vmem = pl.BlockSpec(memory_space=pltpu.VMEM)
    return pl.pallas_call(
        prep_kernel,
        out_shape=(
            jax.ShapeDtypeStruct((blocks, PACK, 128), BF),
            jax.ShapeDtypeStruct((owners_count * CAP, PACK, 128), BF),
            jax.ShapeDtypeStruct((blocks * NEG,), jnp.int32),
            jax.ShapeDtypeStruct((128, 1024), BF),
        ),
        in_specs=[smem, smem, vmem, vmem, vmem, vmem],
        out_specs=(vmem, vmem, smem, vmem),
        scratch_shapes=[
            pltpu.VMEM((blocks, 8, 512), F32),
            pltpu.VMEM((blocks, PACK, 128), F32),
            pltpu.VMEM((blocks, PACK, 128), F32),
            pltpu.SMEM((owners_count,), jnp.int32),
        ],
        compiler_params=pltpu.CompilerParams(vmem_limit_bytes=VMEM),
        name="prep",
    )(owners, wanted, raw, starts, rim, enc_weight)


def halo_rows(pack):
    lane = lax.broadcasted_iota(jnp.int32, (HALO, 128), 1)
    halo = jnp.where(lane == 30, pltpu.roll(pack, 127, 1), 0.0)
    for g in range(4):
        moved = pltpu.roll(pack, (-26 * g - 24) % 128, 1)
        halo = jnp.where((lane >= 6 * g) & (lane < 6 * g + 6), moved, halo)
    return halo


def layer_half(h, level, layer, w_ref):
    moved = pltpu.roll(h, 2**layer, 0)
    gated = jnp.where(level > layer, moved, 0.0)
    return dot(h.astype(BF), w_ref[layer, 0]) + dot(gated.astype(BF), w_ref[layer, 1])


def forward_kernel(pack_ref, bd_ref, w_ref, pred_ref, lat_ref, ctx_ref, slope_ref, level_ref,
                   rim_slope_ref, rim_level_ref, keyed_ref):
    first = pl.program_id(0) == 0
    packs = pack_ref[...].reshape(4 * PACK, 128).astype(F32)
    halo = halo_rows(packs[0:PACK])
    rows = jnp.concatenate([packs, halo], axis=0)
    encoded = silu_of_half(dot(rows.astype(BF), bd_ref[...]))
    pieces, columns = [encoded[4 * PACK:, 0:256]], [halo[:, 30:31]]
    for q in range(4):
        for g in range(4):
            pieces.append(encoded[q * PACK:(q + 1) * PACK, g * 256:(g + 1) * 256])
            columns.append(packs[q * PACK:(q + 1) * PACK, g * 32 + 30:g * 32 + 31])
    latent = jnp.concatenate(pieces, axis=0).astype(BF)
    level = jnp.broadcast_to(jnp.concatenate(columns, axis=0), (HALO + SEGMENT, 256))
    level_ref[...] = level[HALO:, 0:128]
    lat_ref[...] = latent[HALO:]
    h = latent.astype(F32)
    own = h[HALO:]
    key_scale = lax.rsqrt(row_sum(own * own) + EPSILON)
    keyed_ref[...] = dot_nt((own * key_scale).astype(BF), pred_ref[...]).astype(BF)
    slopes = []
    for layer in range(LAYERS):
        half = layer_half(h, level, layer, w_ref)
        tanh = jnp.tanh(half)
        slope = (0.5 * (1.0 + tanh)) * (1.0 + half * (1.0 - tanh))
        slope_ref[layer] = slope[HALO:].astype(BF)
        slopes.append(slope[:HALO].astype(BF))
        h = h + half + half * tanh
    ctx_ref[...] = h[HALO - AHEAD:HALO - AHEAD + SEGMENT].astype(BF)

    @pl.when(first)
    def _():
        rim_level_ref[...] = level[:HALO, 0:128]
        for layer in range(LAYERS):
            rim_slope_ref[layer] = slopes[layer]


def forward(pack, bd, half_weight, pred_weight):
    rows = pack.shape[0] * BLOCK
    steps = rows // SEGMENT
    whole = lambda *shape: pl.BlockSpec(shape, lambda i: (0,) * len(shape))
    rows_of = lambda width: pl.BlockSpec((SEGMENT, width), lambda i: (i, 0))
    return pl.pallas_call(
        forward_kernel,
        grid=(steps,),
        out_shape=(
            jax.ShapeDtypeStruct((rows, 256), BF),
            jax.ShapeDtypeStruct((rows, 256), BF),
            jax.ShapeDtypeStruct((LAYERS, rows, 256), BF),
            jax.ShapeDtypeStruct((rows, 128), F32),
            jax.ShapeDtypeStruct((LAYERS, HALO, 256), BF),
            jax.ShapeDtypeStruct((HALO, 128), F32),
            jax.ShapeDtypeStruct((rows, 256), BF),
        ),
        in_specs=[
            pl.BlockSpec((4, PACK, 128), lambda i: (i, 0, 0)),
            whole(128, 1024),
            whole(LAYERS, 2, 256, 256),
            whole(256, 256),
        ],
        out_specs=(
            rows_of(256),
            rows_of(256),
            pl.BlockSpec((LAYERS, SEGMENT, 256), lambda i: (0, i, 0)),
            rows_of(128),
            whole(LAYERS, HALO, 256),
            whole(HALO, 128),
            rows_of(256),
        ),
        compiler_params=pltpu.CompilerParams(vmem_limit_bytes=VMEM),
        cost_estimate=pl.CostEstimate(
            flops=rows * 2 * 65536 * 10, bytes_accessed=18 * MIB, transcendentals=rows * 256 * 5
        ),
        name="forward",
    )(pack, bd, half_weight, pred_weight)


def kept(count, half):
    shared = ((count - half + 63) >> 6) << 5
    return jnp.where(count > half, jnp.minimum(count, half + shared), count)


def answer_kernel(push_ref, pack_ref, answer_ref, order_ref, bounds_ref, wanted_ref, extra_ref,
                  listed, arrived):
    slots = push_ref.shape[0]
    half = slots // 2
    notes = push_ref[:, 0:16, :].astype(F32)[:, 0, :]
    listed[...] = jnp.transpose(notes)[NOTE:NOTE + 1].astype(jnp.int32)
    pltpu.sync_copy(listed, arrived)

    def clear(i, carry):
        order_ref[i] = 0
        return carry

    lax.fori_loop(0, slots, clear, 0, unroll=8)

    def reply(i, count):
        wanted = arrived[0, i]
        wanted_ref[i] = jnp.maximum(wanted, 0)
        answer_ref[i] = pack_ref[jnp.maximum(wanted, 0)]
        order_ref[count] = i
        return count + jnp.where(wanted >= 0, 1, 0)

    count = lax.fori_loop(0, slots, reply, 0, unroll=8)
    bounds_ref[0] = 0
    bounds_ref[1] = kept(count, half)
    bounds_ref[2] = count
    extra_ref[...] = jnp.zeros_like(extra_ref)
    extra_ref[half] = jnp.full((PACK, 128), count.astype(F32)).astype(BF)

    def share(i, carry):
        extra_ref[i - half] = push_ref[order_ref[i]]
        return carry

    lax.fori_loop(half, jnp.maximum(count, half), share, 0)


def answer(pushed, pack):
    slots = pushed.shape[0]
    smem = pl.BlockSpec(memory_space=pltpu.SMEM)
    vmem = pl.BlockSpec(memory_space=pltpu.VMEM)
    return pl.pallas_call(
        answer_kernel,
        out_shape=(
            jax.ShapeDtypeStruct((slots, PACK, 128), BF),
            jax.ShapeDtypeStruct((slots + 8,), jnp.int32),
            jax.ShapeDtypeStruct((3,), jnp.int32),
            jax.ShapeDtypeStruct((slots,), jnp.int32),
            jax.ShapeDtypeStruct((slots // 2 + 1, PACK, 128), BF),
        ),
        in_specs=[vmem, vmem],
        out_specs=(vmem, smem, smem, smem, vmem),
        scratch_shapes=[pltpu.VMEM((1, slots), jnp.int32), pltpu.SMEM((1, slots), jnp.int32)],
        compiler_params=pltpu.CompilerParams(vmem_limit_bytes=VMEM),
        name="answer",
    )(pushed, pack)


def request_stages(base, order_ref, push_ref, bd_ref, w_ref, ctx_ref, first_out,
                   patches, level, here, there, left, right, gated, half_ref):
    times = LEAD + BLOCK - AHEAD

    def pieces(first, parts=PIECES):
        edges = [first + (times - first) * p // parts for p in range(parts + 1)]
        return [(a * TOGETHER, b * TOGETHER) for a, b in zip(edges[:-1], edges[1:])]

    def parts(a, b):
        return [slice(c, min(c + 32, b)) for c in range(a, b, 32)]

    for j in range(TOGETHER):
        pack = push_ref[order_ref[base + j]].astype(F32)
        patches[pl.ds(j, LEAD, stride=TOGETHER), :] = halo_rows(pack)[HALO - LEAD:]
        for g in range(4):
            count = min(32, BLOCK - AHEAD - g * 32)
            own = pltpu.roll(pack, -32 * g % 128, 1) if g else pack
            at = (LEAD + g * 32) * TOGETHER + j
            patches[pl.ds(at, count, stride=TOGETHER), :] = own[:count]
        if j % 4 == 3:
            yield
    enc = bd_ref[:, 0:256]
    for a, b in pieces(0):
        half_ref[a:b, :] = dot(patches[a:b, :].astype(BF), enc).astype(BF)
        yield
        level[a:b, :] = jnp.broadcast_to(patches[a:b, 30:31], (b - a, 128)).astype(BF)
        for at in parts(a, b):
            here[at, :] = silu_of_half(half_ref[at, :])
        yield
    source, target = here, there
    first = 0
    for layer in range(LAYERS):
        first += 2**layer if layer else 2
        back = 2**layer * TOGETHER
        both = w_ref[layer].reshape(512, 256)
        for a, b in pieces(first):
            for at in parts(a, b):
                gate = jnp.minimum(jnp.maximum(level[at, :] - float(layer), 0.0), 1.0)
                gated[at, :] = source[at.start - back:at.stop - back, :] * wide(gate)
            yield
            x = jnp.concatenate([source[a:b, :], gated[a:b, :]], axis=1)
            half_ref[a:b, :] = dot(x, both).astype(BF)
            yield
            for at in parts(a, b):
                result = source[at, :] + silu_of_half(half_ref[at, :])
                if layer < LAYERS - 1:
                    target[at, :] = result
                else:
                    result = result.astype(F32)
                    to = slice(at.start - first * TOGETHER, at.stop - first * TOGETHER)
                    left[to, :] = result[:, 0:128]
                    right[to, :] = result[:, 128:256]
            yield
        source, target = target, source
    for j in range(TOGETHER):
        rows = pl.ds(j, BLOCK, stride=TOGETHER)
        ctx_ref[first_out + j] = jnp.concatenate([left[rows, :], right[rows, :]], axis=1).astype(BF)
        if j % 4 == 3:
            yield


def recompute_kernel(order_ref, bounds_ref, push_ref, bd_ref, w_ref, ctx_ref, *scratch):
    base = bounds_ref[0] + pl.program_id(0) * PAIRED * TOGETHER

    @pl.when(base < bounds_ref[1])
    def _():
        each = len(scratch) // PAIRED
        waiting = [
            request_stages(
                base + p * TOGETHER, order_ref, push_ref, bd_ref, w_ref, ctx_ref, p * TOGETHER,
                *scratch[p * each:(p + 1) * each],
            )
            for p in range(PAIRED)
        ]
        for p, stages in enumerate(waiting):
            for _ in range(SKEW * (PAIRED - 1 - p)):
                next(stages)
        while waiting:
            waiting = [stages for stages in waiting if next(stages, True) is None]


def last_step(count, together):
    return jnp.maximum(count - 1, 0) // together


def recompute(order, bounds, pushed, bd, half_weight):
    slots = order.shape[0] // TOGETHER * TOGETHER
    together = PAIRED * TOGETHER
    times = LEAD + BLOCK - AHEAD
    whole = lambda *shape: pl.BlockSpec(shape, lambda i, o, c: (0,) * len(shape))
    return pl.pallas_call(
        recompute_kernel,
        grid_spec=pltpu.PrefetchScalarGridSpec(
            num_scalar_prefetch=2,
            grid=(slots // TOGETHER // PAIRED,),
            in_specs=[whole(*pushed.shape), whole(128, 1024), whole(LAYERS, 2, 256, 256)],
            out_specs=pl.BlockSpec(
                (together, BLOCK, 256),
                lambda i, o, c: (
                    jnp.minimum(c[0] // together + i, last_step(c[1], together)), 0, 0
                ),
            ),
            scratch_shapes=[
                pltpu.VMEM((times * TOGETHER, 128), F32),
                pltpu.VMEM((times * TOGETHER, 128), BF),
                pltpu.VMEM((times * TOGETHER, 256), BF),
                pltpu.VMEM((times * TOGETHER, 256), BF),
                pltpu.VMEM((BLOCK * TOGETHER, 128), F32),
                pltpu.VMEM((BLOCK * TOGETHER, 128), F32),
                pltpu.VMEM((times * TOGETHER, 256), BF),
                pltpu.VMEM((times * TOGETHER, 256), BF),
            ] * PAIRED,
        ),
        out_shape=jax.ShapeDtypeStruct((slots, BLOCK, 256), BF),
        compiler_params=pltpu.CompilerParams(vmem_limit_bytes=VMEM),
        cost_estimate=pl.CostEstimate(
            flops=slots * 160 * 2 * 65536 * 10, bytes_accessed=20 * MIB,
            transcendentals=slots * 160 * 256 * 5,
        ),
        name="recompute",
    )(order, bounds, pushed, bd, half_weight)


def score_kernel(slot_ref, answer_ref, ctx_ref, lat_ref, level_ref, pred_ref, bd_ref,
                 pred_grad_ref, target_grad_ref, stats_ref):
    step = pl.program_id(0)

    @pl.when(step == 0)
    def _():
        stats_ref[...] = jnp.zeros_like(stats_ref)

    blocks = range(SCORED)
    slots = [slot_ref[step * SCORED * NEG + i] for i in range(SCORED * NEG)]
    lane = lax.broadcasted_iota(jnp.int32, (BLOCK, 128), 1)
    ats = [slice(g * BLOCK, (g + 1) * BLOCK) for g in blocks]
    packs = [
        jnp.concatenate([answer_ref[slots[g * NEG + j]] for j in range(NEG)], axis=0) for g in blocks
    ]
    raw_pred = [dot(ctx_ref[at, :], pred_ref[...]) for at in ats]
    half = [dot(pack, bd_ref[...]) for pack in packs]
    pred_scale = [lax.rsqrt(row_sum(x * x) + EPSILON) for x in raw_pred]
    unit = [x * y for x, y in zip(raw_pred, pred_scale)]
    query = [x.astype(BF) for x in unit]
    keys = []
    for g in blocks:
        pieces = []
        for j in range(4):
            negative = silu_of_half(half[g][:, j * 256:(j + 1) * 256])
            key_scale = lax.rsqrt(row_sum(negative * negative) + EPSILON)
            pieces.append((negative * (key_scale)).astype(BF))
        keys.append(jnp.concatenate(pieces, axis=0))
    scores = [dot_nt(query[g], keys[g]) for g in blocks]
    exp_neg = [jnp.exp(SCALE * x) for x in scores]
    both = [dot(exp_neg[g].astype(BF), keys[g]) for g in blocks]
    sums = [row_sum(x) for x in exp_neg]
    columns = jnp.zeros((BLOCK, 128), F32)
    for g in blocks:
        at = ats[g]
        query_f = query[g].astype(F32)
        latent = lat_ref[at, :].astype(F32)
        usable = jnp.where(level_ref[at, 0:1] > 2.0, 1.0, 0.0)
        own_scale = lax.rsqrt(row_sum(latent * latent) + EPSILON)
        positive = SCALE * row_sum(query_f * latent) * own_scale
        exp_pos = jnp.exp(positive)
        share = usable / (exp_pos + sums[g])
        d_pos = share * exp_pos - usable
        pull = SCALE * d_pos * own_scale
        query_grad = (SCALE * share) * both[g] + (pull) * latent
        target_grad_ref[at, :] = (
            (pull) * query_f - (d_pos * positive * own_scale * own_scale) * latent
        )
        along = row_sum(unit[g] * query_grad)
        pred_grad_ref[at, :] = (
            (pred_scale[g]) * (query_grad - (along) * unit[g])
        ).astype(BF)
        columns = jnp.where(lane == 2 * g, pred_scale[g], columns)
        columns = jnp.where(lane == 2 * g + 1, share, columns)
    rows = jnp.transpose(columns)
    for i in range(SCORED * NEG):
        g = i // NEG
        stats_ref[slots[i]] = rows[2 * g:2 * g + 2]


def score(slots, answers, ctx, latents, levels, pred_weight, bd):
    rows = ctx.shape[0]
    count = answers.shape[0]
    whole = lambda *shape: pl.BlockSpec(shape, lambda i, s: (0,) * len(shape))
    rows_of = lambda width: pl.BlockSpec((SCORED * BLOCK, width), lambda i, s: (i, 0))
    return pl.pallas_call(
        score_kernel,
        grid_spec=pltpu.PrefetchScalarGridSpec(
            num_scalar_prefetch=1,
            grid=(rows // BLOCK // SCORED,),
            in_specs=[
                whole(count, PACK, 128), rows_of(256), rows_of(256), rows_of(128),
                whole(256, 256), whole(128, 1024),
            ],
            out_specs=(rows_of(256), rows_of(256), whole(count, 2, 128)),
        ),
        out_shape=(
            jax.ShapeDtypeStruct((rows, 256), BF),
            jax.ShapeDtypeStruct((rows, 256), F32),
            jax.ShapeDtypeStruct((count, 2, 128), F32),
        ),
        compiler_params=pltpu.CompilerParams(vmem_limit_bytes=VMEM),
        cost_estimate=pl.CostEstimate(
            flops=rows * 2 * 65536 * 10, bytes_accessed=16 * MIB, transcendentals=rows * 256 * 6
        ),
        name="score",
    )(slots, answers, ctx, latents, levels, pred_weight, bd)


def backward_kernel(pred_grad_ref, slope_ref, level_ref, target_grad_ref, rim_slope_ref,
                    rim_level_ref, pred_ref, w_ref, out_ref, rim_ref, carry):
    @pl.when(pl.program_id(0) == 0)
    def _():
        carry[...] = jnp.zeros_like(carry)

    def earlier(values, distance, place):
        longer = jnp.concatenate([values, carry[place]], axis=0)
        carry[place] = values[0:8]
        return longer[distance:distance + values.shape[0]]

    def through_layers(cotangent, slopes, level):
        for layer in reversed(range(LAYERS)):
            back = cotangent * slopes[layer].astype(F32)
            gated = jnp.where(level > layer, back, 0.0)
            cotangent = (
                cotangent
                + dot(
                    jnp.concatenate([back, earlier(gated, 2**layer, layer)], axis=1).astype(BF),
                    w_ref[layer].reshape(512, 256),
                )
            )
        return cotangent

    context_rows = dot(pred_grad_ref[...], pred_ref[...])
    cotangent = earlier(context_rows, AHEAD, LAYERS)
    level = wide(level_ref[...])
    out_ref[...] = through_layers(cotangent, slope_ref, level) + target_grad_ref[...]

    @pl.when(pl.program_id(0) == pl.num_programs(0) - 1)
    def _():
        cotangent = earlier(jnp.zeros((HALO, 256), F32), AHEAD, LAYERS)
        level = wide(rim_level_ref[...])
        rim_ref[...] = through_layers(cotangent, rim_slope_ref, level)


def backward(pred_grad, slopes, levels, target_grad, rim_slopes, rim_levels, pred_weight, weight):
    rows = pred_grad.shape[0]
    steps = rows // SEGMENT
    whole = lambda *shape: pl.BlockSpec(shape, lambda i: (0,) * len(shape))
    rows_of = lambda width: pl.BlockSpec((SEGMENT, width), lambda i: (steps - 1 - i, 0))
    return pl.pallas_call(
        backward_kernel,
        grid=(steps,),
        out_shape=(
            jax.ShapeDtypeStruct((rows, 256), F32),
            jax.ShapeDtypeStruct((HALO, 256), F32),
        ),
        in_specs=[
            rows_of(256),
            pl.BlockSpec((LAYERS, SEGMENT, 256), lambda i: (0, steps - 1 - i, 0)),
            rows_of(128),
            rows_of(256),
            whole(LAYERS, HALO, 256),
            whole(HALO, 128),
            whole(256, 256),
            whole(LAYERS, 2, 256, 256),
        ],
        out_specs=(rows_of(256), whole(HALO, 256)),
        scratch_shapes=[pltpu.VMEM((LAYERS + 1, 8, 256), F32)],
        compiler_params=pltpu.CompilerParams(vmem_limit_bytes=VMEM),
        cost_estimate=pl.CostEstimate(
            flops=rows * 2 * 65536 * 9, bytes_accessed=22 * MIB, transcendentals=0
        ),
        name="backward",
    )(pred_grad, slopes, levels, target_grad, rim_slopes, rim_levels, pred_weight, weight)


def own_kernel(order_ref, bounds_ref, wanted_ref, ctx_ref, help_ref, stats_ref, keyed_ref, part_ref, lat_ref,
               borrowed_ref, pred_ref, out_ref, total):
    step = pl.program_id(0)
    request_steps = pl.num_programs(0) - total.shape[0] // CHUNK

    @pl.when(step == 0)
    def _():
        total[...] = jnp.zeros_like(total)

    @pl.when((step < request_steps) & (step * GATHERED < bounds_ref[2]))
    def _():
        for part in range(0, GATHERED, 4):
            found = []
            for j in range(part, part + 4):
                at = step * GATHERED + j
                slot = order_ref[at]
                block = wanted_ref[slot]
                rows = pl.ds(pl.multiple_of(block * BLOCK, BLOCK), BLOCK)
                stats = stats_ref[slot]
                helped = jnp.where(at < bounds_ref[2], help_ref[j], jnp.zeros((BLOCK, 256), BF))
                ctx = jnp.where(at < bounds_ref[1], ctx_ref[j], helped)
                pred_scale, share = stats[0:1], stats[1:2]
                scores = dot_nt(keyed_ref[rows, :], ctx) * (SCALE * pred_scale)
                weighted = jnp.exp(scores) * (share * pred_scale)
                weighted = jnp.where(at < bounds_ref[2], weighted, 0.0)
                found.append((rows, dot(weighted.astype(BF), ctx)))
            for rows, addend in found:
                total[rows, :] += addend

    @pl.when(step >= request_steps)
    def _():
        chunk = step - request_steps
        rows = pl.ds(pl.multiple_of(chunk * CHUNK, CHUNK), CHUNK)
        direct = SCALE * dot(total[rows, :].astype(BF), pred_ref[...])
        latent = lat_ref[...].astype(F32)
        key_scale = lax.rsqrt(row_sum(latent * latent) + EPSILON)
        key = latent * key_scale
        along = row_sum(key * direct)
        out_ref[...] = part_ref[...] + key_scale * (direct - along * key)

        @pl.when(step == pl.num_programs(0) - 1)
        def _():
            out_ref[CHUNK - HALO:, :] += borrowed_ref[...]


def own(order, bounds, wanted, ctx, helped, stats, keyed, part, latents, borrowed, pred_weight):
    rows = part.shape[0]
    slots = ctx.shape[0]
    request_steps = slots // GATHERED
    first_help = slots // 2 // GATHERED
    whole = lambda *shape: pl.BlockSpec(shape, lambda i, o, c, w: (0,) * len(shape))
    chunk_of = pl.BlockSpec(
        (CHUNK, 256), lambda i, o, c, w: (jnp.maximum(i - request_steps, 0), 0)
    )
    return pl.pallas_call(
        own_kernel,
        grid_spec=pltpu.PrefetchScalarGridSpec(
            num_scalar_prefetch=3,
            grid=(request_steps + rows // CHUNK,),
            in_specs=[
                pl.BlockSpec(
                    (GATHERED, BLOCK, 256),
                    lambda i, o, c, w: (jnp.minimum(i, last_step(c[1], GATHERED)), 0, 0),
                ),
                pl.BlockSpec(
                    (GATHERED, BLOCK, 256),
                    lambda i, o, c, w: (
                        jnp.clip(i - first_help, 0, last_step(c[2] - slots // 2, GATHERED)), 0, 0
                    ),
                ),
                whole(slots, 2, 128),
                whole(rows, 256),
                chunk_of,
                chunk_of,
                whole(HALO, 256),
                whole(256, 256),
            ],
            out_specs=chunk_of,
            scratch_shapes=[pltpu.VMEM((rows, 256), F32)],
        ),
        out_shape=jax.ShapeDtypeStruct((rows, 256), F32),
        compiler_params=pltpu.CompilerParams(vmem_limit_bytes=VMEM),
        name="own",
    )(order, bounds, wanted, ctx, helped, stats, keyed, part, latents, borrowed, pred_weight)


def shifted(block, axis, distance):
    devices = range(lax.axis_size(axis))
    route = [(i - distance, i) for i in devices if i - distance in devices]
    return lax.ppermute(block, axis, route)


def swapped(block, axis):
    return lax.ppermute(block, axis, [(i, i ^ 1) for i in range(lax.axis_size(axis))])


def exchanged(slots):
    owners_count = slots.shape[0] // CAP
    sent = slots.reshape((owners_count, CAP) + slots.shape[1:])
    got = lax.all_to_all(sent, ("tm", "stream"), split_axis=0, concat_axis=0, tiled=True)
    return got.reshape(slots.shape)


def body(raw, starts, neg_owner, neg_block, enc_weight, tcn_weight, pred_weight):
    raw = raw[0]
    owners_count = lax.axis_size("tm") * lax.axis_size("stream")
    rim_starts = jnp.concatenate(
        [jnp.zeros((1, 128 - HALO), BF), starts[:, -HALO:].astype(BF)], axis=1
    )
    rim = shifted(jnp.concatenate([raw[:, -128:], rim_starts, rim_starts], axis=0), "tm", 1)
    half_weight = (tcn_weight * 0.5).astype(BF)
    tcn_back = jnp.swapaxes(tcn_weight, 2, 3)
    pred_back = pred_weight.T
    pack, push, slots, bd = prep(
        neg_owner[0].T, neg_block[0].T, raw, starts.reshape(-1, BLOCK), rim,
        enc_weight, owners_count,
    )
    pushed = exchanged(push)
    latents, ctx, slopes, levels, rim_slopes, rim_levels, keyed = forward(
        pack, bd, half_weight, pred_weight
    )
    pushed, ctx, tcn_back, pred_back = lax.optimization_barrier(
        (pushed, ctx, tcn_back, pred_back)
    )
    replies, order, bounds, wanted, extra = answer(pushed, pack)
    half = order.shape[0] // TOGETHER * TOGETHER // 2
    shared, replies, order = lax.optimization_barrier((swapped(extra, "tm"), replies, order))
    answers = exchanged(replies)
    request_ctx = recompute(order, bounds, pushed, bd, half_weight)
    shared, request_ctx, answers = lax.optimization_barrier((shared, request_ctx, answers))
    mate_count = shared[half, 0, 0].astype(jnp.int32)
    mate_bounds = jnp.stack([kept(mate_count, half) - half, mate_count - half])
    helped = swapped(
        recompute(
            lax.iota(jnp.int32, half), jnp.maximum(mate_bounds, 0), shared, bd, half_weight
        ),
        "tm",
    )
    pred_grad, target_grad, stats = score(slots, answers, ctx, latents, levels, pred_weight, bd)
    got_stats = exchanged(stats)
    part, rim_grad = backward(
        pred_grad, slopes, levels, target_grad, rim_slopes, rim_levels, pred_back, tcn_back
    )
    borrowed = shifted(rim_grad, "tm", -1)
    return own(
        order, bounds, wanted, request_ctx, helped, got_stats, keyed, part, latents, borrowed, pred_weight
    )[None]


def solution(mesh):
    placed = (
        P("stream", None, "tm"),
        P("stream", "tm"),
        P("stream", "tm", None),
        P("stream", "tm", None),
        P(),
        P(),
        P(),
    )
    return jax.shard_map(
        body, mesh=mesh, in_specs=placed, out_specs=P("stream", "tm", None), check_vma=False
    )
```

```python
import jax
import jax.numpy as jnp
from jax import lax
from jax.experimental import pallas as pl
from jax.experimental.pallas import tpu as pltpu
from jax.sharding import PartitionSpec as P

BLOCK = 128
NEG = 4
HALO = 32
AHEAD = 4
CAP = 2
LAYERS = 4
PACK = 32
TOGETHER = 16
PAIRED = 2
PIECES = 4
SKEW = 1
GATHERED = 64
CHUNK = 1024
NOTE = 95
LEAD = 20
SEGMENT = 512
SCORED = 8
SPAN = 1024
SCALE = 10.0
EPSILON = 1e-06
BF = jnp.bfloat16
F32 = jnp.float32
MIB = 1 << 20
VMEM = 60 * MIB


def dot(a, b):
    return jnp.dot(a, b, preferred_element_type=F32)


def dot_nt(a, b):
    return lax.dot_general(a, b, (((1,), (1,)), ((), ())), preferred_element_type=F32)


def row_sum(x):
    return jnp.sum(x, axis=-1, keepdims=True)


def silu_of_half(half):
    return half + half * jnp.tanh(half)


def wide(x):
    return jnp.concatenate([x, x], axis=1)


def prep_kernel(owner_ref, block_ref, raw_ref, starts_ref, rim_ref, enc_ref,
                pack_ref, push_ref, slot_ref, bd_ref, lines, packs, turned, seen):
    blocks = pack_ref.shape[0]
    lines[...] = jnp.zeros_like(lines)
    for b in range(blocks):
        lines[b, 0:6, :] = raw_ref[:, b * 512:(b + 1) * 512].astype(F32)
    row = lax.broadcasted_iota(jnp.int32, (512, 512), 0)
    col = lax.broadcasted_iota(jnp.int32, (512, 512), 1)
    perm = jnp.where(row == 4 * (col & 127) + (col >> 7), 1.0, 0.0).astype(BF)
    row = lax.broadcasted_iota(jnp.int32, (128, 128), 0)
    col = lax.broadcasted_iota(jnp.int32, (128, 128), 1)
    perm_halo = jnp.where(row == 4 * (col & 31) + (col >> 5), 1.0, 0.0).astype(BF)
    flat = lines[...].reshape(blocks * 8, 512).astype(BF)
    main = dot(flat, perm).reshape(blocks, 8, 512)
    halo = dot(flat[:, 384:512], perm_halo).reshape(blocks, 8, 128)
    rim = rim_ref[...]
    rim_halo = dot(rim, perm_halo)

    lane = lax.broadcasted_iota(jnp.int32, (blocks + 8, 128), 1)
    level_row = lax.broadcasted_iota(jnp.int32, (8, 128), 0)
    rim_f = rim.astype(F32)
    before = jnp.where(level_row == 7, pltpu.roll(rim_f, 1, 0), 0.0)
    started = jnp.concatenate([before, starts_ref[...].astype(F32)], axis=0)
    level = 1.0 - started
    for distance in (1, 2, 4):
        moved = pltpu.roll(started, distance, 1)
        started = jnp.maximum(
            started, jnp.where(lane < distance, pltpu.roll(moved, 1, 0), moved)
        )
        level = level + (1.0 - started)
    level_halo = jnp.where(lane < HALO, pltpu.roll(level, HALO, 1), 0.0)

    for k in range(4):
        packs[:, k * 6:(k + 1) * 6, :] = main[:, 0:6, k * 128:(k + 1) * 128]
    packs[0, 24:30, :] = rim_halo[0:6]
    packs[1:blocks, 24:30, :] = halo[0:blocks - 1, 0:6, :]
    for b in range(blocks):
        packs[b, 30:31, :] = level[8 + b:9 + b]
        packs[b, 31:32, :] = level_halo[7 + b:8 + b]
    quarter = lax.broadcasted_iota(jnp.int32, (PACK, 128), 1) >> 5
    for group in range(blocks // 4):
        four = [packs[group * 4 + q] for q in range(4)]
        parts = []
        for g in range(4):
            part = four[g]
            for q in range(4):
                if q != g:
                    part = jnp.where(quarter == q, pltpu.roll(four[q], (q - g) * 32 % 128, 1), part)
            parts.append(part)
        flipped = jnp.transpose(jnp.concatenate(parts, axis=0))
        for q in range(4):
            turned[group * 4 + q] = flipped[q * 32:(q + 1) * 32]
    pack_ref[...] = turned[...].astype(BF)

    lane = lax.broadcasted_iota(jnp.int32, (PACK, 128), 1)
    note = jnp.where(lane == NOTE, 1.0, 0.0)
    unused = (-note).astype(BF)

    def clear(i, carry):
        push_ref[i] = unused
        return carry

    lax.fori_loop(0, push_ref.shape[0], clear, 0, unroll=8)

    def forget(i, carry):
        seen[i] = 0
        return carry

    lax.fori_loop(0, seen.shape[0], forget, 0, unroll=8)

    def send(i, carry):
        owner = owner_ref[i % NEG, i // NEG]
        rank = seen[owner]
        seen[owner] = rank + 1
        slot = owner * CAP + rank
        slot_ref[i] = slot
        wanted = block_ref[i % NEG, i // NEG].astype(F32)
        push_ref[slot] = (turned[i // NEG] + note * wanted).astype(BF)
        return carry

    lax.fori_loop(0, blocks * NEG, send, 0, unroll=4)

    bd_ref[...] = jnp.zeros_like(bd_ref)
    half_enc = (enc_ref[...].astype(F32) * 0.5).astype(BF)
    for q in range(4):
        bd_ref[q * 32:q * 32 + 24, q * 256:(q + 1) * 256] = half_enc


def prep(owners, wanted, raw, starts, rim, enc_weight, owners_count):
    blocks = starts.shape[0]
    smem = pl.BlockSpec(memory_space=pltpu.SMEM)
    vmem = pl.BlockSpec(memory_space=pltpu.VMEM)
    return pl.pallas_call(
        prep_kernel,
        out_shape=(
            jax.ShapeDtypeStruct((blocks, PACK, 128), BF),
            jax.ShapeDtypeStruct((owners_count * CAP, PACK, 128), BF),
            jax.ShapeDtypeStruct((blocks * NEG,), jnp.int32),
            jax.ShapeDtypeStruct((128, 1024), BF),
        ),
        in_specs=[smem, smem, vmem, vmem, vmem, vmem],
        out_specs=(vmem, vmem, smem, vmem),
        scratch_shapes=[
            pltpu.VMEM((blocks, 8, 512), F32),
            pltpu.VMEM((blocks, PACK, 128), F32),
            pltpu.VMEM((blocks, PACK, 128), F32),
            pltpu.SMEM((owners_count,), jnp.int32),
        ],
        compiler_params=pltpu.CompilerParams(vmem_limit_bytes=VMEM),
        name="prep",
    )(owners, wanted, raw, starts, rim, enc_weight)


def halo_rows(pack):
    lane = lax.broadcasted_iota(jnp.int32, (HALO, 128), 1)
    halo = jnp.where(lane == 30, pltpu.roll(pack, 127, 1), 0.0)
    for g in range(4):
        moved = pltpu.roll(pack, (-26 * g - 24) % 128, 1)
        halo = jnp.where((lane >= 6 * g) & (lane < 6 * g + 6), moved, halo)
    return halo


def layer_half(h, level, layer, w_ref):
    moved = pltpu.roll(h, 2**layer, 0)
    gated = jnp.where(level > layer, moved, 0.0)
    return dot(h.astype(BF), w_ref[layer, 0]) + dot(gated.astype(BF), w_ref[layer, 1])


def forward_kernel(pack_ref, bd_ref, w_ref, pred_ref, lat_ref, ctx_ref, slope_ref, level_ref,
                   rim_slope_ref, rim_level_ref, keyed_ref):
    first = pl.program_id(0) == 0
    packs = pack_ref[...].reshape(4 * PACK, 128).astype(F32)
    halo = halo_rows(packs[0:PACK])
    rows = jnp.concatenate([packs, halo], axis=0)
    encoded = silu_of_half(dot(rows.astype(BF), bd_ref[...]))
    pieces, columns = [encoded[4 * PACK:, 0:256]], [halo[:, 30:31]]
    for q in range(4):
        for g in range(4):
            pieces.append(encoded[q * PACK:(q + 1) * PACK, g * 256:(g + 1) * 256])
            columns.append(packs[q * PACK:(q + 1) * PACK, g * 32 + 30:g * 32 + 31])
    latent = jnp.concatenate(pieces, axis=0).astype(BF)
    level = jnp.broadcast_to(jnp.concatenate(columns, axis=0), (HALO + SEGMENT, 256))
    level_ref[...] = level[HALO:, 0:128]
    lat_ref[...] = latent[HALO:]
    h = latent.astype(F32)
    own = h[HALO:]
    key_scale = lax.rsqrt(row_sum(own * own) + EPSILON)
    keyed_ref[...] = dot_nt((own * key_scale).astype(BF), pred_ref[...]).astype(BF)
    slopes = []
    for layer in range(LAYERS):
        half = layer_half(h, level, layer, w_ref)
        tanh = jnp.tanh(half)
        slope = (0.5 * (1.0 + tanh)) * (1.0 + half * (1.0 - tanh))
        slope_ref[layer] = slope[HALO:].astype(BF)
        slopes.append(slope[:HALO].astype(BF))
        h = h + half + half * tanh
    ctx_ref[...] = h[HALO - AHEAD:HALO - AHEAD + SEGMENT].astype(BF)

    @pl.when(first)
    def _():
        rim_level_ref[...] = level[:HALO, 0:128]
        for layer in range(LAYERS):
            rim_slope_ref[layer] = slopes[layer]


def forward(pack, bd, half_weight, pred_weight):
    rows = pack.shape[0] * BLOCK
    steps = rows // SEGMENT
    whole = lambda *shape: pl.BlockSpec(shape, lambda i: (0,) * len(shape))
    rows_of = lambda width: pl.BlockSpec((SEGMENT, width), lambda i: (i, 0))
    return pl.pallas_call(
        forward_kernel,
        grid=(steps,),
        out_shape=(
            jax.ShapeDtypeStruct((rows, 256), BF),
            jax.ShapeDtypeStruct((rows, 256), BF),
            jax.ShapeDtypeStruct((LAYERS, rows, 256), BF),
            jax.ShapeDtypeStruct((rows, 128), F32),
            jax.ShapeDtypeStruct((LAYERS, HALO, 256), BF),
            jax.ShapeDtypeStruct((HALO, 128), F32),
            jax.ShapeDtypeStruct((rows, 256), BF),
        ),
        in_specs=[
            pl.BlockSpec((4, PACK, 128), lambda i: (i, 0, 0)),
            whole(128, 1024),
            whole(LAYERS, 2, 256, 256),
            whole(256, 256),
        ],
        out_specs=(
            rows_of(256),
            rows_of(256),
            pl.BlockSpec((LAYERS, SEGMENT, 256), lambda i: (0, i, 0)),
            rows_of(128),
            whole(LAYERS, HALO, 256),
            whole(HALO, 128),
            rows_of(256),
        ),
        compiler_params=pltpu.CompilerParams(vmem_limit_bytes=VMEM),
        cost_estimate=pl.CostEstimate(
            flops=rows * 2 * 65536 * 10, bytes_accessed=18 * MIB, transcendentals=rows * 256 * 5
        ),
        name="forward",
    )(pack, bd, half_weight, pred_weight)


def kept(count, half):
    shared = ((count - half + 63) >> 6) << 5
    return jnp.where(count > half, jnp.minimum(count, half + shared), count)


def answer_kernel(push_ref, pack_ref, answer_ref, order_ref, bounds_ref, wanted_ref, extra_ref,
                  listed, arrived):
    slots = push_ref.shape[0]
    half = slots // 2
    notes = push_ref[:, 0:16, :].astype(F32)[:, 0, :]
    listed[...] = jnp.transpose(notes)[NOTE:NOTE + 1].astype(jnp.int32)
    pltpu.sync_copy(listed, arrived)

    def clear(i, carry):
        order_ref[i] = 0
        return carry

    lax.fori_loop(0, slots, clear, 0, unroll=8)

    def reply(i, count):
        wanted = arrived[0, i]
        wanted_ref[i] = jnp.maximum(wanted, 0)
        answer_ref[i] = pack_ref[jnp.maximum(wanted, 0)]
        order_ref[count] = i
        return count + jnp.where(wanted >= 0, 1, 0)

    count = lax.fori_loop(0, slots, reply, 0, unroll=8)
    bounds_ref[0] = 0
    bounds_ref[1] = kept(count, half)
    bounds_ref[2] = count
    extra_ref[...] = jnp.zeros_like(extra_ref)
    extra_ref[half] = jnp.full((PACK, 128), count.astype(F32)).astype(BF)

    def share(i, carry):
        extra_ref[i - half] = push_ref[order_ref[i]]
        return carry

    lax.fori_loop(half, jnp.maximum(count, half), share, 0)


def answer(pushed, pack):
    slots = pushed.shape[0]
    smem = pl.BlockSpec(memory_space=pltpu.SMEM)
    vmem = pl.BlockSpec(memory_space=pltpu.VMEM)
    return pl.pallas_call(
        answer_kernel,
        out_shape=(
            jax.ShapeDtypeStruct((slots, PACK, 128), BF),
            jax.ShapeDtypeStruct((slots + 8,), jnp.int32),
            jax.ShapeDtypeStruct((3,), jnp.int32),
            jax.ShapeDtypeStruct((slots,), jnp.int32),
            jax.ShapeDtypeStruct((slots // 2 + 1, PACK, 128), BF),
        ),
        in_specs=[vmem, vmem],
        out_specs=(vmem, smem, smem, smem, vmem),
        scratch_shapes=[pltpu.VMEM((1, slots), jnp.int32), pltpu.SMEM((1, slots), jnp.int32)],
        compiler_params=pltpu.CompilerParams(vmem_limit_bytes=VMEM),
        name="answer",
    )(pushed, pack)


def request_stages(base, order_ref, push_ref, bd_ref, w_ref, ctx_ref, first_out,
                   patches, level, here, there, left, right, gated, half_ref):
    times = LEAD + BLOCK - AHEAD

    def pieces(first, parts=PIECES):
        edges = [first + (times - first) * p // parts for p in range(parts + 1)]
        return [(a * TOGETHER, b * TOGETHER) for a, b in zip(edges[:-1], edges[1:])]

    def parts(a, b):
        return [slice(c, min(c + 32, b)) for c in range(a, b, 32)]

    for j in range(TOGETHER):
        pack = push_ref[order_ref[base + j]].astype(F32)
        patches[pl.ds(j, LEAD, stride=TOGETHER), :] = halo_rows(pack)[HALO - LEAD:]
        for g in range(4):
            count = min(32, BLOCK - AHEAD - g * 32)
            own = pltpu.roll(pack, -32 * g % 128, 1) if g else pack
            at = (LEAD + g * 32) * TOGETHER + j
            patches[pl.ds(at, count, stride=TOGETHER), :] = own[:count]
        if j % 4 == 3:
            yield
    enc = bd_ref[:, 0:256]
    for a, b in pieces(0):
        half_ref[a:b, :] = dot(patches[a:b, :].astype(BF), enc).astype(BF)
        yield
        level[a:b, :] = jnp.broadcast_to(patches[a:b, 30:31], (b - a, 128)).astype(BF)
        for at in parts(a, b):
            here[at, :] = silu_of_half(half_ref[at, :])
        yield
    source, target = here, there
    first = 0
    for layer in range(LAYERS):
        first += 2**layer if layer else 2
        back = 2**layer * TOGETHER
        both = w_ref[layer].reshape(512, 256)
        for a, b in pieces(first):
            for at in parts(a, b):
                gate = jnp.minimum(jnp.maximum(level[at, :] - float(layer), 0.0), 1.0)
                gated[at, :] = source[at.start - back:at.stop - back, :] * wide(gate)
            yield
            x = jnp.concatenate([source[a:b, :], gated[a:b, :]], axis=1)
            half_ref[a:b, :] = dot(x, both).astype(BF)
            yield
            for at in parts(a, b):
                result = source[at, :] + silu_of_half(half_ref[at, :])
                if layer < LAYERS - 1:
                    target[at, :] = result
                else:
                    result = result.astype(F32)
                    to = slice(at.start - first * TOGETHER, at.stop - first * TOGETHER)
                    left[to, :] = result[:, 0:128]
                    right[to, :] = result[:, 128:256]
            yield
        source, target = target, source
    for j in range(TOGETHER):
        rows = pl.ds(j, BLOCK, stride=TOGETHER)
        ctx_ref[first_out + j] = jnp.concatenate([left[rows, :], right[rows, :]], axis=1).astype(BF)
        if j % 4 == 3:
            yield


def recompute_kernel(order_ref, bounds_ref, push_ref, bd_ref, w_ref, ctx_ref, *scratch):
    base = bounds_ref[0] + pl.program_id(0) * PAIRED * TOGETHER

    @pl.when(base < bounds_ref[1])
    def _():
        each = len(scratch) // PAIRED
        waiting = [
            request_stages(
                base + p * TOGETHER, order_ref, push_ref, bd_ref, w_ref, ctx_ref, p * TOGETHER,
                *scratch[p * each:(p + 1) * each],
            )
            for p in range(PAIRED)
        ]
        for p, stages in enumerate(waiting):
            for _ in range(SKEW * (PAIRED - 1 - p)):
                next(stages)
        while waiting:
            waiting = [stages for stages in waiting if next(stages, True) is None]


def last_step(count, together):
    return jnp.maximum(count - 1, 0) // together


def recompute(order, bounds, pushed, bd, half_weight):
    slots = order.shape[0] // TOGETHER * TOGETHER
    together = PAIRED * TOGETHER
    times = LEAD + BLOCK - AHEAD
    whole = lambda *shape: pl.BlockSpec(shape, lambda i, o, c: (0,) * len(shape))
    return pl.pallas_call(
        recompute_kernel,
        grid_spec=pltpu.PrefetchScalarGridSpec(
            num_scalar_prefetch=2,
            grid=(slots // TOGETHER // PAIRED,),
            in_specs=[whole(*pushed.shape), whole(128, 1024), whole(LAYERS, 2, 256, 256)],
            out_specs=pl.BlockSpec(
                (together, BLOCK, 256),
                lambda i, o, c: (
                    jnp.minimum(c[0] // together + i, last_step(c[1], together)), 0, 0
                ),
            ),
            scratch_shapes=[
                pltpu.VMEM((times * TOGETHER, 128), F32),
                pltpu.VMEM((times * TOGETHER, 128), BF),
                pltpu.VMEM((times * TOGETHER, 256), BF),
                pltpu.VMEM((times * TOGETHER, 256), BF),
                pltpu.VMEM((BLOCK * TOGETHER, 128), F32),
                pltpu.VMEM((BLOCK * TOGETHER, 128), F32),
                pltpu.VMEM((times * TOGETHER, 256), BF),
                pltpu.VMEM((times * TOGETHER, 256), BF),
            ] * PAIRED,
        ),
        out_shape=jax.ShapeDtypeStruct((slots, BLOCK, 256), BF),
        compiler_params=pltpu.CompilerParams(vmem_limit_bytes=VMEM),
        cost_estimate=pl.CostEstimate(
            flops=slots * 160 * 2 * 65536 * 10, bytes_accessed=20 * MIB,
            transcendentals=slots * 160 * 256 * 5,
        ),
        name="recompute",
    )(order, bounds, pushed, bd, half_weight)


def score_kernel(slot_ref, answer_ref, ctx_ref, lat_ref, level_ref, pred_ref, bd_ref,
                 pred_grad_ref, target_grad_ref, stats_ref):
    step = pl.program_id(0)

    @pl.when(step == 0)
    def _():
        stats_ref[...] = jnp.zeros_like(stats_ref)

    blocks = range(SCORED)
    slots = [slot_ref[step * SCORED * NEG + i] for i in range(SCORED * NEG)]
    lane = lax.broadcasted_iota(jnp.int32, (BLOCK, 128), 1)
    ats = [slice(g * BLOCK, (g + 1) * BLOCK) for g in blocks]
    packs = [
        jnp.concatenate([answer_ref[slots[g * NEG + j]] for j in range(NEG)], axis=0) for g in blocks
    ]
    raw_pred = [dot(ctx_ref[at, :], pred_ref[...]) for at in ats]
    half = [dot(pack, bd_ref[...]) for pack in packs]
    pred_scale = [lax.rsqrt(row_sum(x * x) + EPSILON) for x in raw_pred]
    unit = [x * y for x, y in zip(raw_pred, pred_scale)]
    query = [x.astype(BF) for x in unit]
    keys = []
    for g in blocks:
        pieces = []
        for j in range(4):
            negative = silu_of_half(half[g][:, j * 256:(j + 1) * 256])
            key_scale = lax.rsqrt(row_sum(negative * negative) + EPSILON)
            pieces.append((negative * (key_scale)).astype(BF))
        keys.append(jnp.concatenate(pieces, axis=0))
    scores = [dot_nt(query[g], keys[g]) for g in blocks]
    exp_neg = [jnp.exp(SCALE * x) for x in scores]
    both = [dot(exp_neg[g].astype(BF), keys[g]) for g in blocks]
    sums = [row_sum(x) for x in exp_neg]
    columns = jnp.zeros((BLOCK, 128), F32)
    for g in blocks:
        at = ats[g]
        query_f = query[g].astype(F32)
        latent = lat_ref[at, :].astype(F32)
        usable = jnp.where(level_ref[at, 0:1] > 2.0, 1.0, 0.0)
        own_scale = lax.rsqrt(row_sum(latent * latent) + EPSILON)
        positive = SCALE * row_sum(query_f * latent) * own_scale
        exp_pos = jnp.exp(positive)
        share = usable / (exp_pos + sums[g])
        d_pos = share * exp_pos - usable
        pull = SCALE * d_pos * own_scale
        query_grad = (SCALE * share) * both[g] + (pull) * latent
        target_grad_ref[at, :] = (
            (pull) * query_f - (d_pos * positive * own_scale * own_scale) * latent
        )
        along = row_sum(unit[g] * query_grad)
        pred_grad_ref[at, :] = (
            (pred_scale[g]) * (query_grad - (along) * unit[g])
        ).astype(BF)
        columns = jnp.where(lane == 2 * g, pred_scale[g], columns)
        columns = jnp.where(lane == 2 * g + 1, share, columns)
    rows = jnp.transpose(columns)
    for i in range(SCORED * NEG):
        g = i // NEG
        stats_ref[slots[i]] = rows[2 * g:2 * g + 2]


def score(slots, answers, ctx, latents, levels, pred_weight, bd):
    rows = ctx.shape[0]
    count = answers.shape[0]
    whole = lambda *shape: pl.BlockSpec(shape, lambda i, s: (0,) * len(shape))
    rows_of = lambda width: pl.BlockSpec((SCORED * BLOCK, width), lambda i, s: (i, 0))
    return pl.pallas_call(
        score_kernel,
        grid_spec=pltpu.PrefetchScalarGridSpec(
            num_scalar_prefetch=1,
            grid=(rows // BLOCK // SCORED,),
            in_specs=[
                whole(count, PACK, 128), rows_of(256), rows_of(256), rows_of(128),
                whole(256, 256), whole(128, 1024),
            ],
            out_specs=(rows_of(256), rows_of(256), whole(count, 2, 128)),
        ),
        out_shape=(
            jax.ShapeDtypeStruct((rows, 256), BF),
            jax.ShapeDtypeStruct((rows, 256), F32),
            jax.ShapeDtypeStruct((count, 2, 128), F32),
        ),
        compiler_params=pltpu.CompilerParams(vmem_limit_bytes=VMEM),
        cost_estimate=pl.CostEstimate(
            flops=rows * 2 * 65536 * 10, bytes_accessed=16 * MIB, transcendentals=rows * 256 * 6
        ),
        name="score",
    )(slots, answers, ctx, latents, levels, pred_weight, bd)


def backward_kernel(pred_grad_ref, slope_ref, level_ref, target_grad_ref, rim_slope_ref,
                    rim_level_ref, pred_ref, w_ref, out_ref, rim_ref, carry):
    @pl.when(pl.program_id(0) == 0)
    def _():
        carry[...] = jnp.zeros_like(carry)

    def earlier(values, distance, place):
        longer = jnp.concatenate([values, carry[place]], axis=0)
        carry[place] = values[0:8]
        return longer[distance:distance + values.shape[0]]

    def through_layers(cotangent, slopes, level):
        for layer in reversed(range(LAYERS)):
            back = cotangent * slopes[layer].astype(F32)
            gated = jnp.where(level > layer, back, 0.0)
            cotangent = (
                cotangent
                + dot(
                    jnp.concatenate([back, earlier(gated, 2**layer, layer)], axis=1).astype(BF),
                    w_ref[layer].reshape(512, 256),
                )
            )
        return cotangent

    context_rows = dot(pred_grad_ref[...], pred_ref[...])
    cotangent = earlier(context_rows, AHEAD, LAYERS)
    level = wide(level_ref[...])
    out_ref[...] = through_layers(cotangent, slope_ref, level) + target_grad_ref[...]

    @pl.when(pl.program_id(0) == pl.num_programs(0) - 1)
    def _():
        cotangent = earlier(jnp.zeros((HALO, 256), F32), AHEAD, LAYERS)
        level = wide(rim_level_ref[...])
        rim_ref[...] = through_layers(cotangent, rim_slope_ref, level)


def backward(pred_grad, slopes, levels, target_grad, rim_slopes, rim_levels, pred_weight, weight):
    rows = pred_grad.shape[0]
    steps = rows // SPAN
    whole = lambda *shape: pl.BlockSpec(shape, lambda i: (0,) * len(shape))
    rows_of = lambda width: pl.BlockSpec((SPAN, width), lambda i: (steps - 1 - i, 0))
    return pl.pallas_call(
        backward_kernel,
        grid=(steps,),
        out_shape=(
            jax.ShapeDtypeStruct((rows, 256), F32),
            jax.ShapeDtypeStruct((HALO, 256), F32),
        ),
        in_specs=[
            rows_of(256),
            pl.BlockSpec((LAYERS, SPAN, 256), lambda i: (0, steps - 1 - i, 0)),
            rows_of(128),
            rows_of(256),
            whole(LAYERS, HALO, 256),
            whole(HALO, 128),
            whole(256, 256),
            whole(LAYERS, 2, 256, 256),
        ],
        out_specs=(rows_of(256), whole(HALO, 256)),
        scratch_shapes=[pltpu.VMEM((LAYERS + 1, 8, 256), F32)],
        compiler_params=pltpu.CompilerParams(vmem_limit_bytes=VMEM),
        cost_estimate=pl.CostEstimate(
            flops=rows * 2 * 65536 * 9, bytes_accessed=22 * MIB, transcendentals=0
        ),
        name="backward",
    )(pred_grad, slopes, levels, target_grad, rim_slopes, rim_levels, pred_weight, weight)


def own_kernel(order_ref, bounds_ref, wanted_ref, ctx_ref, help_ref, stats_ref, keyed_ref, part_ref, lat_ref,
               borrowed_ref, pred_ref, out_ref, total):
    step = pl.program_id(0)
    request_steps = pl.num_programs(0) - total.shape[0] // CHUNK

    @pl.when(step == 0)
    def _():
        total[...] = jnp.zeros_like(total)

    @pl.when((step < request_steps) & (step * GATHERED < bounds_ref[2]))
    def _():
        for part in range(0, GATHERED, 4):
            found = []
            for j in range(part, part + 4):
                at = step * GATHERED + j
                slot = order_ref[at]
                block = wanted_ref[slot]
                rows = pl.ds(pl.multiple_of(block * BLOCK, BLOCK), BLOCK)
                stats = stats_ref[slot]
                helped = jnp.where(at < bounds_ref[2], help_ref[j], jnp.zeros((BLOCK, 256), BF))
                ctx = jnp.where(at < bounds_ref[1], ctx_ref[j], helped)
                pred_scale, share = stats[0:1], stats[1:2]
                scores = dot_nt(keyed_ref[rows, :], ctx) * (SCALE * pred_scale)
                weighted = jnp.exp(scores) * (share * pred_scale)
                weighted = jnp.where(at < bounds_ref[2], weighted, 0.0)
                found.append((rows, dot(weighted.astype(BF), ctx)))
            for rows, addend in found:
                total[rows, :] += addend

    @pl.when(step >= request_steps)
    def _():
        chunk = step - request_steps
        rows = pl.ds(pl.multiple_of(chunk * CHUNK, CHUNK), CHUNK)
        direct = SCALE * dot(total[rows, :].astype(BF), pred_ref[...])
        latent = lat_ref[...].astype(F32)
        key_scale = lax.rsqrt(row_sum(latent * latent) + EPSILON)
        key = latent * key_scale
        along = row_sum(key * direct)
        out_ref[...] = part_ref[...] + key_scale * (direct - along * key)

        @pl.when(step == pl.num_programs(0) - 1)
        def _():
            out_ref[CHUNK - HALO:, :] += borrowed_ref[...]


def own(order, bounds, wanted, ctx, helped, stats, keyed, part, latents, borrowed, pred_weight):
    rows = part.shape[0]
    slots = ctx.shape[0]
    request_steps = slots // GATHERED
    first_help = slots // 2 // GATHERED
    whole = lambda *shape: pl.BlockSpec(shape, lambda i, o, c, w: (0,) * len(shape))
    chunk_of = pl.BlockSpec(
        (CHUNK, 256), lambda i, o, c, w: (jnp.maximum(i - request_steps, 0), 0)
    )
    return pl.pallas_call(
        own_kernel,
        grid_spec=pltpu.PrefetchScalarGridSpec(
            num_scalar_prefetch=3,
            grid=(request_steps + rows // CHUNK,),
            in_specs=[
                pl.BlockSpec(
                    (GATHERED, BLOCK, 256),
                    lambda i, o, c, w: (jnp.minimum(i, last_step(c[1], GATHERED)), 0, 0),
                ),
                pl.BlockSpec(
                    (GATHERED, BLOCK, 256),
                    lambda i, o, c, w: (
                        jnp.clip(i - first_help, 0, last_step(c[2] - slots // 2, GATHERED)), 0, 0
                    ),
                ),
                whole(slots, 2, 128),
                whole(rows, 256),
                chunk_of,
                chunk_of,
                whole(HALO, 256),
                whole(256, 256),
            ],
            out_specs=chunk_of,
            scratch_shapes=[pltpu.VMEM((rows, 256), F32)],
        ),
        out_shape=jax.ShapeDtypeStruct((rows, 256), F32),
        compiler_params=pltpu.CompilerParams(vmem_limit_bytes=VMEM),
        name="own",
    )(order, bounds, wanted, ctx, helped, stats, keyed, part, latents, borrowed, pred_weight)


def shifted(block, axis, distance):
    devices = range(lax.axis_size(axis))
    route = [(i - distance, i) for i in devices if i - distance in devices]
    return lax.ppermute(block, axis, route)


def swapped(block, axis):
    return lax.ppermute(block, axis, [(i, i ^ 1) for i in range(lax.axis_size(axis))])


def exchanged(slots):
    owners_count = slots.shape[0] // CAP
    sent = slots.reshape((owners_count, CAP) + slots.shape[1:])
    got = lax.all_to_all(sent, ("tm", "stream"), split_axis=0, concat_axis=0, tiled=True)
    return got.reshape(slots.shape)


def body(raw, starts, neg_owner, neg_block, enc_weight, tcn_weight, pred_weight):
    raw = raw[0]
    owners_count = lax.axis_size("tm") * lax.axis_size("stream")
    rim_starts = jnp.concatenate(
        [jnp.zeros((1, 128 - HALO), BF), starts[:, -HALO:].astype(BF)], axis=1
    )
    rim = shifted(jnp.concatenate([raw[:, -128:], rim_starts, rim_starts], axis=0), "tm", 1)
    half_weight = (tcn_weight * 0.5).astype(BF)
    tcn_back = jnp.swapaxes(tcn_weight, 2, 3)
    pred_back = pred_weight.T
    pack, push, slots, bd = prep(
        neg_owner[0].T, neg_block[0].T, raw, starts.reshape(-1, BLOCK), rim,
        enc_weight, owners_count,
    )
    pushed = exchanged(push)
    latents, ctx, slopes, levels, rim_slopes, rim_levels, keyed = forward(
        pack, bd, half_weight, pred_weight
    )
    pushed, ctx, tcn_back, pred_back = lax.optimization_barrier(
        (pushed, ctx, tcn_back, pred_back)
    )
    replies, order, bounds, wanted, extra = answer(pushed, pack)
    half = order.shape[0] // TOGETHER * TOGETHER // 2
    shared, replies, order = lax.optimization_barrier((swapped(extra, "tm"), replies, order))
    answers = exchanged(replies)
    request_ctx = recompute(order, bounds, pushed, bd, half_weight)
    shared, request_ctx, answers = lax.optimization_barrier((shared, request_ctx, answers))
    mate_count = shared[half, 0, 0].astype(jnp.int32)
    mate_bounds = jnp.stack([kept(mate_count, half) - half, mate_count - half])
    helped = swapped(
        recompute(
            lax.iota(jnp.int32, half), jnp.maximum(mate_bounds, 0), shared, bd, half_weight
        ),
        "tm",
    )
    pred_grad, target_grad, stats = score(slots, answers, ctx, latents, levels, pred_weight, bd)
    got_stats = exchanged(stats)
    part, rim_grad = backward(
        pred_grad, slopes, levels, target_grad, rim_slopes, rim_levels, pred_back, tcn_back
    )
    borrowed = shifted(rim_grad, "tm", -1)
    return own(
        order, bounds, wanted, request_ctx, helped, got_stats, keyed, part, latents, borrowed, pred_weight
    )[None]


def solution(mesh):
    placed = (
        P("stream", None, "tm"),
        P("stream", "tm"),
        P("stream", "tm", None),
        P("stream", "tm", None),
        P(),
        P(),
        P(),
    )
    return jax.shard_map(
        body, mesh=mesh, in_specs=placed, out_specs=P("stream", "tm", None), check_vma=False
    )
```

```python
import jax
import jax.numpy as jnp
from jax import lax
from jax.experimental import pallas as pl
from jax.experimental.pallas import tpu as pltpu
from jax.sharding import PartitionSpec as P

BLOCK = 128
NEG = 4
HALO = 32
AHEAD = 4
CAP = 2
LAYERS = 4
PACK = 32
TOGETHER = 16
PAIRED = 1
PIECES = 4
SKEW = 1
GATHERED = 64
CHUNK = 1024
NOTE = 95
LEAD = 20
SEGMENT = 512
SCORED = 4
SPAN = 1024
SCALE = 10.0
EPSILON = 1e-06
BF = jnp.bfloat16
F32 = jnp.float32
MIB = 1 << 20
VMEM = 60 * MIB


def dot(a, b):
    return jnp.dot(a, b, preferred_element_type=F32)


def dot_nt(a, b):
    return lax.dot_general(a, b, (((1,), (1,)), ((), ())), preferred_element_type=F32)


def row_sum(x):
    return jnp.sum(x, axis=-1, keepdims=True)


def silu_of_half(half):
    return half + half * jnp.tanh(half)


def wide(x):
    return jnp.concatenate([x, x], axis=1)


def prep_kernel(owner_ref, block_ref, raw_ref, starts_ref, rim_ref, enc_ref,
                pack_ref, push_ref, slot_ref, bd_ref, lines, packs, turned, seen):
    blocks = pack_ref.shape[0]
    lines[...] = jnp.zeros_like(lines)
    for b in range(blocks):
        lines[b, 0:6, :] = raw_ref[:, b * 512:(b + 1) * 512].astype(F32)
    row = lax.broadcasted_iota(jnp.int32, (512, 512), 0)
    col = lax.broadcasted_iota(jnp.int32, (512, 512), 1)
    perm = jnp.where(row == 4 * (col & 127) + (col >> 7), 1.0, 0.0).astype(BF)
    row = lax.broadcasted_iota(jnp.int32, (128, 128), 0)
    col = lax.broadcasted_iota(jnp.int32, (128, 128), 1)
    perm_halo = jnp.where(row == 4 * (col & 31) + (col >> 5), 1.0, 0.0).astype(BF)
    flat = lines[...].reshape(blocks * 8, 512).astype(BF)
    main = dot(flat, perm).reshape(blocks, 8, 512)
    halo = dot(flat[:, 384:512], perm_halo).reshape(blocks, 8, 128)
    rim = rim_ref[...]
    rim_halo = dot(rim, perm_halo)

    lane = lax.broadcasted_iota(jnp.int32, (blocks + 8, 128), 1)
    level_row = lax.broadcasted_iota(jnp.int32, (8, 128), 0)
    rim_f = rim.astype(F32)
    before = jnp.where(level_row == 7, pltpu.roll(rim_f, 1, 0), 0.0)
    started = jnp.concatenate([before, starts_ref[...].astype(F32)], axis=0)
    level = 1.0 - started
    for distance in (1, 2, 4):
        moved = pltpu.roll(started, distance, 1)
        started = jnp.maximum(
            started, jnp.where(lane < distance, pltpu.roll(moved, 1, 0), moved)
        )
        level = level + (1.0 - started)
    level_halo = jnp.where(lane < HALO, pltpu.roll(level, HALO, 1), 0.0)

    for k in range(4):
        packs[:, k * 6:(k + 1) * 6, :] = main[:, 0:6, k * 128:(k + 1) * 128]
    packs[0, 24:30, :] = rim_halo[0:6]
    packs[1:blocks, 24:30, :] = halo[0:blocks - 1, 0:6, :]
    for b in range(blocks):
        packs[b, 30:31, :] = level[8 + b:9 + b]
        packs[b, 31:32, :] = level_halo[7 + b:8 + b]
    quarter = lax.broadcasted_iota(jnp.int32, (PACK, 128), 1) >> 5
    for group in range(blocks // 4):
        four = [packs[group * 4 + q] for q in range(4)]
        parts = []
        for g in range(4):
            part = four[g]
            for q in range(4):
                if q != g:
                    part = jnp.where(quarter == q, pltpu.roll(four[q], (q - g) * 32 % 128, 1), part)
            parts.append(part)
        flipped = jnp.transpose(jnp.concatenate(parts, axis=0))
        for q in range(4):
            turned[group * 4 + q] = flipped[q * 32:(q + 1) * 32]
    pack_ref[...] = turned[...].astype(BF)

    lane = lax.broadcasted_iota(jnp.int32, (PACK, 128), 1)
    note = jnp.where(lane == NOTE, 1.0, 0.0)
    unused = (-note).astype(BF)

    def clear(i, carry):
        push_ref[i] = unused
        return carry

    lax.fori_loop(0, push_ref.shape[0], clear, 0, unroll=8)

    def forget(i, carry):
        seen[i] = 0
        return carry

    lax.fori_loop(0, seen.shape[0], forget, 0, unroll=8)

    def send(i, carry):
        owner = owner_ref[i % NEG, i // NEG]
        rank = seen[owner]
        seen[owner] = rank + 1
        slot = owner * CAP + rank
        slot_ref[i] = slot
        wanted = block_ref[i % NEG, i // NEG].astype(F32)
        push_ref[slot] = (turned[i // NEG] + note * wanted).astype(BF)
        return carry

    lax.fori_loop(0, blocks * NEG, send, 0, unroll=4)

    bd_ref[...] = jnp.zeros_like(bd_ref)
    half_enc = (enc_ref[...].astype(F32) * 0.5).astype(BF)
    for q in range(4):
        bd_ref[q * 32:q * 32 + 24, q * 256:(q + 1) * 256] = half_enc


def prep(owners, wanted, raw, starts, rim, enc_weight, owners_count):
    blocks = starts.shape[0]
    smem = pl.BlockSpec(memory_space=pltpu.SMEM)
    vmem = pl.BlockSpec(memory_space=pltpu.VMEM)
    return pl.pallas_call(
        prep_kernel,
        out_shape=(
            jax.ShapeDtypeStruct((blocks, PACK, 128), BF),
            jax.ShapeDtypeStruct((owners_count * CAP, PACK, 128), BF),
            jax.ShapeDtypeStruct((blocks * NEG,), jnp.int32),
            jax.ShapeDtypeStruct((128, 1024), BF),
        ),
        in_specs=[smem, smem, vmem, vmem, vmem, vmem],
        out_specs=(vmem, vmem, smem, vmem),
        scratch_shapes=[
            pltpu.VMEM((blocks, 8, 512), F32),
            pltpu.VMEM((blocks, PACK, 128), F32),
            pltpu.VMEM((blocks, PACK, 128), F32),
            pltpu.SMEM((owners_count,), jnp.int32),
        ],
        compiler_params=pltpu.CompilerParams(vmem_limit_bytes=VMEM),
        name="prep",
    )(owners, wanted, raw, starts, rim, enc_weight)


def halo_rows(pack):
    lane = lax.broadcasted_iota(jnp.int32, (HALO, 128), 1)
    halo = jnp.where(lane == 30, pltpu.roll(pack, 127, 1), 0.0)
    for g in range(4):
        moved = pltpu.roll(pack, (-26 * g - 24) % 128, 1)
        halo = jnp.where((lane >= 6 * g) & (lane < 6 * g + 6), moved, halo)
    return halo


def layer_half(h, level, layer, w_ref):
    moved = pltpu.roll(h, 2**layer, 0)
    gated = jnp.where(level > layer, moved, 0.0)
    return dot(h.astype(BF), w_ref[layer, 0]) + dot(gated.astype(BF), w_ref[layer, 1])


def forward_kernel(pack_ref, bd_ref, w_ref, pred_ref, lat_ref, query_ref, slope_ref, level_ref,
                   rim_slope_ref, rim_level_ref, keyed_ref, scale_ref):
    first = pl.program_id(0) == 0
    packs = pack_ref[...].reshape(4 * PACK, 128).astype(F32)
    halo = halo_rows(packs[0:PACK])
    rows = jnp.concatenate([packs, halo], axis=0)
    encoded = silu_of_half(dot(rows.astype(BF), bd_ref[...]))
    pieces, columns = [encoded[4 * PACK:, 0:256]], [halo[:, 30:31]]
    for q in range(4):
        for g in range(4):
            pieces.append(encoded[q * PACK:(q + 1) * PACK, g * 256:(g + 1) * 256])
            columns.append(packs[q * PACK:(q + 1) * PACK, g * 32 + 30:g * 32 + 31])
    latent = jnp.concatenate(pieces, axis=0).astype(BF)
    level = jnp.broadcast_to(jnp.concatenate(columns, axis=0), (HALO + SEGMENT, 256))
    level_ref[...] = level[HALO:, 0:128]
    lat_ref[...] = latent[HALO:]
    h = latent.astype(F32)
    own = h[HALO:]
    key_scale = lax.rsqrt(row_sum(own * own) + EPSILON)
    keyed_ref[...] = dot_nt((own * key_scale).astype(BF), pred_ref[...]).astype(BF)
    slopes = []
    for layer in range(LAYERS):
        half = layer_half(h, level, layer, w_ref)
        tanh = jnp.tanh(half)
        slope = (0.5 * (1.0 + tanh)) * (1.0 + half * (1.0 - tanh))
        slope_ref[layer] = slope[HALO:].astype(BF)
        slopes.append(slope[:HALO].astype(BF))
        h = h + half + half * tanh
    raw_pred = dot(h[HALO - AHEAD:HALO - AHEAD + SEGMENT].astype(BF), pred_ref[...])
    pred_scale = lax.rsqrt(row_sum(raw_pred * raw_pred) + EPSILON)
    query_ref[...] = (raw_pred * pred_scale).astype(BF)
    scale_ref[...] = jnp.broadcast_to(pred_scale, (SEGMENT, 128))

    @pl.when(first)
    def _():
        rim_level_ref[...] = level[:HALO, 0:128]
        for layer in range(LAYERS):
            rim_slope_ref[layer] = slopes[layer]


def forward(pack, bd, half_weight, pred_weight):
    rows = pack.shape[0] * BLOCK
    steps = rows // SEGMENT
    whole = lambda *shape: pl.BlockSpec(shape, lambda i: (0,) * len(shape))
    rows_of = lambda width: pl.BlockSpec((SEGMENT, width), lambda i: (i, 0))
    return pl.pallas_call(
        forward_kernel,
        grid=(steps,),
        out_shape=(
            jax.ShapeDtypeStruct((rows, 256), BF),
            jax.ShapeDtypeStruct((rows, 256), BF),
            jax.ShapeDtypeStruct((LAYERS, rows, 256), BF),
            jax.ShapeDtypeStruct((rows, 128), F32),
            jax.ShapeDtypeStruct((LAYERS, HALO, 256), BF),
            jax.ShapeDtypeStruct((HALO, 128), F32),
            jax.ShapeDtypeStruct((rows, 256), BF),
            jax.ShapeDtypeStruct((rows, 128), F32),
        ),
        in_specs=[
            pl.BlockSpec((4, PACK, 128), lambda i: (i, 0, 0)),
            whole(128, 1024),
            whole(LAYERS, 2, 256, 256),
            whole(256, 256),
        ],
        out_specs=(
            rows_of(256),
            rows_of(256),
            pl.BlockSpec((LAYERS, SEGMENT, 256), lambda i: (0, i, 0)),
            rows_of(128),
            whole(LAYERS, HALO, 256),
            whole(HALO, 128),
            rows_of(256),
            rows_of(128),
        ),
        compiler_params=pltpu.CompilerParams(vmem_limit_bytes=VMEM),
        cost_estimate=pl.CostEstimate(
            flops=rows * 2 * 65536 * 10, bytes_accessed=18 * MIB, transcendentals=rows * 256 * 5
        ),
        name="forward",
    )(pack, bd, half_weight, pred_weight)


def kept(count, half):
    shared = ((count - half + 63) >> 6) << 5
    return jnp.where(count > half, jnp.minimum(count, half + shared), count)


def answer_kernel(push_ref, pack_ref, answer_ref, order_ref, bounds_ref, wanted_ref, extra_ref,
                  listed, arrived):
    slots = push_ref.shape[0]
    half = slots // 2
    notes = push_ref[:, 0:16, :].astype(F32)[:, 0, :]
    listed[...] = jnp.transpose(notes)[NOTE:NOTE + 1].astype(jnp.int32)
    pltpu.sync_copy(listed, arrived)

    def clear(i, carry):
        order_ref[i] = 0
        return carry

    lax.fori_loop(0, slots, clear, 0, unroll=8)

    def reply(i, count):
        wanted = arrived[0, i]
        wanted_ref[i] = jnp.maximum(wanted, 0)
        answer_ref[i] = pack_ref[jnp.maximum(wanted, 0)]
        order_ref[count] = i
        return count + jnp.where(wanted >= 0, 1, 0)

    count = lax.fori_loop(0, slots, reply, 0, unroll=8)
    bounds_ref[0] = 0
    bounds_ref[1] = kept(count, half)
    bounds_ref[2] = count
    extra_ref[...] = jnp.zeros_like(extra_ref)
    extra_ref[half] = jnp.full((PACK, 128), count.astype(F32)).astype(BF)

    def share(i, carry):
        extra_ref[i - half] = push_ref[order_ref[i]]
        return carry

    lax.fori_loop(half, jnp.maximum(count, half), share, 0)


def answer(pushed, pack):
    slots = pushed.shape[0]
    smem = pl.BlockSpec(memory_space=pltpu.SMEM)
    vmem = pl.BlockSpec(memory_space=pltpu.VMEM)
    return pl.pallas_call(
        answer_kernel,
        out_shape=(
            jax.ShapeDtypeStruct((slots, PACK, 128), BF),
            jax.ShapeDtypeStruct((slots + 8,), jnp.int32),
            jax.ShapeDtypeStruct((3,), jnp.int32),
            jax.ShapeDtypeStruct((slots,), jnp.int32),
            jax.ShapeDtypeStruct((slots // 2 + 1, PACK, 128), BF),
        ),
        in_specs=[vmem, vmem],
        out_specs=(vmem, smem, smem, smem, vmem),
        scratch_shapes=[pltpu.VMEM((1, slots), jnp.int32), pltpu.SMEM((1, slots), jnp.int32)],
        compiler_params=pltpu.CompilerParams(vmem_limit_bytes=VMEM),
        name="answer",
    )(pushed, pack)


def request_stages(base, order_ref, push_ref, bd_ref, w_ref, ctx_ref, first_out,
                   patches, level, here, there, left, right, gated, half_ref):
    times = LEAD + BLOCK - AHEAD

    def pieces(first, parts=PIECES):
        edges = [first + (times - first) * p // parts for p in range(parts + 1)]
        return [(a * TOGETHER, b * TOGETHER) for a, b in zip(edges[:-1], edges[1:])]

    def parts(a, b):
        return [slice(c, min(c + 32, b)) for c in range(a, b, 32)]

    for j in range(TOGETHER):
        pack = push_ref[order_ref[base + j]].astype(F32)
        patches[pl.ds(j, LEAD, stride=TOGETHER), :] = halo_rows(pack)[HALO - LEAD:]
        for g in range(4):
            count = min(32, BLOCK - AHEAD - g * 32)
            own = pltpu.roll(pack, -32 * g % 128, 1) if g else pack
            at = (LEAD + g * 32) * TOGETHER + j
            patches[pl.ds(at, count, stride=TOGETHER), :] = own[:count]
        if j % 4 == 3:
            yield
    enc = bd_ref[:, 0:256]
    for a, b in pieces(0):
        half_ref[a:b, :] = dot(patches[a:b, :].astype(BF), enc).astype(BF)
        yield
        level[a:b, :] = jnp.broadcast_to(patches[a:b, 30:31], (b - a, 128)).astype(BF)
        for at in parts(a, b):
            here[at, :] = silu_of_half(half_ref[at, :])
        yield
    source, target = here, there
    first = 0
    for layer in range(LAYERS):
        first += 2**layer if layer else 2
        back = 2**layer * TOGETHER
        both = w_ref[layer].reshape(512, 256)
        for a, b in pieces(first):
            for at in parts(a, b):
                gate = jnp.minimum(jnp.maximum(level[at, :] - float(layer), 0.0), 1.0)
                gated[at, :] = source[at.start - back:at.stop - back, :] * wide(gate)
            yield
            x = jnp.concatenate([source[a:b, :], gated[a:b, :]], axis=1)
            half_ref[a:b, :] = dot(x, both).astype(BF)
            yield
            for at in parts(a, b):
                result = source[at, :] + silu_of_half(half_ref[at, :])
                if layer < LAYERS - 1:
                    target[at, :] = result
                else:
                    result = result.astype(F32)
                    to = slice(at.start - first * TOGETHER, at.stop - first * TOGETHER)
                    left[to, :] = result[:, 0:128]
                    right[to, :] = result[:, 128:256]
            yield
        source, target = target, source
    for j in range(TOGETHER):
        rows = pl.ds(j, BLOCK, stride=TOGETHER)
        ctx_ref[first_out + j] = jnp.concatenate([left[rows, :], right[rows, :]], axis=1).astype(BF)
        if j % 4 == 3:
            yield


def recompute_kernel(order_ref, bounds_ref, push_ref, bd_ref, w_ref, ctx_ref, *scratch):
    base = bounds_ref[0] + pl.program_id(0) * PAIRED * TOGETHER

    @pl.when(base < bounds_ref[1])
    def _():
        each = len(scratch) // PAIRED
        waiting = [
            request_stages(
                base + p * TOGETHER, order_ref, push_ref, bd_ref, w_ref, ctx_ref, p * TOGETHER,
                *scratch[p * each:(p + 1) * each],
            )
            for p in range(PAIRED)
        ]
        for p, stages in enumerate(waiting):
            for _ in range(SKEW * (PAIRED - 1 - p)):
                next(stages)
        while waiting:
            waiting = [stages for stages in waiting if next(stages, True) is None]


def last_step(count, together):
    return jnp.maximum(count - 1, 0) // together


def recompute(order, bounds, pushed, bd, half_weight):
    slots = order.shape[0] // TOGETHER * TOGETHER
    together = PAIRED * TOGETHER
    times = LEAD + BLOCK - AHEAD
    whole = lambda *shape: pl.BlockSpec(shape, lambda i, o, c: (0,) * len(shape))
    return pl.pallas_call(
        recompute_kernel,
        grid_spec=pltpu.PrefetchScalarGridSpec(
            num_scalar_prefetch=2,
            grid=(slots // TOGETHER // PAIRED,),
            in_specs=[whole(*pushed.shape), whole(128, 1024), whole(LAYERS, 2, 256, 256)],
            out_specs=pl.BlockSpec(
                (together, BLOCK, 256),
                lambda i, o, c: (
                    jnp.minimum(c[0] // together + i, last_step(c[1], together)), 0, 0
                ),
            ),
            scratch_shapes=[
                pltpu.VMEM((times * TOGETHER, 128), F32),
                pltpu.VMEM((times * TOGETHER, 128), BF),
                pltpu.VMEM((times * TOGETHER, 256), BF),
                pltpu.VMEM((times * TOGETHER, 256), BF),
                pltpu.VMEM((BLOCK * TOGETHER, 128), F32),
                pltpu.VMEM((BLOCK * TOGETHER, 128), F32),
                pltpu.VMEM((times * TOGETHER, 256), BF),
                pltpu.VMEM((times * TOGETHER, 256), BF),
            ] * PAIRED,
        ),
        out_shape=jax.ShapeDtypeStruct((slots, BLOCK, 256), BF),
        compiler_params=pltpu.CompilerParams(vmem_limit_bytes=VMEM),
        cost_estimate=pl.CostEstimate(
            flops=slots * 160 * 2 * 65536 * 10, bytes_accessed=20 * MIB,
            transcendentals=slots * 160 * 256 * 5,
        ),
        name="recompute",
    )(order, bounds, pushed, bd, half_weight)


def score_kernel(slot_ref, answer_ref, query_ref, lat_ref, level_ref, scale_ref, bd_ref,
                 pred_grad_ref, target_grad_ref, stats_ref):
    step = pl.program_id(0)

    @pl.when(step == 0)
    def _():
        stats_ref[...] = jnp.zeros_like(stats_ref)

    blocks = range(SCORED)
    slots = [slot_ref[step * SCORED * NEG + i] for i in range(SCORED * NEG)]
    lane = lax.broadcasted_iota(jnp.int32, (BLOCK, 128), 1)
    ats = [slice(g * BLOCK, (g + 1) * BLOCK) for g in blocks]
    packs = [
        jnp.concatenate([answer_ref[slots[g * NEG + j]] for j in range(NEG)], axis=0) for g in blocks
    ]
    half = [dot(pack, bd_ref[...]) for pack in packs]
    pred_scale = [scale_ref[at, 0:1] for at in ats]
    query = [query_ref[at, :] for at in ats]
    keys = []
    for g in blocks:
        pieces = []
        for j in range(4):
            negative = silu_of_half(half[g][:, j * 256:(j + 1) * 256])
            key_scale = lax.rsqrt(row_sum(negative * negative) + EPSILON)
            pieces.append((negative * (key_scale)).astype(BF))
        keys.append(jnp.concatenate(pieces, axis=0))
    scores = [dot_nt(query[g], keys[g]) for g in blocks]
    exp_neg = [jnp.exp(SCALE * x) for x in scores]
    both = [dot(exp_neg[g].astype(BF), keys[g]) for g in blocks]
    sums = [row_sum(x) for x in exp_neg]
    columns = jnp.zeros((BLOCK, 128), F32)
    for g in blocks:
        at = ats[g]
        query_f = query[g].astype(F32)
        latent = lat_ref[at, :].astype(F32)
        usable = jnp.where(level_ref[at, 0:1] > 2.0, 1.0, 0.0)
        own_scale = lax.rsqrt(row_sum(latent * latent) + EPSILON)
        positive = SCALE * row_sum(query_f * latent) * own_scale
        exp_pos = jnp.exp(positive)
        share = usable / (exp_pos + sums[g])
        d_pos = share * exp_pos - usable
        pull = SCALE * d_pos * own_scale
        query_grad = (SCALE * share) * both[g] + (pull) * latent
        target_grad_ref[at, :] = (
            (pull) * query_f - (d_pos * positive * own_scale * own_scale) * latent
        )
        along = row_sum(query_f * query_grad)
        pred_grad_ref[at, :] = (
            (pred_scale[g]) * (query_grad - (along) * query_f)
        ).astype(BF)
        columns = jnp.where(lane == 2 * g, pred_scale[g], columns)
        columns = jnp.where(lane == 2 * g + 1, share, columns)
    rows = jnp.transpose(columns)
    for i in range(SCORED * NEG):
        g = i // NEG
        stats_ref[slots[i]] = rows[2 * g:2 * g + 2]


def score(slots, answers, queries, latents, levels, scales, bd):
    rows = queries.shape[0]
    count = answers.shape[0]
    whole = lambda *shape: pl.BlockSpec(shape, lambda i, s: (0,) * len(shape))
    rows_of = lambda width: pl.BlockSpec((SCORED * BLOCK, width), lambda i, s: (i, 0))
    return pl.pallas_call(
        score_kernel,
        grid_spec=pltpu.PrefetchScalarGridSpec(
            num_scalar_prefetch=1,
            grid=(rows // BLOCK // SCORED,),
            in_specs=[
                whole(count, PACK, 128), rows_of(256), rows_of(256), rows_of(128),
                rows_of(128), whole(128, 1024),
            ],
            out_specs=(rows_of(256), rows_of(256), whole(count, 2, 128)),
        ),
        out_shape=(
            jax.ShapeDtypeStruct((rows, 256), BF),
            jax.ShapeDtypeStruct((rows, 256), F32),
            jax.ShapeDtypeStruct((count, 2, 128), F32),
        ),
        compiler_params=pltpu.CompilerParams(vmem_limit_bytes=VMEM),
        cost_estimate=pl.CostEstimate(
            flops=rows * 2 * 65536 * 10, bytes_accessed=16 * MIB, transcendentals=rows * 256 * 6
        ),
        name="score",
    )(slots, answers, queries, latents, levels, scales, bd)


def backward_kernel(pred_grad_ref, slope_ref, level_ref, target_grad_ref, rim_slope_ref,
                    rim_level_ref, pred_ref, w_ref, out_ref, rim_ref, carry):
    @pl.when(pl.program_id(0) == 0)
    def _():
        carry[...] = jnp.zeros_like(carry)

    def earlier(values, distance, place):
        longer = jnp.concatenate([values, carry[place]], axis=0)
        carry[place] = values[0:8]
        return longer[distance:distance + values.shape[0]]

    def through_layers(cotangent, slopes, level):
        for layer in reversed(range(LAYERS)):
            back = cotangent * slopes[layer].astype(F32)
            gated = jnp.where(level > layer, back, 0.0)
            cotangent = (
                cotangent
                + dot(
                    jnp.concatenate([back, earlier(gated, 2**layer, layer)], axis=1).astype(BF),
                    w_ref[layer].reshape(512, 256),
                )
            )
        return cotangent

    context_rows = dot(pred_grad_ref[...], pred_ref[...])
    cotangent = earlier(context_rows, AHEAD, LAYERS)
    level = wide(level_ref[...])
    out_ref[...] = through_layers(cotangent, slope_ref, level) + target_grad_ref[...]

    @pl.when(pl.program_id(0) == pl.num_programs(0) - 1)
    def _():
        cotangent = earlier(jnp.zeros((HALO, 256), F32), AHEAD, LAYERS)
        level = wide(rim_level_ref[...])
        rim_ref[...] = through_layers(cotangent, rim_slope_ref, level)


def backward(pred_grad, slopes, levels, target_grad, rim_slopes, rim_levels, pred_weight, weight):
    rows = pred_grad.shape[0]
    steps = rows // SPAN
    whole = lambda *shape: pl.BlockSpec(shape, lambda i: (0,) * len(shape))
    rows_of = lambda width: pl.BlockSpec((SPAN, width), lambda i: (steps - 1 - i, 0))
    return pl.pallas_call(
        backward_kernel,
        grid=(steps,),
        out_shape=(
            jax.ShapeDtypeStruct((rows, 256), F32),
            jax.ShapeDtypeStruct((HALO, 256), F32),
        ),
        in_specs=[
            rows_of(256),
            pl.BlockSpec((LAYERS, SPAN, 256), lambda i: (0, steps - 1 - i, 0)),
            rows_of(128),
            rows_of(256),
            whole(LAYERS, HALO, 256),
            whole(HALO, 128),
            whole(256, 256),
            whole(LAYERS, 2, 256, 256),
        ],
        out_specs=(rows_of(256), whole(HALO, 256)),
        scratch_shapes=[pltpu.VMEM((LAYERS + 1, 8, 256), F32)],
        compiler_params=pltpu.CompilerParams(vmem_limit_bytes=VMEM),
        cost_estimate=pl.CostEstimate(
            flops=rows * 2 * 65536 * 9, bytes_accessed=22 * MIB, transcendentals=0
        ),
        name="backward",
    )(pred_grad, slopes, levels, target_grad, rim_slopes, rim_levels, pred_weight, weight)


def own_kernel(order_ref, bounds_ref, wanted_ref, ctx_ref, help_ref, stats_ref, keyed_ref, part_ref, lat_ref,
               borrowed_ref, pred_ref, out_ref, total):
    step = pl.program_id(0)
    request_steps = pl.num_programs(0) - total.shape[0] // CHUNK

    @pl.when(step == 0)
    def _():
        total[...] = jnp.zeros_like(total)

    @pl.when((step < request_steps) & (step * GATHERED < bounds_ref[2]))
    def _():
        for part in range(0, GATHERED, 4):
            found = []
            for j in range(part, part + 4):
                at = step * GATHERED + j
                slot = order_ref[at]
                block = wanted_ref[slot]
                rows = pl.ds(pl.multiple_of(block * BLOCK, BLOCK), BLOCK)
                stats = stats_ref[slot]
                helped = jnp.where(at < bounds_ref[2], help_ref[j], jnp.zeros((BLOCK, 256), BF))
                ctx = jnp.where(at < bounds_ref[1], ctx_ref[j], helped)
                pred_scale, share = stats[0:1], stats[1:2]
                scores = dot_nt(keyed_ref[rows, :], ctx) * (SCALE * pred_scale)
                weighted = jnp.exp(scores) * (share * pred_scale)
                weighted = jnp.where(at < bounds_ref[2], weighted, 0.0)
                found.append((rows, dot(weighted.astype(BF), ctx)))
            for rows, addend in found:
                total[rows, :] += addend

    @pl.when(step >= request_steps)
    def _():
        chunk = step - request_steps
        rows = pl.ds(pl.multiple_of(chunk * CHUNK, CHUNK), CHUNK)
        direct = SCALE * dot(total[rows, :].astype(BF), pred_ref[...])
        latent = lat_ref[...].astype(F32)
        key_scale = lax.rsqrt(row_sum(latent * latent) + EPSILON)
        key = latent * key_scale
        along = row_sum(key * direct)
        out_ref[...] = part_ref[...] + key_scale * (direct - along * key)

        @pl.when(step == pl.num_programs(0) - 1)
        def _():
            out_ref[CHUNK - HALO:, :] += borrowed_ref[...]


def own(order, bounds, wanted, ctx, helped, stats, keyed, part, latents, borrowed, pred_weight):
    rows = part.shape[0]
    slots = ctx.shape[0]
    request_steps = slots // GATHERED
    first_help = slots // 2 // GATHERED
    whole = lambda *shape: pl.BlockSpec(shape, lambda i, o, c, w: (0,) * len(shape))
    chunk_of = pl.BlockSpec(
        (CHUNK, 256), lambda i, o, c, w: (jnp.maximum(i - request_steps, 0), 0)
    )
    return pl.pallas_call(
        own_kernel,
        grid_spec=pltpu.PrefetchScalarGridSpec(
            num_scalar_prefetch=3,
            grid=(request_steps + rows // CHUNK,),
            in_specs=[
                pl.BlockSpec(
                    (GATHERED, BLOCK, 256),
                    lambda i, o, c, w: (jnp.minimum(i, last_step(c[1], GATHERED)), 0, 0),
                ),
                pl.BlockSpec(
                    (GATHERED, BLOCK, 256),
                    lambda i, o, c, w: (
                        jnp.clip(i - first_help, 0, last_step(c[2] - slots // 2, GATHERED)), 0, 0
                    ),
                ),
                whole(slots, 2, 128),
                whole(rows, 256),
                chunk_of,
                chunk_of,
                whole(HALO, 256),
                whole(256, 256),
            ],
            out_specs=chunk_of,
            scratch_shapes=[pltpu.VMEM((rows, 256), F32)],
        ),
        out_shape=jax.ShapeDtypeStruct((rows, 256), F32),
        compiler_params=pltpu.CompilerParams(vmem_limit_bytes=VMEM),
        name="own",
    )(order, bounds, wanted, ctx, helped, stats, keyed, part, latents, borrowed, pred_weight)


def shifted(block, axis, distance):
    devices = range(lax.axis_size(axis))
    route = [(i - distance, i) for i in devices if i - distance in devices]
    return lax.ppermute(block, axis, route)


def swapped(block, axis):
    return lax.ppermute(block, axis, [(i, i ^ 1) for i in range(lax.axis_size(axis))])


def exchanged(slots):
    owners_count = slots.shape[0] // CAP
    sent = slots.reshape((owners_count, CAP) + slots.shape[1:])
    got = lax.all_to_all(sent, ("tm", "stream"), split_axis=0, concat_axis=0, tiled=True)
    return got.reshape(slots.shape)


def body(raw, starts, neg_owner, neg_block, enc_weight, tcn_weight, pred_weight):
    raw = raw[0]
    owners_count = lax.axis_size("tm") * lax.axis_size("stream")
    rim_starts = jnp.concatenate(
        [jnp.zeros((1, 128 - HALO), BF), starts[:, -HALO:].astype(BF)], axis=1
    )
    rim = shifted(jnp.concatenate([raw[:, -128:], rim_starts, rim_starts], axis=0), "tm", 1)
    half_weight = (tcn_weight * 0.5).astype(BF)
    tcn_back = jnp.swapaxes(tcn_weight, 2, 3)
    pred_back = pred_weight.T
    pack, push, slots, bd = prep(
        neg_owner[0].T, neg_block[0].T, raw, starts.reshape(-1, BLOCK), rim,
        enc_weight, owners_count,
    )
    pushed = exchanged(push)
    latents, queries, slopes, levels, rim_slopes, rim_levels, keyed, scales = forward(
        pack, bd, half_weight, pred_weight
    )
    pushed, queries, tcn_back, pred_back = lax.optimization_barrier(
        (pushed, queries, tcn_back, pred_back)
    )
    replies, order, bounds, wanted, extra = answer(pushed, pack)
    half = order.shape[0] // TOGETHER * TOGETHER // 2
    shared, replies, order = lax.optimization_barrier((swapped(extra, "tm"), replies, order))
    answers = exchanged(replies)
    request_ctx = recompute(order, bounds, pushed, bd, half_weight)
    shared, request_ctx, answers = lax.optimization_barrier((shared, request_ctx, answers))
    mate_count = shared[half, 0, 0].astype(jnp.int32)
    mate_bounds = jnp.stack([kept(mate_count, half) - half, mate_count - half])
    helped = swapped(
        recompute(
            lax.iota(jnp.int32, half), jnp.maximum(mate_bounds, 0), shared, bd, half_weight
        ),
        "tm",
    )
    pred_grad, target_grad, stats = score(slots, answers, queries, latents, levels, scales, bd)
    got_stats = exchanged(stats)
    part, rim_grad = backward(
        pred_grad, slopes, levels, target_grad, rim_slopes, rim_levels, pred_back, tcn_back
    )
    borrowed = shifted(rim_grad, "tm", -1)
    return own(
        order, bounds, wanted, request_ctx, helped, got_stats, keyed, part, latents, borrowed, pred_weight
    )[None]


def solution(mesh):
    placed = (
        P("stream", None, "tm"),
        P("stream", "tm"),
        P("stream", "tm", None),
        P("stream", "tm", None),
        P(),
        P(),
        P(),
    )
    return jax.shard_map(
        body, mesh=mesh, in_specs=placed, out_specs=P("stream", "tm", None), check_vma=False
    )
```

```python
import jax
import jax.numpy as jnp
from jax import lax
from jax.experimental import pallas as pl
from jax.experimental.pallas import tpu as pltpu
from jax.sharding import PartitionSpec as P

BLOCK = 128
NEG = 4
HALO = 32
AHEAD = 4
CAP = 2
LAYERS = 4
PACK = 32
TOGETHER = 16
PAIRED = 1
PIECES = 4
SKEW = 1
GATHERED = 64
CHUNK = 1024
NOTE = 95
LEAD = 20
SEGMENT = 512
SCORED = 4
SPAN = 1024
SCALE = 10.0
EPSILON = 1e-06
BF = jnp.bfloat16
F32 = jnp.float32
MIB = 1 << 20
VMEM = 60 * MIB


def dot(a, b):
    return jnp.dot(a, b, preferred_element_type=F32)


def dot_nt(a, b):
    return lax.dot_general(a, b, (((1,), (1,)), ((), ())), preferred_element_type=F32)


def row_sum(x):
    return jnp.sum(x, axis=-1, keepdims=True)


def silu_of_half(half):
    return half + half * jnp.tanh(half)


def wide(x):
    return jnp.concatenate([x, x], axis=1)


def prep_kernel(owner_ref, block_ref, raw_ref, starts_ref, rim_ref, enc_ref,
                pack_ref, push_ref, slot_ref, bd_ref, lines, packs, turned, seen):
    blocks = pack_ref.shape[0]
    lines[...] = jnp.zeros_like(lines)
    for b in range(blocks):
        lines[b, 0:6, :] = raw_ref[:, b * 512:(b + 1) * 512].astype(F32)
    row = lax.broadcasted_iota(jnp.int32, (512, 512), 0)
    col = lax.broadcasted_iota(jnp.int32, (512, 512), 1)
    perm = jnp.where(row == 4 * (col & 127) + (col >> 7), 1.0, 0.0).astype(BF)
    row = lax.broadcasted_iota(jnp.int32, (128, 128), 0)
    col = lax.broadcasted_iota(jnp.int32, (128, 128), 1)
    perm_halo = jnp.where(row == 4 * (col & 31) + (col >> 5), 1.0, 0.0).astype(BF)
    flat = lines[...].reshape(blocks * 8, 512).astype(BF)
    main = dot(flat, perm).reshape(blocks, 8, 512)
    halo = dot(flat[:, 384:512], perm_halo).reshape(blocks, 8, 128)
    rim = rim_ref[...]
    rim_halo = dot(rim, perm_halo)

    lane = lax.broadcasted_iota(jnp.int32, (blocks + 8, 128), 1)
    level_row = lax.broadcasted_iota(jnp.int32, (8, 128), 0)
    rim_f = rim.astype(F32)
    before = jnp.where(level_row == 7, pltpu.roll(rim_f, 1, 0), 0.0)
    started = jnp.concatenate([before, starts_ref[...].astype(F32)], axis=0)
    level = 1.0 - started
    for distance in (1, 2, 4):
        moved = pltpu.roll(started, distance, 1)
        started = jnp.maximum(
            started, jnp.where(lane < distance, pltpu.roll(moved, 1, 0), moved)
        )
        level = level + (1.0 - started)
    level_halo = jnp.where(lane < HALO, pltpu.roll(level, HALO, 1), 0.0)

    for k in range(4):
        packs[:, k * 6:(k + 1) * 6, :] = main[:, 0:6, k * 128:(k + 1) * 128]
    packs[0, 24:30, :] = rim_halo[0:6]
    packs[1:blocks, 24:30, :] = halo[0:blocks - 1, 0:6, :]
    for b in range(blocks):
        packs[b, 30:31, :] = level[8 + b:9 + b]
        packs[b, 31:32, :] = level_halo[7 + b:8 + b]
    quarter = lax.broadcasted_iota(jnp.int32, (PACK, 128), 1) >> 5
    for group in range(blocks // 4):
        four = [packs[group * 4 + q] for q in range(4)]
        parts = []
        for g in range(4):
            part = four[g]
            for q in range(4):
                if q != g:
                    part = jnp.where(quarter == q, pltpu.roll(four[q], (q - g) * 32 % 128, 1), part)
            parts.append(part)
        flipped = jnp.transpose(jnp.concatenate(parts, axis=0))
        for q in range(4):
            turned[group * 4 + q] = flipped[q * 32:(q + 1) * 32]
    pack_ref[...] = turned[...].astype(BF)

    lane = lax.broadcasted_iota(jnp.int32, (PACK, 128), 1)
    note = jnp.where(lane == NOTE, 1.0, 0.0)
    unused = (-note).astype(BF)

    def clear(i, carry):
        push_ref[i] = unused
        return carry

    lax.fori_loop(0, push_ref.shape[0], clear, 0, unroll=8)

    def forget(i, carry):
        seen[i] = 0
        return carry

    lax.fori_loop(0, seen.shape[0], forget, 0, unroll=8)

    def send(i, carry):
        owner = owner_ref[i % NEG, i // NEG]
        rank = seen[owner]
        seen[owner] = rank + 1
        slot = owner * CAP + rank
        slot_ref[i] = slot
        wanted = block_ref[i % NEG, i // NEG].astype(F32)
        push_ref[slot] = (turned[i // NEG] + note * wanted).astype(BF)
        return carry

    lax.fori_loop(0, blocks * NEG, send, 0, unroll=4)

    bd_ref[...] = jnp.zeros_like(bd_ref)
    half_enc = (enc_ref[...].astype(F32) * 0.5).astype(BF)
    for q in range(4):
        bd_ref[q * 32:q * 32 + 24, q * 256:(q + 1) * 256] = half_enc


def prep(owners, wanted, raw, starts, rim, enc_weight, owners_count):
    blocks = starts.shape[0]
    smem = pl.BlockSpec(memory_space=pltpu.SMEM)
    vmem = pl.BlockSpec(memory_space=pltpu.VMEM)
    return pl.pallas_call(
        prep_kernel,
        out_shape=(
            jax.ShapeDtypeStruct((blocks, PACK, 128), BF),
            jax.ShapeDtypeStruct((owners_count * CAP, PACK, 128), BF),
            jax.ShapeDtypeStruct((blocks * NEG,), jnp.int32),
            jax.ShapeDtypeStruct((128, 1024), BF),
        ),
        in_specs=[smem, smem, vmem, vmem, vmem, vmem],
        out_specs=(vmem, vmem, smem, vmem),
        scratch_shapes=[
            pltpu.VMEM((blocks, 8, 512), F32),
            pltpu.VMEM((blocks, PACK, 128), F32),
            pltpu.VMEM((blocks, PACK, 128), F32),
            pltpu.SMEM((owners_count,), jnp.int32),
        ],
        compiler_params=pltpu.CompilerParams(vmem_limit_bytes=VMEM),
        name="prep",
    )(owners, wanted, raw, starts, rim, enc_weight)


def halo_rows(pack):
    lane = lax.broadcasted_iota(jnp.int32, (HALO, 128), 1)
    halo = jnp.where(lane == 30, pltpu.roll(pack, 127, 1), 0.0)
    for g in range(4):
        moved = pltpu.roll(pack, (-26 * g - 24) % 128, 1)
        halo = jnp.where((lane >= 6 * g) & (lane < 6 * g + 6), moved, halo)
    return halo


def layer_half(h, level, layer, w_ref):
    moved = pltpu.roll(h, 2**layer, 0)
    gated = jnp.where(level > layer, moved, 0.0)
    return dot(h.astype(BF), w_ref[layer, 0]) + dot(gated.astype(BF), w_ref[layer, 1])


def forward_kernel(pack_ref, bd_ref, w_ref, pred_ref, lat_ref, query_ref, slope_ref, level_ref,
                   rim_slope_ref, rim_level_ref, keyed_ref, scale_ref):
    first = pl.program_id(0) == 0
    packs = pack_ref[...].reshape(4 * PACK, 128).astype(F32)
    halo = halo_rows(packs[0:PACK])
    rows = jnp.concatenate([packs, halo], axis=0)
    encoded = silu_of_half(dot(rows.astype(BF), bd_ref[...]))
    pieces, columns = [encoded[4 * PACK:, 0:256]], [halo[:, 30:31]]
    for q in range(4):
        for g in range(4):
            pieces.append(encoded[q * PACK:(q + 1) * PACK, g * 256:(g + 1) * 256])
            columns.append(packs[q * PACK:(q + 1) * PACK, g * 32 + 30:g * 32 + 31])
    latent = jnp.concatenate(pieces, axis=0).astype(BF)
    level = jnp.broadcast_to(jnp.concatenate(columns, axis=0), (HALO + SEGMENT, 256))
    level_ref[...] = level[HALO:, 0:128]
    lat_ref[...] = latent[HALO:]
    h = latent.astype(F32)
    own = h[HALO:]
    key_scale = lax.rsqrt(row_sum(own * own) + EPSILON)
    keyed_ref[...] = dot_nt((own * key_scale).astype(BF), pred_ref[...]).astype(BF)
    slopes = []
    for layer in range(LAYERS):
        half = layer_half(h, level, layer, w_ref)
        tanh = jnp.tanh(half)
        slope = (0.5 * (1.0 + tanh)) * (1.0 + half * (1.0 - tanh))
        slope_ref[layer] = slope[HALO:].astype(BF)
        slopes.append(slope[:HALO].astype(BF))
        h = h + half + half * tanh
    raw_pred = dot(h[HALO - AHEAD:HALO - AHEAD + SEGMENT].astype(BF), pred_ref[...])
    pred_scale = lax.rsqrt(row_sum(raw_pred * raw_pred) + EPSILON)
    query_ref[...] = (raw_pred * pred_scale).astype(BF)
    scale_ref[...] = jnp.broadcast_to(pred_scale, (SEGMENT, 128))

    @pl.when(first)
    def _():
        rim_level_ref[...] = level[:HALO, 0:128]
        for layer in range(LAYERS):
            rim_slope_ref[layer] = slopes[layer]


def forward(pack, bd, half_weight, pred_weight):
    rows = pack.shape[0] * BLOCK
    steps = rows // SEGMENT
    whole = lambda *shape: pl.BlockSpec(shape, lambda i: (0,) * len(shape))
    rows_of = lambda width: pl.BlockSpec((SEGMENT, width), lambda i: (i, 0))
    return pl.pallas_call(
        forward_kernel,
        grid=(steps,),
        out_shape=(
            jax.ShapeDtypeStruct((rows, 256), BF),
            jax.ShapeDtypeStruct((rows, 256), BF),
            jax.ShapeDtypeStruct((LAYERS, rows, 256), BF),
            jax.ShapeDtypeStruct((rows, 128), F32),
            jax.ShapeDtypeStruct((LAYERS, HALO, 256), BF),
            jax.ShapeDtypeStruct((HALO, 128), F32),
            jax.ShapeDtypeStruct((rows, 256), BF),
            jax.ShapeDtypeStruct((rows, 128), F32),
        ),
        in_specs=[
            pl.BlockSpec((4, PACK, 128), lambda i: (i, 0, 0)),
            whole(128, 1024),
            whole(LAYERS, 2, 256, 256),
            whole(256, 256),
        ],
        out_specs=(
            rows_of(256),
            rows_of(256),
            pl.BlockSpec((LAYERS, SEGMENT, 256), lambda i: (0, i, 0)),
            rows_of(128),
            whole(LAYERS, HALO, 256),
            whole(HALO, 128),
            rows_of(256),
            rows_of(128),
        ),
        compiler_params=pltpu.CompilerParams(vmem_limit_bytes=VMEM),
        cost_estimate=pl.CostEstimate(
            flops=rows * 2 * 65536 * 10, bytes_accessed=18 * MIB, transcendentals=rows * 256 * 5
        ),
        name="forward",
    )(pack, bd, half_weight, pred_weight)


def kept(count, half):
    shared = ((count - half + 63) >> 6) << 5
    return jnp.where(count > half, jnp.minimum(count, half + shared), count)


def answer_kernel(push_ref, pack_ref, answer_ref, order_ref, bounds_ref, wanted_ref, extra_ref,
                  listed, arrived):
    slots = push_ref.shape[0]
    half = slots // 2
    notes = push_ref[:, 0:16, :].astype(F32)[:, 0, :]
    listed[...] = jnp.transpose(notes)[NOTE:NOTE + 1].astype(jnp.int32)
    pltpu.sync_copy(listed, arrived)

    def clear(i, carry):
        order_ref[i] = 0
        return carry

    lax.fori_loop(0, slots, clear, 0, unroll=8)

    def reply(i, count):
        wanted = arrived[0, i]
        wanted_ref[i] = jnp.maximum(wanted, 0)
        answer_ref[i] = pack_ref[jnp.maximum(wanted, 0)]
        order_ref[count] = i
        return count + jnp.where(wanted >= 0, 1, 0)

    count = lax.fori_loop(0, slots, reply, 0, unroll=8)
    bounds_ref[0] = 0
    bounds_ref[1] = kept(count, half)
    bounds_ref[2] = count
    extra_ref[...] = jnp.zeros_like(extra_ref)
    extra_ref[half] = jnp.full((PACK, 128), count.astype(F32)).astype(BF)

    def share(i, carry):
        extra_ref[i - half] = push_ref[order_ref[i]]
        return carry

    lax.fori_loop(half, jnp.maximum(count, half), share, 0)


def answer(pushed, pack):
    slots = pushed.shape[0]
    smem = pl.BlockSpec(memory_space=pltpu.SMEM)
    vmem = pl.BlockSpec(memory_space=pltpu.VMEM)
    return pl.pallas_call(
        answer_kernel,
        out_shape=(
            jax.ShapeDtypeStruct((slots, PACK, 128), BF),
            jax.ShapeDtypeStruct((slots + 8,), jnp.int32),
            jax.ShapeDtypeStruct((3,), jnp.int32),
            jax.ShapeDtypeStruct((slots,), jnp.int32),
            jax.ShapeDtypeStruct((slots // 2 + 1, PACK, 128), BF),
        ),
        in_specs=[vmem, vmem],
        out_specs=(vmem, smem, smem, smem, vmem),
        scratch_shapes=[pltpu.VMEM((1, slots), jnp.int32), pltpu.SMEM((1, slots), jnp.int32)],
        compiler_params=pltpu.CompilerParams(vmem_limit_bytes=VMEM),
        name="answer",
    )(pushed, pack)


def request_stages(base, order_ref, push_ref, bd_ref, w_ref, ctx_ref, first_out,
                   patches, level, here, there, left, right, gated, half_ref):
    times = LEAD + BLOCK - AHEAD

    def pieces(first, parts=PIECES):
        edges = [first + (times - first) * p // parts for p in range(parts + 1)]
        return [(a * TOGETHER, b * TOGETHER) for a, b in zip(edges[:-1], edges[1:])]

    def parts(a, b):
        return [slice(c, min(c + 32, b)) for c in range(a, b, 32)]

    for j in range(TOGETHER):
        pack = push_ref[order_ref[base + j]].astype(F32)
        patches[pl.ds(j, LEAD, stride=TOGETHER), :] = halo_rows(pack)[HALO - LEAD:]
        for g in range(4):
            own = pltpu.roll(pack, -32 * g % 128, 1) if g else pack
            at = (LEAD + g * 32) * TOGETHER + j
            patches[pl.ds(at, PACK, stride=TOGETHER), :] = own
        if j % 4 == 3:
            yield
    enc = bd_ref[:, 0:256]
    for a, b in pieces(0):
        half_ref[a:b, :] = dot(patches[a:b, :].astype(BF), enc).astype(BF)
        yield
        level[a:b, :] = jnp.broadcast_to(patches[a:b, 30:31], (b - a, 128)).astype(BF)
        for at in parts(a, b):
            here[at, :] = silu_of_half(half_ref[at, :])
        yield
    source, target = here, there
    first = 0
    for layer in range(LAYERS):
        first += 2**layer if layer else 2
        back = 2**layer * TOGETHER
        both = w_ref[layer].reshape(512, 256)
        for a, b in pieces(first):
            for at in parts(a, b):
                gate = jnp.minimum(jnp.maximum(level[at, :] - float(layer), 0.0), 1.0)
                gated[at, :] = source[at.start - back:at.stop - back, :] * wide(gate)
            yield
            x = jnp.concatenate([source[a:b, :], gated[a:b, :]], axis=1)
            half_ref[a:b, :] = dot(x, both).astype(BF)
            yield
            for at in parts(a, b):
                result = source[at, :] + silu_of_half(half_ref[at, :])
                if layer < LAYERS - 1:
                    target[at, :] = result
                else:
                    result = result.astype(F32)
                    to = slice(at.start - first * TOGETHER, at.stop - first * TOGETHER)
                    left[to, :] = result[:, 0:128]
                    right[to, :] = result[:, 128:256]
            yield
        source, target = target, source
    for j in range(TOGETHER):
        rows = pl.ds(j, BLOCK, stride=TOGETHER)
        ctx_ref[first_out + j] = jnp.concatenate([left[rows, :], right[rows, :]], axis=1).astype(BF)
        if j % 4 == 3:
            yield


def recompute_kernel(order_ref, bounds_ref, push_ref, bd_ref, w_ref, ctx_ref, *scratch):
    base = bounds_ref[0] + pl.program_id(0) * PAIRED * TOGETHER

    @pl.when(base < bounds_ref[1])
    def _():
        each = len(scratch) // PAIRED
        waiting = [
            request_stages(
                base + p * TOGETHER, order_ref, push_ref, bd_ref, w_ref, ctx_ref, p * TOGETHER,
                *scratch[p * each:(p + 1) * each],
            )
            for p in range(PAIRED)
        ]
        for p, stages in enumerate(waiting):
            for _ in range(SKEW * (PAIRED - 1 - p)):
                next(stages)
        while waiting:
            waiting = [stages for stages in waiting if next(stages, True) is None]


def last_step(count, together):
    return jnp.maximum(count - 1, 0) // together


def recompute(order, bounds, pushed, bd, half_weight):
    slots = order.shape[0] // TOGETHER * TOGETHER
    together = PAIRED * TOGETHER
    times = LEAD + BLOCK - AHEAD
    whole = lambda *shape: pl.BlockSpec(shape, lambda i, o, c: (0,) * len(shape))
    return pl.pallas_call(
        recompute_kernel,
        grid_spec=pltpu.PrefetchScalarGridSpec(
            num_scalar_prefetch=2,
            grid=(slots // TOGETHER // PAIRED,),
            in_specs=[whole(*pushed.shape), whole(128, 1024), whole(LAYERS, 2, 256, 256)],
            out_specs=pl.BlockSpec(
                (together, BLOCK, 256),
                lambda i, o, c: (
                    jnp.minimum(c[0] // together + i, last_step(c[1], together)), 0, 0
                ),
            ),
            scratch_shapes=[
                pltpu.VMEM(((LEAD + BLOCK) * TOGETHER, 128), F32),
                pltpu.VMEM((times * TOGETHER, 128), BF),
                pltpu.VMEM((times * TOGETHER, 256), BF),
                pltpu.VMEM((times * TOGETHER, 256), BF),
                pltpu.VMEM((BLOCK * TOGETHER, 128), F32),
                pltpu.VMEM((BLOCK * TOGETHER, 128), F32),
                pltpu.VMEM((times * TOGETHER, 256), BF),
                pltpu.VMEM((times * TOGETHER, 256), BF),
            ] * PAIRED,
        ),
        out_shape=jax.ShapeDtypeStruct((slots, BLOCK, 256), BF),
        compiler_params=pltpu.CompilerParams(vmem_limit_bytes=VMEM),
        cost_estimate=pl.CostEstimate(
            flops=slots * 160 * 2 * 65536 * 10, bytes_accessed=20 * MIB,
            transcendentals=slots * 160 * 256 * 5,
        ),
        name="recompute",
    )(order, bounds, pushed, bd, half_weight)


def score_kernel(slot_ref, answer_ref, query_ref, lat_ref, level_ref, scale_ref, bd_ref,
                 pred_grad_ref, target_grad_ref, stats_ref):
    step = pl.program_id(0)

    @pl.when(step == 0)
    def _():
        stats_ref[...] = jnp.zeros_like(stats_ref)

    blocks = range(SCORED)
    slots = [slot_ref[step * SCORED * NEG + i] for i in range(SCORED * NEG)]
    lane = lax.broadcasted_iota(jnp.int32, (BLOCK, 128), 1)
    ats = [slice(g * BLOCK, (g + 1) * BLOCK) for g in blocks]
    packs = [
        jnp.concatenate([answer_ref[slots[g * NEG + j]] for j in range(NEG)], axis=0) for g in blocks
    ]
    half = [dot(pack, bd_ref[...]) for pack in packs]
    pred_scale = [scale_ref[at, 0:1] for at in ats]
    query = [query_ref[at, :] for at in ats]
    keys = []
    for g in blocks:
        pieces = []
        for j in range(4):
            negative = silu_of_half(half[g][:, j * 256:(j + 1) * 256])
            key_scale = lax.rsqrt(row_sum(negative * negative) + EPSILON)
            pieces.append((negative * (key_scale)).astype(BF))
        keys.append(jnp.concatenate(pieces, axis=0))
    scores = [dot_nt(query[g], keys[g]) for g in blocks]
    exp_neg = [jnp.exp(SCALE * x) for x in scores]
    both = [dot(exp_neg[g].astype(BF), keys[g]) for g in blocks]
    sums = [row_sum(x) for x in exp_neg]
    columns = jnp.zeros((BLOCK, 128), F32)
    for g in blocks:
        at = ats[g]
        query_f = query[g].astype(F32)
        latent = lat_ref[at, :].astype(F32)
        usable = jnp.where(level_ref[at, 0:1] > 2.0, 1.0, 0.0)
        own_scale = lax.rsqrt(row_sum(latent * latent) + EPSILON)
        positive = SCALE * row_sum(query_f * latent) * own_scale
        exp_pos = jnp.exp(positive)
        share = usable / (exp_pos + sums[g])
        d_pos = share * exp_pos - usable
        pull = SCALE * d_pos * own_scale
        query_grad = (SCALE * share) * both[g] + (pull) * latent
        target_grad_ref[at, :] = (
            (pull) * query_f - (d_pos * positive * own_scale * own_scale) * latent
        )
        along = row_sum(query_f * query_grad)
        pred_grad_ref[at, :] = (
            (pred_scale[g]) * (query_grad - (along) * query_f)
        ).astype(BF)
        columns = jnp.where(lane == 2 * g, pred_scale[g], columns)
        columns = jnp.where(lane == 2 * g + 1, share, columns)
    rows = jnp.transpose(columns)
    for i in range(SCORED * NEG):
        g = i // NEG
        stats_ref[slots[i]] = rows[2 * g:2 * g + 2]


def score(slots, answers, queries, latents, levels, scales, bd):
    rows = queries.shape[0]
    count = answers.shape[0]
    whole = lambda *shape: pl.BlockSpec(shape, lambda i, s: (0,) * len(shape))
    rows_of = lambda width: pl.BlockSpec((SCORED * BLOCK, width), lambda i, s: (i, 0))
    return pl.pallas_call(
        score_kernel,
        grid_spec=pltpu.PrefetchScalarGridSpec(
            num_scalar_prefetch=1,
            grid=(rows // BLOCK // SCORED,),
            in_specs=[
                whole(count, PACK, 128), rows_of(256), rows_of(256), rows_of(128),
                rows_of(128), whole(128, 1024),
            ],
            out_specs=(rows_of(256), rows_of(256), whole(count, 2, 128)),
        ),
        out_shape=(
            jax.ShapeDtypeStruct((rows, 256), BF),
            jax.ShapeDtypeStruct((rows, 256), F32),
            jax.ShapeDtypeStruct((count, 2, 128), F32),
        ),
        compiler_params=pltpu.CompilerParams(vmem_limit_bytes=VMEM),
        cost_estimate=pl.CostEstimate(
            flops=rows * 2 * 65536 * 10, bytes_accessed=16 * MIB, transcendentals=rows * 256 * 6
        ),
        name="score",
    )(slots, answers, queries, latents, levels, scales, bd)


def backward_kernel(pred_grad_ref, slope_ref, level_ref, target_grad_ref, rim_slope_ref,
                    rim_level_ref, pred_ref, w_ref, out_ref, rim_ref, carry):
    @pl.when(pl.program_id(0) == 0)
    def _():
        carry[...] = jnp.zeros_like(carry)

    def earlier(values, distance, place):
        longer = jnp.concatenate([values, carry[place]], axis=0)
        carry[place] = values[0:8]
        return longer[distance:distance + values.shape[0]]

    def through_layers(cotangent, slopes, level):
        for layer in reversed(range(LAYERS)):
            back = cotangent * slopes[layer].astype(F32)
            gated = jnp.where(level > layer, back, 0.0)
            cotangent = (
                cotangent
                + dot(
                    jnp.concatenate([back, earlier(gated, 2**layer, layer)], axis=1).astype(BF),
                    w_ref[layer].reshape(512, 256),
                )
            )
        return cotangent

    context_rows = dot(pred_grad_ref[...], pred_ref[...])
    cotangent = earlier(context_rows, AHEAD, LAYERS)
    level = wide(level_ref[...])
    out_ref[...] = through_layers(cotangent, slope_ref, level) + target_grad_ref[...]

    @pl.when(pl.program_id(0) == pl.num_programs(0) - 1)
    def _():
        cotangent = earlier(jnp.zeros((HALO, 256), F32), AHEAD, LAYERS)
        level = wide(rim_level_ref[...])
        rim_ref[...] = through_layers(cotangent, rim_slope_ref, level)


def backward(pred_grad, slopes, levels, target_grad, rim_slopes, rim_levels, pred_weight, weight):
    rows = pred_grad.shape[0]
    steps = rows // SPAN
    whole = lambda *shape: pl.BlockSpec(shape, lambda i: (0,) * len(shape))
    rows_of = lambda width: pl.BlockSpec((SPAN, width), lambda i: (steps - 1 - i, 0))
    return pl.pallas_call(
        backward_kernel,
        grid=(steps,),
        out_shape=(
            jax.ShapeDtypeStruct((rows, 256), F32),
            jax.ShapeDtypeStruct((HALO, 256), F32),
        ),
        in_specs=[
            rows_of(256),
            pl.BlockSpec((LAYERS, SPAN, 256), lambda i: (0, steps - 1 - i, 0)),
            rows_of(128),
            rows_of(256),
            whole(LAYERS, HALO, 256),
            whole(HALO, 128),
            whole(256, 256),
            whole(LAYERS, 2, 256, 256),
        ],
        out_specs=(rows_of(256), whole(HALO, 256)),
        scratch_shapes=[pltpu.VMEM((LAYERS + 1, 8, 256), F32)],
        compiler_params=pltpu.CompilerParams(vmem_limit_bytes=VMEM),
        cost_estimate=pl.CostEstimate(
            flops=rows * 2 * 65536 * 9, bytes_accessed=22 * MIB, transcendentals=0
        ),
        name="backward",
    )(pred_grad, slopes, levels, target_grad, rim_slopes, rim_levels, pred_weight, weight)


def own_kernel(order_ref, bounds_ref, wanted_ref, ctx_ref, help_ref, stats_ref, keyed_ref, part_ref, lat_ref,
               borrowed_ref, pred_ref, out_ref, total):
    step = pl.program_id(0)
    request_steps = pl.num_programs(0) - total.shape[0] // CHUNK

    @pl.when(step == 0)
    def _():
        total[...] = jnp.zeros_like(total)

    @pl.when((step < request_steps) & (step * GATHERED < bounds_ref[2]))
    def _():
        for part in range(0, GATHERED, 4):
            found = []
            for j in range(part, part + 4):
                at = step * GATHERED + j
                slot = order_ref[at]
                block = wanted_ref[slot]
                rows = pl.ds(pl.multiple_of(block * BLOCK, BLOCK), BLOCK)
                stats = stats_ref[slot]
                helped = jnp.where(at < bounds_ref[2], help_ref[j], jnp.zeros((BLOCK, 256), BF))
                ctx = jnp.where(at < bounds_ref[1], ctx_ref[j], helped)
                pred_scale, share = stats[0:1], stats[1:2]
                scores = dot_nt(keyed_ref[rows, :], ctx) * (SCALE * pred_scale)
                weighted = jnp.exp(scores) * (share * pred_scale)
                weighted = jnp.where(at < bounds_ref[2], weighted, 0.0)
                found.append((rows, dot(weighted.astype(BF), ctx)))
            for rows, addend in found:
                total[rows, :] += addend

    @pl.when(step >= request_steps)
    def _():
        chunk = step - request_steps
        rows = pl.ds(pl.multiple_of(chunk * CHUNK, CHUNK), CHUNK)
        direct = SCALE * dot(total[rows, :].astype(BF), pred_ref[...])
        latent = lat_ref[...].astype(F32)
        key_scale = lax.rsqrt(row_sum(latent * latent) + EPSILON)
        key = latent * key_scale
        along = row_sum(key * direct)
        out_ref[...] = part_ref[...] + key_scale * (direct - along * key)

        @pl.when(step == pl.num_programs(0) - 1)
        def _():
            out_ref[CHUNK - HALO:, :] += borrowed_ref[...]


def own(order, bounds, wanted, ctx, helped, stats, keyed, part, latents, borrowed, pred_weight):
    rows = part.shape[0]
    slots = ctx.shape[0]
    request_steps = slots // GATHERED
    first_help = slots // 2 // GATHERED
    whole = lambda *shape: pl.BlockSpec(shape, lambda i, o, c, w: (0,) * len(shape))
    chunk_of = pl.BlockSpec(
        (CHUNK, 256), lambda i, o, c, w: (jnp.maximum(i - request_steps, 0), 0)
    )
    return pl.pallas_call(
        own_kernel,
        grid_spec=pltpu.PrefetchScalarGridSpec(
            num_scalar_prefetch=3,
            grid=(request_steps + rows // CHUNK,),
            in_specs=[
                pl.BlockSpec(
                    (GATHERED, BLOCK, 256),
                    lambda i, o, c, w: (jnp.minimum(i, last_step(c[1], GATHERED)), 0, 0),
                ),
                pl.BlockSpec(
                    (GATHERED, BLOCK, 256),
                    lambda i, o, c, w: (
                        jnp.clip(i - first_help, 0, last_step(c[2] - slots // 2, GATHERED)), 0, 0
                    ),
                ),
                whole(slots, 2, 128),
                whole(rows, 256),
                chunk_of,
                chunk_of,
                whole(HALO, 256),
                whole(256, 256),
            ],
            out_specs=chunk_of,
            scratch_shapes=[pltpu.VMEM((rows, 256), F32)],
        ),
        out_shape=jax.ShapeDtypeStruct((rows, 256), F32),
        compiler_params=pltpu.CompilerParams(vmem_limit_bytes=VMEM),
        name="own",
    )(order, bounds, wanted, ctx, helped, stats, keyed, part, latents, borrowed, pred_weight)


def shifted(block, axis, distance):
    devices = range(lax.axis_size(axis))
    route = [(i - distance, i) for i in devices if i - distance in devices]
    return lax.ppermute(block, axis, route)


def swapped(block, axis):
    return lax.ppermute(block, axis, [(i, i ^ 1) for i in range(lax.axis_size(axis))])


def exchanged(slots):
    owners_count = slots.shape[0] // CAP
    sent = slots.reshape((owners_count, CAP) + slots.shape[1:])
    got = lax.all_to_all(sent, ("tm", "stream"), split_axis=0, concat_axis=0, tiled=True)
    return got.reshape(slots.shape)


def body(raw, starts, neg_owner, neg_block, enc_weight, tcn_weight, pred_weight):
    raw = raw[0]
    owners_count = lax.axis_size("tm") * lax.axis_size("stream")
    rim_starts = jnp.concatenate(
        [jnp.zeros((1, 128 - HALO), BF), starts[:, -HALO:].astype(BF)], axis=1
    )
    rim = shifted(jnp.concatenate([raw[:, -128:], rim_starts, rim_starts], axis=0), "tm", 1)
    half_weight = (tcn_weight * 0.5).astype(BF)
    tcn_back = jnp.swapaxes(tcn_weight, 2, 3)
    pred_back = pred_weight.T
    pack, push, slots, bd = prep(
        neg_owner[0].T, neg_block[0].T, raw, starts.reshape(-1, BLOCK), rim,
        enc_weight, owners_count,
    )
    pushed = exchanged(push)
    latents, queries, slopes, levels, rim_slopes, rim_levels, keyed, scales = forward(
        pack, bd, half_weight, pred_weight
    )
    pushed, queries, tcn_back, pred_back = lax.optimization_barrier(
        (pushed, queries, tcn_back, pred_back)
    )
    replies, order, bounds, wanted, extra = answer(pushed, pack)
    half = order.shape[0] // TOGETHER * TOGETHER // 2
    shared, replies, order = lax.optimization_barrier((swapped(extra, "tm"), replies, order))
    answers = exchanged(replies)
    request_ctx = recompute(order, bounds, pushed, bd, half_weight)
    shared, request_ctx, answers = lax.optimization_barrier((shared, request_ctx, answers))
    mate_count = shared[half, 0, 0].astype(jnp.int32)
    mate_bounds = jnp.stack([kept(mate_count, half) - half, mate_count - half])
    helped = swapped(
        recompute(
            lax.iota(jnp.int32, half), jnp.maximum(mate_bounds, 0), shared, bd, half_weight
        ),
        "tm",
    )
    pred_grad, target_grad, stats = score(slots, answers, queries, latents, levels, scales, bd)
    got_stats = exchanged(stats)
    part, rim_grad = backward(
        pred_grad, slopes, levels, target_grad, rim_slopes, rim_levels, pred_back, tcn_back
    )
    borrowed = shifted(rim_grad, "tm", -1)
    return own(
        order, bounds, wanted, request_ctx, helped, got_stats, keyed, part, latents, borrowed, pred_weight
    )[None]


def solution(mesh):
    placed = (
        P("stream", None, "tm"),
        P("stream", "tm"),
        P("stream", "tm", None),
        P("stream", "tm", None),
        P(),
        P(),
        P(),
    )
    return jax.shard_map(
        body, mesh=mesh, in_specs=placed, out_specs=P("stream", "tm", None), check_vma=False
    )
```
